32 devices in a mesh: dir: 2 (over core), seq: 4 (over z), batch: 4 (over y, x).
Axes of the slice: x: 2, y: 2, z: 4, core: 2. Of those that a mesh axis runs over, the one named last changes fastest.
Arguments:
- inputs: bfloat16 [8, 2048, 512], P('batch', 'seq'), may hold values from -12 to 12
- cotangent: bfloat16 [8, 2048, 512], P('batch', 'seq'), may hold values from -6 to 6
- lengths: int32 [8], P('batch'), may hold values from 1 to 2048, as said below
- bn_gain: float32 [2, 512], replicated, may hold values from 0.5 to 1.5
- bn_bias: float32 [2, 512], replicated, may hold values from -4 to 4
- in_proj: bfloat16 [2, 2, 512, 768], P(None, 'dir'), may hold values from -0.25 to 0.25
- out_proj: bfloat16 [2, 2, 768, 512], P(None, 'dir'), may hold values from -0.3125 to 0.3125
- lambda_rate: float32 [2, 2, 384], P(None, 'dir'), may hold values from 0.0015467961 to 0.25
- step_size: float32 [2, 2, 384], P(None, 'dir'), may hold values from 0.0015467961 to 0.25
- lambda_freq: float32 [2, 2, 384], P(None, 'dir'), may hold values from -3 to 3
- feedthrough: float32 [2, 512], replicated, may hold values from -6 to 6
- glu_weight: bfloat16 [2, 512, 512], replicated, may hold values from -0.25 to 0.25
- glu_bias: float32 [2, 512], replicated, may hold values from -4 to 4
- running_mean: float32 [2, 512], replicated, may hold values from -6 to 6
- running_var: float32 [2, 512], replicated, may hold values from 0.5 to 2
Outputs:
- activations: float32 [8, 2048, 512], P('batch', 'seq')
- input_grad: float32 [8, 2048, 512], P('batch', 'seq')
- grad_bn_gain: float32 [2, 512], replicated
- grad_bn_bias: float32 [2, 512], replicated
- grad_in_proj: float32 [2, 2, 512, 768], P(None, 'dir')
- grad_out_proj: float32 [2, 2, 768, 512], P(None, 'dir')
- grad_lambda_rate: float32 [2, 2, 384], P(None, 'dir')
- grad_step_size: float32 [2, 2, 384], P(None, 'dir')
- grad_lambda_freq: float32 [2, 2, 384], P(None, 'dir')
- grad_feedthrough: float32 [2, 512], replicated
- grad_glu_weight: float32 [2, 512, 512], replicated
- grad_glu_bias: float32 [2, 512], replicated
- new_running_mean: float32 [2, 512], replicated
- new_running_var: float32 [2, 512], replicated
The draws below stay inside these ranges and needn't reach their ends.
Inputs may be any that keep to these rules, and one draw needn't show every extreme that they name: `lengths`: in each aligned block of 2 sequences (those of one index of batch) one sequence, drawn from the seed, has length 2048.
All inputs are finite; a program needn't handle non-finite values.
Results may differ from the reference program's by a relative error of at most 0.015.
Values may be sent and summed in bfloat16 or wider, within the bound.
A program may use at most 192 MiB of HBM per device.

```python
import math
from functools import partial
import jax
import jax.numpy as jnp
from jax import lax

H = 512
P_SIZE = 384
LAYERS = 2
SEQ_DEV = 2
SEQLEN = 2048
NSEQ = 8


def rate_target(key, low_end, high_end):
    unit = jax.random.uniform(key, (LAYERS, 2, P_SIZE), jnp.float32)
    return jnp.exp(jnp.log(low_end) + unit * (jnp.log(high_end) - jnp.log(low_end)))


def draw_lambda_rate(key, part):
    target = rate_target(key, 0.01 / SEQLEN, 0.03)
    key = jax.random.fold_in(key, 21)
    spread = jax.random.uniform(key, target.shape, jnp.float32, 0.7, 1.4)
    return jnp.sqrt(target) * spread


def draw_step_size(key, part):
    target = rate_target(key, 0.01 / SEQLEN, 0.03)
    key = jax.random.fold_in(key, 22)
    spread = jax.random.uniform(key, target.shape, jnp.float32, 0.7, 1.4)
    return jnp.sqrt(target) * spread


def draw_inputs(key, part):
    key = jax.random.fold_in(key, 5)
    fraction = jnp.arange(SEQLEN, dtype=jnp.float32) / SEQLEN
    sample = jnp.clip(jax.random.normal(key, (NSEQ, SEQLEN, H), jnp.float32), -4.0, 4.0)
    growth = 3.0 ** fraction
    return (sample * growth[None, :, None]).astype(jnp.bfloat16)


def draw_lengths(key, part):
    key = jax.random.fold_in(key, 11)
    first_key, second_key = jax.random.split(key)
    ragged = jax.random.randint(first_key, (NSEQ,), 1, SEQLEN + 1)
    chosen = jax.random.randint(second_key, (NSEQ // SEQ_DEV,), 0, SEQ_DEV)
    within = jnp.arange(NSEQ, dtype=jnp.int32) % SEQ_DEV
    picked = jnp.repeat(chosen, SEQ_DEV)
    return jnp.where(within == picked, SEQLEN, ragged).astype(jnp.int32)


def levels(own_key, extent, shards, low, top_value):
    level = 1.0
    for axis_at, shards_of in shards:
        steps = jax.random.uniform(jax.random.fold_in(jax.random.fold_in(own_key, 6), axis_at), (shards_of,), jnp.float32, low / len(shards), top_value / len(shards))
        level = level * jnp.repeat(jnp.exp(steps), extent[axis_at] // shards_of).reshape((-1,) + (1,) * (len(extent) - 1 - axis_at))
    return level


def gaussian(key, dims, scale, most, cuts=(), kind=jnp.bfloat16):
    values = jax.random.normal(key, dims, jnp.float32) * scale
    if len(cuts) > 0:
        values = levels(key, dims, cuts, -0.22, 0.18) * values
    return jnp.clip(values, min=-most, max=most).astype(kind)


def setup_inputs(seed: int = 0) -> dict:
    arg_keys = jax.random.split(jax.random.key(seed), 16)
    inputs = draw_inputs(jax.random.fold_in(arg_keys[15], 71), 0)
    cotangent = gaussian(arg_keys[1], (NSEQ, SEQLEN, H), 1.0, 6.0, ((0, 4), (1, 4)))
    lengths = draw_lengths(jax.random.fold_in(arg_keys[15], 71), 0)
    bn_gain = jnp.clip(1.0 + 0.1 * jax.random.normal(arg_keys[3], (LAYERS, H), jnp.float32), 0.5, 1.5)
    bn_bias = gaussian(arg_keys[4], (LAYERS, H), 0.3, 4.0, (), jnp.float32)
    in_proj = gaussian(arg_keys[5], (LAYERS, 2, H, 2 * P_SIZE), H ** -0.5, 0.25, ((1, 2),))
    out_proj = gaussian(arg_keys[6], (LAYERS, 2, 2 * P_SIZE, H), P_SIZE ** -0.5, 0.3125, ((1, 2),))
    lambda_rate = draw_lambda_rate(jax.random.fold_in(arg_keys[15], 71), 0)
    step_size = draw_step_size(jax.random.fold_in(arg_keys[15], 71), 0)
    lambda_freq = jnp.clip(jax.random.uniform(arg_keys[9], (LAYERS, 2, P_SIZE), jnp.float32, -3.0, 3.0) * levels(arg_keys[9], (LAYERS, 2, P_SIZE), ((1, 2),), -0.4, 0.0), -3.0, 3.0)
    feedthrough = gaussian(arg_keys[10], (LAYERS, H), 0.5, 6.0, (), jnp.float32)
    glu_weight = gaussian(arg_keys[11], (LAYERS, H, H), H ** -0.5, 0.25)
    glu_bias = gaussian(arg_keys[12], (LAYERS, H), 0.3, 4.0, (), jnp.float32)
    running_mean = gaussian(arg_keys[13], (LAYERS, H), 1.0, 6.0, (), jnp.float32)
    running_var = jnp.clip(jnp.exp(jax.random.uniform(arg_keys[14], (LAYERS, H), jnp.float32, math.log(0.5), math.log(2.0))), 0.5, 2.0)
    return {"inputs": inputs, "cotangent": cotangent, "lengths": lengths, "bn_gain": bn_gain, "bn_bias": bn_bias, "in_proj": in_proj, "out_proj": out_proj, "lambda_rate": lambda_rate, "step_size": step_size, "lambda_freq": lambda_freq, "feedthrough": feedthrough, "glu_weight": glu_weight, "glu_bias": glu_bias, "running_mean": running_mean, "running_var": running_var}


highest = lax.Precision.HIGHEST
epsilon = 1e-05
momentum = 0.9

@jax.custom_vjp
def low(v):
    return lax.optimization_barrier(v.astype(jnp.bfloat16)).astype(jnp.float32)

@jax.custom_vjp
def low_back(v):
    return v

def low_keep(v):
    return (low(v), None)

def low_pass(kept, grad):
    return (grad,)

def back_keep(v):
    return (v, None)

def back_low(kept, grad):
    return (low(grad),)
low.defvjp(low_keep, low_pass)
low_back.defvjp(back_keep, back_low)

def complex_combine(early, later):
    dec_re, dec_im, sta_re, sta_im = early
    new_re, new_im, add_re, add_im = later
    return (new_re * dec_re - new_im * dec_im, new_re * dec_im + new_im * dec_re, new_re * sta_re - new_im * sta_im + add_re, new_re * sta_im + new_im * sta_re + add_im)

def transition(rate_vec, step_vec, freq_vec):
    half_a = 0.5 * step_vec * rate_vec
    half_c = 0.5 * step_vec * freq_vec
    denominator = (1.0 + half_a) * (1.0 + half_a) + half_c * half_c
    lam_re = (1.0 - half_a * half_a - half_c * half_c) / denominator
    lam_im = 2.0 * half_c / denominator
    kap_re = step_vec * (1.0 + half_a) / denominator
    kap_im = step_vec * half_c / denominator
    return (lam_re, lam_im, kap_re, kap_im)

def sequence_scan(drive_term, lam_re, lam_im):
    state_width = lam_re.shape[0]
    dec_re = jnp.broadcast_to(lam_re, drive_term[:, :state_width].shape)
    dec_im = jnp.broadcast_to(lam_im, dec_re.shape)
    result = lax.associative_scan(complex_combine, (dec_re, dec_im, drive_term[:, :state_width], drive_term[:, state_width:]), axis=0)
    return jnp.concatenate([result[2], result[3]], axis=1)

def apply_layer(stream, valid_mask, total_valid, weights):
    gain_row, bias_row, proj_in, proj_out, rate_vec, step_vec, freq_vec, feed_vec, glu_mat, glu_vec = weights
    batch_mean = lax.optimization_barrier(jnp.sum(valid_mask * stream, axis=(0, 1))) / total_valid
    batch_var = lax.optimization_barrier(jnp.sum(valid_mask * stream * stream, axis=(0, 1))) / total_valid - batch_mean * batch_mean
    normed = low((stream - batch_mean) * lax.rsqrt(batch_var + epsilon) * gain_row + bias_row)
    mixed_sum = feed_vec * normed
    for heading in range(2):
        lam_re, lam_im, kap_re, kap_im = transition(rate_vec[heading], step_vec[heading], freq_vec[heading])
        projected = low_back(jnp.einsum('nth,hp->ntp', normed, proj_in[heading], precision=highest))
        state_width = lam_re.shape[0]
        proj_re = projected[..., :state_width]
        proj_im = projected[..., state_width:]
        drive_term = valid_mask * jnp.concatenate([kap_re * proj_re - kap_im * proj_im, kap_re * proj_im + kap_im * proj_re], axis=-1)
        if heading == 1:
            drive_term = drive_term[:, ::-1]
        scanner = jax.checkpoint(partial(sequence_scan, lam_re=lam_re, lam_im=lam_im))
        states = lax.map(scanner, drive_term)
        if heading == 1:
            states = states[:, ::-1]
        mixed_sum = mixed_sum + low_back(jnp.einsum('ntp,ph->nth', low(states), proj_out[heading], precision=highest))
    activated = low(jax.nn.gelu(mixed_sum))
    gate_logit = low_back(jnp.einsum('nth,hk->ntk', activated, glu_mat, precision=highest) + glu_vec)
    return (stream + valid_mask * activated * jax.nn.sigmoid(gate_logit), batch_mean, batch_var)

def reference(inputs, cotangent, lengths, bn_gain, bn_bias, in_proj, out_proj, lambda_rate, step_size, lambda_freq, feedthrough, glu_weight, glu_bias, running_mean, running_var):
    positions = jnp.arange(SEQLEN, dtype=jnp.int32)
    valid_mask = (positions[None, :] < lengths[:, None]).astype(jnp.float32)[..., None]
    total_valid = jnp.sum(valid_mask)
    weights = (bn_gain, bn_bias, in_proj.astype(jnp.float32), out_proj.astype(jnp.float32), lambda_rate, step_size, lambda_freq, feedthrough, glu_weight.astype(jnp.float32), glu_bias)

    def forward(stream, weights):
        layer_means = []
        layer_vars = []
        for layer_no in range(LAYERS):
            stream, batch_mean, batch_var = apply_layer(stream, valid_mask, total_valid, [item[layer_no] for item in weights])
            layer_means.append(batch_mean)
            layer_vars.append(batch_var)
        return (stream, (jnp.stack(layer_means), jnp.stack(layer_vars)))
    activations, pullback, moments = jax.vjp(forward, inputs.astype(jnp.float32), weights, has_aux=True)
    input_grad, gradients = pullback(cotangent.astype(jnp.float32))
    new_mean = momentum * running_mean + (1.0 - momentum) * moments[0]
    new_var = momentum * running_var + (1.0 - momentum) * moments[1]
    return (activations, input_grad, gradients[0], gradients[1], gradients[2], gradients[3], gradients[4], gradients[5], gradients[6], gradients[7], gradients[8], gradients[9], new_mean, new_var)
```

```python
import functools

import jax
import jax.numpy as jnp
from jax import lax
from jax.experimental import pallas as pl
from jax.experimental.pallas import tpu as pltpu
from jax.sharding import PartitionSpec as P

LAYERS = 2
EPSILON = 1e-05
MOMENTUM = 0.9
F32 = jnp.float32
BF16 = jnp.bfloat16
AXES = ("dir", "seq", "batch")
MESH = pl.DeviceIdType.MESH
LANES = 128
CHUNKS = 8
WIDE = 256
VMEM_BYTES = 62 << 20


def transition(rate_vec, step_vec, freq_vec):
    half_a = 0.5 * step_vec * rate_vec
    half_c = 0.5 * step_vec * freq_vec
    denominator = (1.0 + half_a) * (1.0 + half_a) + half_c * half_c
    lam_re = (1.0 - half_a * half_a - half_c * half_c) / denominator
    lam_im = 2.0 * half_c / denominator
    kap_re = step_vec * (1.0 + half_a) / denominator
    kap_im = step_vec * half_c / denominator
    return (lam_re, lam_im, kap_re, kap_im)


def dot(a, b, ca, cb):
    return lax.dot_general(a, b, (((ca,), (cb,)), ((), ())), preferred_element_type=F32)


def cmul(a, b):
    return (a[0] * b[0] - a[1] * b[1], a[0] * b[1] + a[1] * b[0])


def conj(a):
    return (a[0], -a[1])


def widen(mask):
    return jnp.concatenate([mask] * 4, axis=-1)


class Geometry:
    def __init__(self, sizes, local_shape, states):
        self.D, self.S, self.B = (sizes[a] for a in AXES)
        self.sizes = dict(sizes)
        self.seqs, self.T, self.H = local_shape
        self.Pn = states
        self.W = 2 * states
        self.J = self.T // CHUNKS
        self.N = self.D * self.S * self.B
        self.unit = 16 * self.S * self.B
        up = lambda n: -(-n // self.unit) * self.unit
        self.out_rows = (self.H // WIDE) * self.W
        self.half_rows = (self.H // WIDE) * (self.H // 2)
        self.in_rows = (self.Pn // LANES) * self.H
        self.used = {"X": self.out_rows + self.half_rows, "I": self.in_rows}
        self.rows = {k: up(v) for k, v in self.used.items()}
        self.colors = {}
        for k, n in self.rows.items():
            second = (n // 4) // self.unit * self.unit
            first = n - second
            colors = [(0, first, ("batch", "seq"))]
            if second:
                colors.append((first, second, ("seq", "batch")))
            self.colors[k] = colors


class Net:
    def __init__(self, geo, send_sems, recv_sems):
        self.geo, self.send_sems, self.recv_sems = geo, send_sems, recv_sems
        self.used_send = 0
        self.used_recv = 0
        self.at = {a: lax.axis_index(a) for a in AXES}
        self.unsent = []

    def send_sem(self):
        self.used_send += 1
        return self.send_sems.at[self.used_send - 1]

    def recv_sem(self):
        self.used_recv += 1
        return self.recv_sems.at[self.used_recv - 1]

    def index(self, axes):
        lin = 0
        for a in axes:
            lin = lin * self.geo.sizes[a] + self.at[a]
        return lin

    def count(self, axes):
        n = 1
        for a in axes:
            n *= self.geo.sizes[a]
        return n

    def peers(self, axes, act):
        n = self.count(axes)

        def at_offset(k):
            where, lin, rest, coords = {}, 0, k, []
            for a in reversed(axes):
                size = self.geo.sizes[a]
                off = rest % size
                rest = rest // size
                coords.append((a, lax.rem(self.at[a] + off, size)))
            for a, c in reversed(coords):
                where[a] = c
                lin = lin * self.geo.sizes[a] + c
            act(where, lin, k)

        if n <= 64:
            for k in range(n - 1, 0, -1):
                at_offset(k)
        else:

            def body(k, _):
                at_offset(k)
                return 0

            lax.fori_loop(1, n, body, 0)

    def put(self, src, dst, send, recv, peer):
        pltpu.make_async_remote_copy(
            src_ref=src, dst_ref=dst, send_sem=send, recv_sem=recv, device_id=peer, device_id_type=MESH
        ).start()

    def wait(self, ref, sem):
        pltpu.make_async_copy(ref, ref, sem).wait()

    def gather(self, src, land, axes):
        n = self.count(axes)
        send, recv = self.send_sem(), self.recv_sem()
        slot = self.index(axes)
        self.peers(axes, lambda peer, lin, k: self.put(src, land.at[slot], send, recv, peer))
        land[slot] = src[...]
        size = land.at[pl.ds(0, n - 1)]
        self.unsent.append((size, send))
        return functools.partial(self.wait, size, recv)

    def swap(self, pieces):
        peer = {"dir": 1 - self.at["dir"]}
        waits = []
        for src, dst, size in pieces:
            send, recv = self.send_sem(), self.recv_sem()
            self.put(src, dst, send, recv, peer)
            self.unsent.append((size, send))
            waits.append(functools.partial(self.wait, size, recv))
        return waits

    def finish(self):
        for size, send in self.unsent:
            self.wait(size, send)


def scratch_shapes(geo):
    T, H, W, J, S, N, Pn = geo.T, geo.H, geo.W, geo.J, geo.S, geo.N, geo.Pn
    L, D = LAYERS, geo.D
    v = {
        "mask": ((J, CHUNKS, LANES), F32),
        "win": ((L, D, H, W), BF16),
        "wout": ((L, D, W, H), BF16),
        "glw": ((L, H, H), BF16),
        "prm": ((3, D, L, 1, Pn), F32),
        "tab": ((L, D, 16, CHUNKS, Pn), F32),
        "xs": ((L + 1, J, CHUNKS, H), F32),
        "stat": ((16, H), F32),
        "nrm": ((L, T, H), BF16),
        "u": ((L, D, T, W), F32),
        "st": ((L, D, T + 32, W), BF16),
        "act": ((L, T, H), BF16),
        "sig": ((L, J, CHUNKS, H), BF16),
        "dge": ((L, J, CHUNKS, H), BF16),
        "tmp": ((J, CHUNKS, H), F32),
        "g": ((J, CHUNKS, H), F32),
        "dmx": ((J, CHUNKS, H), F32),
        "dml": ((T, H), BF16),
        "dgt": ((T, H), BF16),
        "ds": ((D, T, W), F32),
        "r": ((D, T, W), BF16),
        "msg0": ((2, H + LANES), F32),
        "land0": ((N, 2, H + LANES), F32),
        "msg": ((3, 2, H), F32),
        "land": ((3, N, 2, H), F32),
        "smsg": ((2 * L, 1, D * W), F32),
        "sland": ((2 * L, S, 1, D * W), F32),
        "tiny": ((L, 1, 2 * H + 4 * W), F32),
        "tland1": ((L, D * geo.B, 1, 2 * H + 4 * W), F32),
        "tmid": ((L, 1, 2 * H + 4 * W), F32),
        "tland2": ((L, S, 1, 2 * H + 4 * W), F32),
        "tsum": ((L, 1, 2 * H + 4 * W), F32),
        "glf": ((L, D, geo.half_rows, WIDE), BF16),
    }
    for k, rows in geo.rows.items():
        v["g" + k] = ((D, rows, WIDE), BF16)
        v["p" + k] = ((L, rows, WIDE), BF16)
        v["f" + k] = ((L, rows, WIDE), BF16)
        for c, (_, n, order) in enumerate(geo.colors[k]):
            n1, n2 = (geo.sizes[a] for a in order)
            v[f"a{k}{c}"] = ((L, n1 - 1, n // n1, WIDE), BF16)
            v[f"r{k}{c}"] = ((L, n // n1, WIDE), BF16)
            v[f"b{k}{c}"] = ((L, n2 - 1, n // n1 // n2, WIDE), BF16)
    return v


class Reduction:
    def __init__(self, geo, net, kind, layer, m):
        self.geo, self.net, self.kind, self.layer, self.m = geo, net, kind, layer, m
        self.rows = geo.rows[kind]
        self.colors = geo.colors[kind]
        self.full = m["f" + kind].at[layer]
        self.mine = m["g" + kind].at[net.at["dir"]]

    def pair_send(self):
        landing = self.m["p" + self.kind].at[self.layer]
        other = self.m["g" + self.kind].at[1 - self.net.at["dir"]]
        (self.pair_wait,) = self.net.swap([(other, landing, landing)])
        self.held = [self.net.unsent.pop()]

    def settle(self):
        for size, send in self.held:
            self.net.wait(size, send)

    def pair_done(self):
        self.pair_wait()
        landing = self.m["p" + self.kind].at[self.layer]
        block = 64

        def body(i, _):
            at = pl.ds(i * block, block)
            self.mine[at] = (self.mine[at].astype(F32) + landing[at].astype(F32)).astype(BF16)
            return 0

        lax.fori_loop(0, self.rows // block, body, 0)

    def scatter(self, axis, src, base, part, land):
        net, n = self.net, self.geo.sizes[axis]
        send, recv = net.send_sem(), net.recv_sem()
        net.peers(
            (axis,),
            lambda peer, lin, k: net.put(
                src.at[pl.ds(base + lin * part, part)], land.at[k - 1], send, recv, peer
            ),
        )
        net.unsent.append((land, send))
        return functools.partial(net.wait, land, recv)

    def add(self, own, own_at, land, n, out, out_at, part):
        block = 16

        def body(i, _):
            total = own[pl.ds(own_at + i * block, block)].astype(F32)
            for k in range(min(n - 1, 7)):
                total = total + land[k, pl.ds(i * block, block)].astype(F32)
            if n - 1 > 7:
                total = lax.fori_loop(
                    7, n - 1, lambda k, t: t + land[k, pl.ds(i * block, block)].astype(F32), total
                )
            out[pl.ds(out_at + i * block, block)] = total.astype(BF16)
            return 0

        lax.fori_loop(0, part // block, body, 0)

    def spread(self, axis, base, part):
        net, n = self.net, self.geo.sizes[axis]
        send, recv = net.send_sem(), net.recv_sem()
        mine = self.full.at[pl.ds(base, part)]
        net.peers((axis,), lambda peer, lin, k: net.put(mine, mine, send, recv, peer))
        size = self.full.at[pl.ds(0, (n - 1) * part)]
        net.unsent.append((size, send))
        return functools.partial(net.wait, size, recv)

    def buffers(self, c):
        return tuple(self.m[f"{x}{self.kind}{c}"].at[self.layer] for x in "arb")

    def parts(self, c):
        base, n, (first, second) = self.colors[c]
        part1 = n // self.geo.sizes[first]
        part2 = part1 // self.geo.sizes[second]
        at1 = base + self.net.at[first] * part1
        at2 = self.net.at[second] * part2
        return base, first, second, part1, part2, at1, at2

    def each(self, act):
        for c in range(len(self.colors)):
            act(c)

    def step1(self):
        self.wait1 = {}

        def act(c):
            base, first, _, part1, *_ = self.parts(c)
            self.wait1[c] = self.scatter(first, self.mine, base, part1, self.buffers(c)[0])
            self.held.append(self.net.unsent.pop())

        self.each(act)

    def step2(self):
        self.wait2 = {}

        def act(c):
            base, first, second, part1, part2, at1, at2 = self.parts(c)
            land1, red, land2 = self.buffers(c)
            self.wait1[c]()
            self.add(self.mine, at1, land1, self.geo.sizes[first], red, 0, part1)
            self.wait2[c] = self.scatter(second, red, 0, part2, land2)

        self.each(act)

    def step3(self):
        self.wait3 = {}

        def act(c):
            base, first, second, part1, part2, at1, at2 = self.parts(c)
            land1, red, land2 = self.buffers(c)
            self.wait2[c]()
            self.add(red, at2, land2, self.geo.sizes[second], self.full, at1 + at2, part2)
            self.wait3[c] = self.spread(second, at1 + at2, part2)

        self.each(act)

    def step4(self):
        self.wait4 = {}

        def act(c):
            base, first, second, part1, part2, at1, at2 = self.parts(c)
            self.wait3[c]()
            self.wait4[c] = self.spread(first, at1, part1)

        self.each(act)

    def done(self):
        self.each(lambda c: self.wait4[c]())


def body(geo, names, *refs):
    T, H, W, J, S, N, Pn = geo.T, geo.H, geo.W, geo.J, geo.S, geo.N, geo.Pn
    (lengths, inputs, cotangent, gain, bias, in_proj, out_proj, rate, step, freq, feed, gluw, glub, rmean, rvar) = refs[:15]
    (o_act, o_ig, o_gx, o_gl, o_gi, o_small, o_lam) = refs[15:22]
    scr = refs[22:]
    m = dict(zip(names, scr))
    m["xin"], m["cin"], m["pm"] = m["dgt"], m["dml"], m["r"].at[0, :, 0:T]
    send_sems, recv_sems, local_sems = scr[len(names) :]
    net = Net(geo, send_sems, recv_sems)
    me_d, me_s = net.at["dir"], net.at["seq"]
    local = [0]

    def fetch(src, dst):
        sem = local_sems.at[local[0]]
        local[0] += 1
        copy = pltpu.make_async_copy(src, dst, sem)
        copy.start()
        return copy.wait

    barrier = pltpu.get_barrier_semaphore()
    net.peers(AXES, lambda peer, lin, k: pl.semaphore_signal(barrier, 1, device_id=peer, device_id_type=MESH))
    w_x = fetch(inputs.at[me_d], m["xin"])
    w_c = fetch(cotangent.at[me_d], m["cin"])
    raw = (rate, step, freq)
    w_p = [fetch(raw[i], m["prm"].at[i, me_d]) for i in range(3)]
    w_in = [fetch(in_proj.at[l, 0], m["win"].at[l, me_d]) for l in range(LAYERS)]
    w_out = [fetch(out_proj.at[l, 0], m["wout"].at[l, me_d]) for l in range(LAYERS)]
    w_g = fetch(gluw, m["glw"])

    length = lengths[me_d]
    shape = (J, CHUNKS, LANES)
    position = (
        me_s * T
        + lax.broadcasted_iota(jnp.int32, shape, 1) * J
        + lax.broadcasted_iota(jnp.int32, shape, 0)
    )
    m["mask"][...] = jnp.where(position < length, 1.0, 0.0).astype(F32)

    def permutation(i, _):
        at = pl.ds(i * 64, 64)
        row = i * 64 + lax.broadcasted_iota(jnp.int32, (64, T), 0)
        col = lax.broadcasted_iota(jnp.int32, (64, T), 1)
        wanted = lax.rem(row, CHUNKS) * J + lax.div(row, CHUNKS)
        m["pm"][at] = jnp.where(col == wanted, 1.0, 0.0).astype(BF16)
        return 0

    lax.fori_loop(0, T // 64, permutation, 0)

    def product(a, b_at, ca, cb, n, out):
        def tile(i, _):
            at = pl.multiple_of(i * WIDE, WIDE)
            out(at, dot(a(), b_at(at), ca, cb))
            return 0

        lax.fori_loop(0, n // WIDE, tile, 0)

    def into(ref3):
        def store(at, value):
            ref3[:, :, pl.ds(at, WIDE)] = value.reshape(J, CHUNKS, WIDE)

        return store

    def reorder(src, dst):
        product(lambda: m["pm"][...], lambda at: src[:, pl.ds(at, WIDE)], 1, 0, H, into(dst))

    GROUP = 4
    ROWS = GROUP * CHUNKS

    def rows(ref, i):
        return ref[pl.ds(i * GROUP, GROUP)].astype(F32)

    def flat(ref, i):
        return ref[pl.ds(i * ROWS, ROWS)].astype(F32).reshape(GROUP, CHUNKS, -1)

    def put_flat(ref, i, value):
        ref[pl.ds(i * ROWS, ROWS)] = value.reshape(ROWS, -1).astype(BF16)

    def sweep(act, sums=0):
        zero = tuple(jnp.zeros((CHUNKS, H), F32) for _ in range(sums))

        def one(i, acc):
            more = act(i)
            if not sums:
                return acc
            return tuple(a + jnp.sum(v, axis=0) for a, v in zip(acc, more))

        acc = lax.fori_loop(0, T // ROWS, one, zero)
        return tuple(jnp.sum(a, axis=0, keepdims=True) for a in acc)

    def rep(row):
        return jnp.broadcast_to(row, (CHUNKS, row.shape[-1]))

    masked = lambda i: widen(rows(m["mask"], i))

    w_x()
    reorder(m["xin"], m["xs"].at[0])

    def first(i):
        x = rows(m["xs"].at[0], i)
        xm = x * masked(i)
        return xm, xm * x

    s1, s2 = sweep(first, 2)
    here = jnp.sum(jnp.sum(m["mask"][...], axis=0), axis=0, keepdims=True)
    m["msg0"][0:1, 0:H] = s1
    m["msg0"][1:2, 0:H] = s2
    m["msg0"][:, H:] = jnp.broadcast_to(here, (2, LANES))

    pl.semaphore_wait(barrier, N - 1)
    stats_wait = net.gather(m["msg0"], m["land0"], AXES)
    send_in, send_out = [None] * LAYERS, [None] * LAYERS
    prm_waits = net.swap([(raw[i], m["prm"].at[i, me_d], m["prm"].at[i, me_d]) for i in range(3)])
    for l in range(LAYERS):
        (send_in[l],) = net.swap([(in_proj.at[l, 0], m["win"].at[l, me_d], m["win"].at[l, me_d])])
        (send_out[l],) = net.swap([(out_proj.at[l, 0], m["wout"].at[l, me_d], m["wout"].at[l, me_d])])

    for w in w_p + prm_waits:
        w()
    for l in range(LAYERS):
        for dd in range(geo.D):
            lr, li, kr, ki = transition(*(m["prm"][i, dd, l] for i in range(3)))
            power = (lr, li)
            for _ in range((J).bit_length() - 1):
                power = cmul(power, power)
            ladder = [power]
            for _ in range(3):
                ladder.append(cmul(ladder[-1], ladder[-1]))
            wide = [tuple(rep(v) for v in p) for p in ladder]
            chunk = lax.broadcasted_iota(jnp.int32, (CHUNKS, Pn), 0)
            one = (jnp.ones((CHUNKS, Pn), F32), jnp.zeros((CHUNKS, Pn), F32))
            up, down = one, one
            for k in range(3):
                bit = lax.rem(lax.div(chunk, 1 << k), 2)
                grown = cmul(up, wide[k])
                up = tuple(jnp.where(bit == 1, a, b) for a, b in zip(grown, up))
                grown = cmul(down, wide[k])
                down = tuple(jnp.where(bit == 0, a, b) for a, b in zip(grown, down))
            table = [rep(lr), rep(li), *up, *down]
            for p in wide:
                table.extend(p)
            table.extend([rep(kr), rep(ki)])
            for k, v in enumerate(table):
                m["tab"][l, dd, k] = v

    def entry(l, dd, k, minus):
        re, im = m["tab"][l, dd, 2 * k], m["tab"][l, dd, 2 * k + 1]
        return (re, -im) if minus else (re, im)

    def fold(l):
        for dd in range(geo.D):
            kr, ki = m["tab"][l, dd, 14][0:1], m["tab"][l, dd, 15][0:1]

            def some(i, _):
                at = pl.ds(i * 16, 16)
                w = m["win"][l, dd, at].astype(F32)
                re, im = w[:, :Pn], w[:, Pn:]
                m["win"][l, dd, at] = jnp.concatenate([kr * re - ki * im, kr * im + ki * re], axis=1).astype(BF16)
                return 0

            lax.fori_loop(0, H // 16, some, 0)

    for l in range(LAYERS):
        w_in[l]()
        send_in[l]()
        fold(l)
        w_out[l]()
        send_out[l]()
    w_c()
    reorder(m["cin"], m["g"])
    w_g()

    def split(block):
        return block[:, :Pn], block[:, Pn:]

    def advance(lam, h, d):
        return (lam[0] * h[0] - lam[1] * h[1] + d[0], lam[0] * h[1] + lam[1] * h[0] + d[1])

    def scan(l, up_dd, src, minus, start, emit):
        dn_dd = 1 - up_dd
        lam_up, lam_dn = entry(l, up_dd, 0, minus), entry(l, dn_dd, 0, minus)
        n = T // 16

        def two(i, carry):
            hu, hd = carry[:2], carry[2:]
            at_u, at_d = i * 16, (n - 1 - i) * 16
            bu, bd = src[up_dd, pl.ds(at_u, 16)], src[dn_dd, pl.ds(at_d, 16)]
            keep_u, keep_d = [], []
            for k in range(2):
                hu = advance(lam_up, hu, split(bu[8 * k : 8 * k + 8]))
                hd = advance(lam_dn, hd, split(bd[8 - 8 * k : 16 - 8 * k]))
                keep_u.append(jnp.concatenate(hu, axis=1))
                keep_d.append(jnp.concatenate(hd, axis=1))
            if emit is not None:
                emit(up_dd, at_u, jnp.concatenate(keep_u, axis=0).astype(BF16))
                emit(dn_dd, at_d, jnp.concatenate(keep_d[::-1], axis=0).astype(BF16))
            return (*hu, *hd)

        out = lax.fori_loop(0, n, two, start, unroll=2)
        return out[:2], out[2:]

    chunk_at = lax.broadcasted_iota(jnp.int32, (CHUNKS, Pn), 0)

    def within(l, dd, ends, rising, minus):
        shift = (lambda v, k: pltpu.roll(v, k, 0)) if rising else (lambda v, k: pltpu.roll(v, CHUNKS - k, 0))
        inside = (lambda k: chunk_at >= k) if rising else (lambda k: chunk_at < CHUNKS - k)
        a = tuple(jnp.where(inside(1), shift(v, 1), 0.0) for v in ends)
        for k in range(3):
            far = tuple(jnp.where(inside(1 << k), shift(v, 1 << k), 0.0) for v in a)
            more = cmul(entry(l, dd, 3 + k, minus), far)
            a = (a[0] + more[0], a[1] + more[1])
        return a

    def carries(k, l, up_dd, ends_up, ends_dn, minus, meanwhile):
        dn_dd = 1 - up_dd
        pieces = [None] * geo.D
        for dd, ends, which in ((up_dd, ends_up, 2), (dn_dd, ends_dn, 1)):
            total = cmul(entry(l, dd, which, minus), ends)
            pieces[dd] = jnp.concatenate([jnp.sum(v, axis=0, keepdims=True) for v in total], axis=1)
        m["smsg"][k] = jnp.concatenate(pieces, axis=1)
        land = m["sland"].at[k]
        arrived = net.gather(m["smsg"].at[k], land, ("seq",))
        here_up = within(l, up_dd, ends_up, True, minus)
        here_dn = within(l, dn_dd, ends_dn, False, minus)
        meanwhile()
        arrived()

        def enter(dd, rising):
            whole = tuple(v[0:1] for v in entry(l, dd, 6, minus))
            zero = jnp.zeros((1, Pn), F32)

            def lap(i, state):
                at = i if rising else S - 1 - i
                piece = land[at][:, dd * W : (dd + 1) * W]
                new = advance(whole, state, split(piece))
                reached = (at < me_s) if rising else (at > me_s)
                return tuple(jnp.where(reached, a, b) for a, b in zip(new, state))

            state = (zero, zero)
            if S <= 8:
                for i in range(S):
                    state = lap(i, state)
                return state
            return lax.fori_loop(0, S, lap, state)

        outs = []
        for dd, rising, here_ends, which in ((up_dd, True, here_up, 1), (dn_dd, False, here_dn, 2)):
            far = cmul(entry(l, dd, which, minus), tuple(rep(v) for v in enter(dd, rising)))
            outs.append((here_ends[0] + far[0], here_ends[1] + far[1]))
        return outs

    zeros4 = tuple(jnp.zeros((CHUNKS, Pn), F32) for _ in range(4))
    nothing = lambda: None

    def stat(l, k):
        return m["stat"][4 * l + k : 4 * l + k + 1]

    def set_stat(l, k, value):
        m["stat"][4 * l + k : 4 * l + k + 1] = value

    c0 = 0.7978845608028654
    c1 = 0.044715
    for l in range(LAYERS):
        stats_wait()
        if l == 0:
            sums = jnp.sum(m["land0"][...], axis=0)
            m["stat"][15:16] = 1.0 / widen(sums[0:1, H:])
            sums = sums[:, :H]
        else:
            sums = jnp.sum(m["land"][0], axis=0)
        inv_count = m["stat"][15:16]
        mean = sums[0:1] * inv_count
        var = sums[1:2] * inv_count - mean * mean
        inv = lax.rsqrt(var + EPSILON)
        set_stat(l, 0, mean)
        set_stat(l, 1, inv)
        o_small[6 * l + 4 : 6 * l + 5] = MOMENTUM * rmean[l : l + 1] + (1.0 - MOMENTUM) * mean
        o_small[6 * l + 5 : 6 * l + 6] = MOMENTUM * rvar[l : l + 1] + (1.0 - MOMENTUM) * var
        v_mean, v_scale, v_bias = rep(mean), rep(inv * gain[l : l + 1]), rep(bias[l : l + 1])

        def normalise(i):
            x = rows(m["xs"].at[l], i)
            put_flat(m["nrm"].at[l], i, ((x - v_mean) * v_scale + v_bias) * masked(i))

        sweep(normalise)
        for dd in range(geo.D):

            def keep(at, value):
                m["u"][l, dd, :, pl.ds(at, WIDE)] = value

            product(lambda: m["nrm"][l], lambda at: m["win"][l, dd, :, pl.ds(at, WIDE)], 1, 0, W, keep)
        ends_up, ends_dn = scan(l, 0, m["u"].at[l], False, zeros4, None)
        in_up, in_dn = carries(l, l, 0, ends_up, ends_dn, False, nothing)
        both = lambda v: jnp.concatenate([jnp.concatenate(v, axis=1)] * 2, axis=0).astype(BF16)
        m["st"][l, 0, 0:16] = both(in_up)
        m["st"][l, 1, T + 16 : T + 32] = both(in_dn)

        def save(dd, at, value):
            m["st"][l, dd, pl.ds(16 + at, 16)] = value

        scan(l, 0, m["u"].at[l], False, (*in_up, *in_dn), save)

        def mix(i, _):
            at = pl.ds(pl.multiple_of(i * WIDE, WIDE), WIDE)
            total = dot(m["st"][l, 0, 16 : T + 16], m["wout"][l, 0, :, at], 1, 0)
            total = total + dot(m["st"][l, 1, 16 : T + 16], m["wout"][l, 1, :, at], 1, 0)
            m["tmp"][:, :, at] = total.reshape(J, CHUNKS, WIDE)
            return 0

        lax.fori_loop(0, H // WIDE, mix, 0)
        v_feed = rep(feed[l : l + 1])

        def activate(i):
            v = rows(m["tmp"], i) + v_feed * flat(m["nrm"].at[l], i)
            sq = v * v
            t = jnp.tanh(c0 * v * (1.0 + c1 * sq))
            half = 0.5 * (1.0 + t)
            put_flat(m["act"].at[l], i, v * half)
            slope = half + 0.5 * v * (1.0 - t * t) * (c0 * (1.0 + 3.0 * c1 * sq))
            m["dge"][l, pl.ds(i * GROUP, GROUP)] = slope.astype(BF16)

        sweep(activate)
        product(lambda: m["act"][l], lambda at: m["glw"][l, :, pl.ds(at, WIDE)], 1, 0, H, into(m["tmp"]))
        v_glub = rep(glub[l : l + 1])

        def gate(i):
            sig = 0.5 + 0.5 * jnp.tanh(0.5 * (rows(m["tmp"], i) + v_glub))
            m["sig"][l, pl.ds(i * GROUP, GROUP)] = sig.astype(BF16)
            mk = masked(i)
            x = rows(m["xs"].at[l], i) + mk * flat(m["act"].at[l], i) * sig
            m["xs"][l + 1, pl.ds(i * GROUP, GROUP)] = x
            if l + 1 < LAYERS:
                xm = x * mk
                return xm, xm * x

        sums = sweep(gate, 2 if l + 1 < LAYERS else 0)
        if l + 1 < LAYERS:
            m["msg"][0, 0:1] = sums[0]
            m["msg"][0, 1:2] = sums[1]
            stats_wait = net.gather(m["msg"].at[0], m["land"].at[0], AXES)

    out_waits = []

    def deliver(src, dst):
        send, recv = net.send_sem(), net.recv_sem()
        sem = local_sems.at[local[0]]
        local[0] += 1
        for c in range(CHUNKS):
            to = dst.at[me_d, pl.ds(c * J, J)]
            net.put(src.at[:, c], to, send, recv, {"dir": 1 - me_d})
            pltpu.make_async_copy(src.at[:, c], to, sem).start()
        net.unsent.append((dst.at[me_d], send))
        out_waits.append(functools.partial(net.wait, dst.at[1 - me_d], recv))
        out_waits.append(functools.partial(net.wait, dst.at[me_d], sem))

    deliver(m["xs"].at[LAYERS], o_act)

    reductions = {(k, l): Reduction(geo, net, k, l, m) for k in geo.rows for l in range(LAYERS)}

    def clear_rest(kind, l):
        used, rows_all = geo.used[kind], geo.rows[kind]
        if used < rows_all:
            for dd in range(geo.D):
                m["g" + kind][dd, used:rows_all] = jnp.zeros((rows_all - used, WIDE), BF16)

    def out_grads(l):
        if l + 1 < LAYERS:
            reductions["X", l + 1].settle()
        clear_rest("X", l)
        for dd in range(geo.D):

            def keep(i, _):
                at = pl.ds(pl.multiple_of(i * WIDE, WIDE), WIDE)
                value = dot(m["st"][l, dd, 16 : T + 16], m["dml"][:, at], 0, 0)
                m["gX"][dd, pl.ds(pl.multiple_of(i * W, 16), W)] = value.astype(BF16)
                return 0

            lax.fori_loop(0, H // WIDE, keep, 0)

        def keep_gate(i, _):
            at = pl.ds(pl.multiple_of(i * WIDE, WIDE), WIDE)
            value = dot(m["act"][l], m["dgt"][:, at], 0, 0).astype(BF16)
            half = H // 2
            for dd in range(2):
                m["gX"][dd, pl.ds(pl.multiple_of(geo.out_rows + i * half, 16), half)] = value[dd * half : (dd + 1) * half]
            return 0

        lax.fori_loop(0, H // WIDE, keep_gate, 0)

    def in_grads(l):
        if l + 1 < LAYERS:
            reductions["I", l + 1].settle()
        clear_rest("I", l)
        for dd in range(geo.D):

            def keep(i, _):
                at = pl.multiple_of(i * LANES, LANES)
                kr = m["tab"][l, dd, 14, 0:1, pl.ds(at, LANES)]
                ki = m["tab"][l, dd, 15, 0:1, pl.ds(at, LANES)]
                rhs = jnp.concatenate([m["r"][dd, :, pl.ds(at, LANES)], m["r"][dd, :, pl.ds(at + Pn, LANES)]], axis=1)
                value = dot(m["nrm"][l], rhs, 0, 0)
                re, im = value[:, :LANES], value[:, LANES:]
                value = jnp.concatenate([kr * re + ki * im, kr * im - ki * re], axis=1)
                m["gI"][dd, pl.ds(pl.multiple_of(i * H, 16), H)] = value.astype(BF16)
                return 0

            lax.fori_loop(0, Pn // LANES, keep, 0)

    def tiny_sums(l, d_glub, d_feed):
        m["tiny"][l, :, 0:H] = d_glub
        m["tiny"][l, :, H : 2 * H] = d_feed
        for dd in range(geo.D):

            def some(i, acc):
                at = i * 16
                rr, ri = split(m["r"][dd, pl.ds(at, 16)].astype(F32))
                ur, ui = split(m["u"][l, dd, pl.ds(at, 16)])
                cur = m["st"][l, dd, pl.ds(at + 16, 16)].astype(F32)
                if dd == 0:
                    near = m["st"][l, dd, pl.ds(at, 16)].astype(F32)
                    prev = jnp.concatenate([near[8:], cur[:8]], axis=0)
                else:
                    near = m["st"][l, dd, pl.ds(at + 32, 16)].astype(F32)
                    prev = jnp.concatenate([cur[8:], near[:8]], axis=0)
                hr, hi = split(prev)
                new = (rr * hr + ri * hi, ri * hr - rr * hi, rr * ur + ri * ui, ri * ur - rr * ui)
                return tuple(a + v[:8] + v[8:] for a, v in zip(acc, new))

            acc = lax.fori_loop(0, T // 16, some, zeros4)
            base = 2 * H + dd * 2 * W
            for k, v in enumerate(acc):
                m["tiny"][l, :, base + k * Pn : base + (k + 1) * Pn] = jnp.sum(v, axis=0, keepdims=True)
        return net.gather(m["tiny"].at[l], m["tland1"].at[l], ("dir", "batch"))

    def tiny_middle(l, wait):
        wait()
        m["tmid"][l] = jnp.sum(m["tland1"][l], axis=0)
        return net.gather(m["tmid"].at[l], m["tland2"].at[l], ("seq",))

    def tiny_end(l, wait):
        wait()
        m["tsum"][l] = jnp.sum(m["tland2"][l], axis=0)
        o_small[6 * l + 2 : 6 * l + 3] = m["tsum"][l, :, H : 2 * H]
        o_small[6 * l + 3 : 6 * l + 4] = m["tsum"][l, :, 0:H]
        base = pl.multiple_of(2 * H + me_d * 2 * W, LANES)
        dlr, dli, ar, ai = (m["tsum"][l, :, pl.ds(pl.multiple_of(base + k * Pn, LANES), Pn)] for k in range(4))
        kr, ki = m["tab"][l, me_d, 14][0:1], m["tab"][l, me_d, 15][0:1]
        size = kr * kr + ki * ki
        dkr, dki = (ar * kr - ai * ki) / size, (ar * ki + ai * kr) / size
        _, pull = jax.vjp(transition, *(m["prm"][i, me_d, l] for i in range(3)))
        for k, v in enumerate(pull((dlr, dli, dkr, dki))):
            o_lam[3 * l + k : 3 * l + k + 1] = v

    def gate_share(l):
        src = m["fX"].at[l, pl.ds(geo.out_rows, geo.half_rows)]
        dst = m["glf"].at[l, me_d]
        (wait,) = net.swap([(src, dst, dst)])
        m["glf"][l, me_d] = m["fX"][l, geo.out_rows : geo.out_rows + geo.half_rows]
        return wait

    tiny_wait = {}
    for l in reversed(range(LAYERS)):
        X, I = reductions["X", l], reductions["I", l]

        def open_gate(i):
            dout = rows(m["g"], i) * masked(i)
            sig = rows(m["sig"].at[l], i)
            v = (dout * flat(m["act"].at[l], i) * sig * (1.0 - sig)).astype(BF16)
            put_flat(m["dgt"], i, v)
            return (v.astype(F32),)

        (d_glub,) = sweep(open_gate, 1)
        product(lambda: m["dgt"][...], lambda at: m["glw"][l, pl.ds(at, WIDE)], 1, 1, H, into(m["tmp"]))

        def through(i):
            dout = rows(m["g"], i) * masked(i)
            d = (rows(m["tmp"], i) + dout * rows(m["sig"].at[l], i)) * rows(m["dge"].at[l], i)
            m["dmx"][pl.ds(i * GROUP, GROUP)] = d
            put_flat(m["dml"], i, d)
            return (d * flat(m["nrm"].at[l], i),)

        (d_feed,) = sweep(through, 1)
        for dd in range(geo.D):

            def keep(at, value):
                m["ds"][dd, :, pl.ds(at, WIDE)] = value

            product(lambda: m["dml"][...], lambda at: m["wout"][l, dd, pl.ds(at, WIDE)], 1, 1, W, keep)
        ends_up, ends_dn = scan(l, 1, m["ds"], True, zeros4, None)

        def window():
            out_grads(l)
            X.pair_send()
            if l == 0:
                reductions["I", 1].step2()
                reductions["X", 1].step3()
                tiny_wait[1] = tiny_middle(1, tiny_wait[1])

        in_up, in_dn = carries(LAYERS + l, l, 1, ends_up, ends_dn, True, window)

        def save(dd, at, value):
            m["r"][dd, pl.ds(at, 16)] = value

        scan(l, 1, m["ds"], True, (*in_up, *in_dn), save)

        def back(i, _):
            at = pl.ds(pl.multiple_of(i * WIDE, WIDE), WIDE)
            total = dot(m["r"][0], m["win"][l, 0, at], 1, 1)
            total = total + dot(m["r"][1], m["win"][l, 1, at], 1, 1)
            m["tmp"][:, :, at] = total.reshape(J, CHUNKS, WIDE)
            return 0

        lax.fori_loop(0, H // WIDE, back, 0)
        v_feed, v_mean, v_inv = rep(feed[l : l + 1]), rep(stat(l, 0)), rep(stat(l, 1))

        def normed_grad(i):
            d = (v_feed * rows(m["dmx"], i) + rows(m["tmp"], i)) * masked(i)
            m["tmp"][pl.ds(i * GROUP, GROUP)] = d
            return d, d * ((rows(m["xs"].at[l], i) - v_mean) * v_inv)

        plain, scaled = sweep(normed_grad, 2)
        slot = 1 + l
        m["msg"][slot, 0:1] = plain
        m["msg"][slot, 1:2] = scaled
        arrived = net.gather(m["msg"].at[slot], m["land"].at[slot], AXES)
        X.pair_done()
        X.step1()
        in_grads(l)
        I.pair_send()
        tiny_wait[l] = tiny_sums(l, d_glub, d_feed)
        if l == 0:
            reductions["X", 1].step4()
            reductions["I", 1].step3()
        I.pair_done()
        I.step1()
        if l > 0:
            X.step2()
        arrived()
        sums = jnp.sum(m["land"][slot], axis=0)
        plain, scaled = sums[0:1], sums[1:2]
        o_small[6 * l + 0 : 6 * l + 1] = scaled
        o_small[6 * l + 1 : 6 * l + 2] = plain
        inv = stat(l, 1)
        inv_count = m["stat"][15:16]
        v_scale = rep(inv * gain[l : l + 1])
        v_plain, v_scaled = rep(plain * inv_count), rep(scaled * inv_count * inv)

        def stream_grad(i):
            lead = rows(m["tmp"], i) - masked(i) * (v_plain + (rows(m["xs"].at[l], i) - v_mean) * v_scaled)
            at = pl.ds(i * GROUP, GROUP)
            m["g"][at] = m["g"][at] + v_scale * lead

        sweep(stream_grad)

    deliver(m["g"], o_ig)

    X1, I1, X0, I0 = (reductions[k, l] for l in (1, 0) for k in ("X", "I"))
    tails = []

    def hand_out(red, dst):
        tails.append(fetch(red.full, dst))

    X1.done()
    hand_out(X1, o_gx.at[1])
    g1 = gate_share(1)
    X0.step2()
    I1.step4()
    tiny_wait[0] = tiny_middle(0, tiny_wait[0])
    tiny_end(1, tiny_wait[1])
    I0.step2()
    X0.step3()
    I1.done()
    hand_out(I1, o_gi.at[1])
    I0.step3()
    X0.step4()
    tiny_end(0, tiny_wait[0])
    g1()
    tails.append(fetch(m["glf"].at[1], o_gl.at[1]))
    I0.step4()
    X0.done()
    hand_out(X0, o_gx.at[0])
    g0 = gate_share(0)
    I0.done()
    hand_out(I0, o_gi.at[0])
    g0()
    tails.append(fetch(m["glf"].at[0], o_gl.at[0]))
    for k in geo.rows:
        reductions[k, 0].settle()
    for w in tails + out_waits:
        w()
    net.finish()


def on_device(sizes, inputs, cotangent, lengths, gain, bias, in_proj, out_proj, rate, step, freq, feed, gluw, glub, rmean, rvar):
    geo = Geometry(sizes, inputs.shape, rate.shape[-1])
    T, H, W = geo.T, geo.H, geo.W
    v = scratch_shapes(geo)
    hbm = pl.BlockSpec(memory_space=pl.ANY)
    vmem = pl.BlockSpec(memory_space=pltpu.VMEM)
    smem = pl.BlockSpec(memory_space=pltpu.SMEM)
    outs = [
        jax.ShapeDtypeStruct((geo.seqs, T, H), F32),
        jax.ShapeDtypeStruct((geo.seqs, T, H), F32),
        jax.ShapeDtypeStruct((LAYERS, geo.rows["X"], WIDE), BF16),
        jax.ShapeDtypeStruct((LAYERS, geo.D, geo.half_rows, WIDE), BF16),
        jax.ShapeDtypeStruct((LAYERS, geo.rows["I"], WIDE), BF16),
        jax.ShapeDtypeStruct((6 * LAYERS, H), F32),
        jax.ShapeDtypeStruct((3 * LAYERS, geo.Pn), F32),
    ]
    act, ig, gx, gl, gi, small, lam = pl.pallas_call(
        functools.partial(body, geo, tuple(v)),
        out_shape=outs,
        in_specs=[smem, hbm, hbm, vmem, vmem, hbm, hbm, hbm, hbm, hbm, vmem, hbm, vmem, vmem, vmem],
        out_specs=[hbm, hbm, hbm, hbm, hbm, vmem, vmem],
        scratch_shapes=[pltpu.VMEM(*s) for s in v.values()]
        + [pltpu.SemaphoreType.DMA((64,)), pltpu.SemaphoreType.DMA((64,)), pltpu.SemaphoreType.DMA((32,))],
        compiler_params=pltpu.CompilerParams(
            collective_id=0, has_side_effects=True, vmem_limit_bytes=VMEM_BYTES
        ),
    )(lengths, inputs, cotangent, gain, bias, in_proj, out_proj, rate, step, freq, feed, gluw, glub, rmean, rvar)
    L = LAYERS
    g_in = gi[:, : geo.in_rows].reshape(L, geo.Pn // LANES, H, 2, LANES)
    g_in = g_in.transpose(0, 2, 3, 1, 4).reshape(L, 1, H, W).astype(F32)
    g_out = gx[:, : geo.out_rows].reshape(L, H // WIDE, W, WIDE)
    g_out = g_out.transpose(0, 2, 1, 3).reshape(L, 1, W, H).astype(F32)
    g_glu = gl.reshape(L, 2, H // WIDE, H // 2, WIDE).transpose(0, 1, 3, 2, 4).reshape(L, H, H).astype(F32)
    small = small.reshape(L, 6, H)
    lam = lam.reshape(L, 3, 1, geo.Pn)
    return (
        act,
        ig,
        small[:, 0],
        small[:, 1],
        g_in,
        g_out,
        lam[:, 0],
        lam[:, 1],
        lam[:, 2],
        small[:, 2],
        g_glu,
        small[:, 3],
        small[:, 4],
        small[:, 5],
    )


def solution(mesh):
    tokens = P("batch", "seq", None)
    per_dir = P(None, "dir", None)
    mats = P(None, "dir", None, None)
    in_specs = (tokens, tokens, P("batch"), P(), P(), mats, mats, per_dir, per_dir, per_dir) + (P(),) * 5
    out_specs = (tokens, tokens, P(), P(), mats, mats, per_dir, per_dir, per_dir) + (P(),) * 5
    return jax.shard_map(
        functools.partial(on_device, dict(mesh.shape)),
        mesh=mesh,
        in_specs=in_specs,
        out_specs=out_specs,
        check_vma=False,
    )
```

```python
import functools
import math

import jax
import jax.numpy as jnp
from jax import lax
from jax.experimental import pallas as pl
from jax.experimental.pallas import tpu as pltpu
from jax.sharding import PartitionSpec as P

LAYERS = 2
EPSILON = 1e-05
MOMENTUM = 0.9
F32 = jnp.float32
BF16 = jnp.bfloat16
AXES = ("dir", "seq", "batch")
MESH = pl.DeviceIdType.MESH
LANES = 128
CHUNKS = 8
WIDE = 256
SPARE_BYTES = 5 << 19


def transition(rate_vec, step_vec, freq_vec):
    half_a = 0.5 * step_vec * rate_vec
    half_c = 0.5 * step_vec * freq_vec
    denominator = (1.0 + half_a) * (1.0 + half_a) + half_c * half_c
    lam_re = (1.0 - half_a * half_a - half_c * half_c) / denominator
    lam_im = 2.0 * half_c / denominator
    kap_re = step_vec * (1.0 + half_a) / denominator
    kap_im = step_vec * half_c / denominator
    return (lam_re, lam_im, kap_re, kap_im)


def dot(a, b, ca, cb):
    return lax.dot_general(a, b, (((ca,), (cb,)), ((), ())), preferred_element_type=F32)


def cmul(a, b):
    return (a[0] * b[0] - a[1] * b[1], a[0] * b[1] + a[1] * b[0])


def conj(a):
    return (a[0], -a[1])


def widen(mask):
    return jnp.concatenate([mask] * 4, axis=-1)


class Geometry:
    def __init__(self, sizes, local_shape, states):
        self.D, self.S, self.B = (sizes[a] for a in AXES)
        self.sizes = dict(sizes)
        self.seqs, self.T, self.H = local_shape
        self.Pn = states
        self.W = 2 * states
        self.J = self.T // CHUNKS
        self.N = self.D * self.S * self.B
        self.unit = 16 * self.S * self.B
        up = lambda n: -(-n // self.unit) * self.unit
        self.out_rows = (self.H // WIDE) * self.W
        self.half_rows = (self.H // WIDE) * (self.H // 2)
        self.in_rows = (self.Pn // LANES) * self.H
        self.used = {"X": self.out_rows + self.half_rows, "I": self.in_rows}
        self.rows = {k: up(v) for k, v in self.used.items()}
        self.colors = {}
        for k, n in self.rows.items():
            second = (n // 4) // self.unit * self.unit
            first = n - second
            colors = [(0, first, ("batch", "seq"))]
            if second:
                colors.append((first, second, ("seq", "batch")))
            self.colors[k] = colors


class Net:
    def __init__(self, geo, send_sems, recv_sems):
        self.geo, self.send_sems, self.recv_sems = geo, send_sems, recv_sems
        self.used_send = 0
        self.used_recv = 0
        self.at = {a: lax.axis_index(a) for a in AXES}
        self.unsent = []

    def send_sem(self):
        self.used_send += 1
        return self.send_sems.at[self.used_send - 1]

    def recv_sem(self):
        self.used_recv += 1
        return self.recv_sems.at[self.used_recv - 1]

    def index(self, axes):
        lin = 0
        for a in axes:
            lin = lin * self.geo.sizes[a] + self.at[a]
        return lin

    def count(self, axes):
        n = 1
        for a in axes:
            n *= self.geo.sizes[a]
        return n

    def peers(self, axes, act):
        n = self.count(axes)

        def at_offset(k):
            where, lin, rest, coords = {}, 0, k, []
            for a in reversed(axes):
                size = self.geo.sizes[a]
                off = rest % size
                rest = rest // size
                coords.append((a, lax.rem(self.at[a] + off, size)))
            for a, c in reversed(coords):
                where[a] = c
                lin = lin * self.geo.sizes[a] + c
            act(where, lin, k)

        if n <= 64:
            for k in range(n - 1, 0, -1):
                at_offset(k)
        else:

            def body(k, _):
                at_offset(k)
                return 0

            lax.fori_loop(1, n, body, 0)

    def put(self, src, dst, send, recv, peer):
        pltpu.make_async_remote_copy(
            src_ref=src, dst_ref=dst, send_sem=send, recv_sem=recv, device_id=peer, device_id_type=MESH
        ).start()

    def wait(self, ref, sem):
        pltpu.make_async_copy(ref, ref, sem).wait()

    def gather(self, src, land, axes):
        n = self.count(axes)
        send, recv = self.send_sem(), self.recv_sem()
        slot = self.index(axes)
        self.peers(axes, lambda peer, lin, k: self.put(src, land.at[slot], send, recv, peer))
        land[slot] = src[...]
        size = land.at[pl.ds(0, n - 1)]
        self.unsent.append((size, send))
        return functools.partial(self.wait, size, recv)

    def swap(self, pieces):
        peer = {"dir": 1 - self.at["dir"]}
        waits = []
        for src, dst, size in pieces:
            send, recv = self.send_sem(), self.recv_sem()
            self.put(src, dst, send, recv, peer)
            self.unsent.append((size, send))
            waits.append(functools.partial(self.wait, size, recv))
        return waits

    def finish(self):
        for size, send in self.unsent:
            self.wait(size, send)


def scratch_shapes(geo):
    T, H, W, J, S, N, Pn = geo.T, geo.H, geo.W, geo.J, geo.S, geo.N, geo.Pn
    L, D = LAYERS, geo.D
    v = {
        "mask": ((J, CHUNKS, LANES), F32),
        "win": ((L, D, H, W), BF16),
        "wout": ((L, D, W, H), BF16),
        "glw": ((L, H, H), BF16),
        "prm": ((3, D, L, 1, Pn), F32),
        "tab": ((L, D, 16, CHUNKS, Pn), F32),
        "xs": ((L + 1, J, CHUNKS, H), F32),
        "stat": ((16, H), F32),
        "nrm": ((L, T, H), BF16),
        "u": ((L, D, T, W), F32),
        "st": ((L, D, T + 32, W), BF16),
        "act": ((L, T, H), BF16),
        "sig": ((L, J, CHUNKS, H), BF16),
        "dge": ((L, J, CHUNKS, H), BF16),
        "tmp": ((J, CHUNKS, H), F32),
        "g": ((J, CHUNKS, H), F32),
        "dmx": ((J, CHUNKS, H), F32),
        "dml": ((T, H), BF16),
        "dgt": ((T, H), BF16),
        "ds": ((D, T, W), F32),
        "r": ((D, T, W), BF16),
        "msg0": ((2, H + LANES), F32),
        "land0": ((N, 2, H + LANES), F32),
        "msg": ((3, 2, H), F32),
        "land": ((3, N, 2, H), F32),
        "smsg": ((2 * L, 1, D * W), F32),
        "sland": ((2 * L, S, 1, D * W), F32),
        "tiny": ((L, 1, 2 * H + 4 * W), F32),
        "tland1": ((L, D * geo.B, 1, 2 * H + 4 * W), F32),
        "tmid": ((L, 1, 2 * H + 4 * W), F32),
        "tland2": ((L, S, 1, 2 * H + 4 * W), F32),
        "tsum": ((L, 1, 2 * H + 4 * W), F32),
    }
    for k, rows in geo.rows.items():
        v["g" + k] = ((D, rows, WIDE), BF16)
        v["p" + k] = ((L, rows, WIDE), BF16)
        for c, (_, n, order) in enumerate(geo.colors[k]):
            n1, n2 = (geo.sizes[a] for a in order)
            v[f"a{k}{c}"] = ((L, n1 - 1, n // n1, WIDE), BF16)
            v[f"r{k}{c}"] = ((L, n // n1, WIDE), BF16)
            v[f"b{k}{c}"] = ((L, n2 - 1, n // n1 // n2, WIDE), BF16)
    return v


class Reduction:
    def __init__(self, geo, net, kind, layer, m):
        self.geo, self.net, self.kind, self.layer, self.m = geo, net, kind, layer, m
        self.rows = geo.rows[kind]
        self.colors = geo.colors[kind]
        self.full = m["f" + kind].at[layer]
        self.mine = m["g" + kind].at[net.at["dir"]]

    def pair_send(self):
        landing = self.m["p" + self.kind].at[self.layer]
        other = self.m["g" + self.kind].at[1 - self.net.at["dir"]]
        (self.pair_wait,) = self.net.swap([(other, landing, landing)])
        self.held = [self.net.unsent.pop()]

    def settle(self):
        for size, send in self.held:
            self.net.wait(size, send)

    def pair_done(self):
        self.pair_wait()
        landing = self.m["p" + self.kind].at[self.layer]
        block = 64

        def body(i, _):
            at = pl.ds(i * block, block)
            self.mine[at] = (self.mine[at].astype(F32) + landing[at].astype(F32)).astype(BF16)
            return 0

        lax.fori_loop(0, self.rows // block, body, 0)

    def scatter(self, axis, src, base, part, land):
        net, n = self.net, self.geo.sizes[axis]
        send, recv = net.send_sem(), net.recv_sem()
        net.peers(
            (axis,),
            lambda peer, lin, k: net.put(
                src.at[pl.ds(base + lin * part, part)], land.at[k - 1], send, recv, peer
            ),
        )
        net.unsent.append((land, send))
        return functools.partial(net.wait, land, recv)

    def add(self, own, own_at, land, n, out, out_at, part):
        block = 16

        def body(i, _):
            total = own[pl.ds(own_at + i * block, block)].astype(F32)
            for k in range(min(n - 1, 7)):
                total = total + land[k, pl.ds(i * block, block)].astype(F32)
            if n - 1 > 7:
                total = lax.fori_loop(
                    7, n - 1, lambda k, t: t + land[k, pl.ds(i * block, block)].astype(F32), total
                )
            out[pl.ds(out_at + i * block, block)] = total.astype(BF16)
            return 0

        lax.fori_loop(0, part // block, body, 0)

    def spread(self, axis, base, part):
        net, n = self.net, self.geo.sizes[axis]
        send, recv = net.send_sem(), net.recv_sem()
        mine = self.full.at[pl.ds(base, part)]
        net.peers((axis,), lambda peer, lin, k: net.put(mine, mine, send, recv, peer))
        size = self.full.at[pl.ds(0, (n - 1) * part)]
        net.unsent.append((size, send))
        return functools.partial(net.wait, size, recv)

    def buffers(self, c):
        return tuple(self.m[f"{x}{self.kind}{c}"].at[self.layer] for x in "arb")

    def parts(self, c):
        base, n, (first, second) = self.colors[c]
        part1 = n // self.geo.sizes[first]
        part2 = part1 // self.geo.sizes[second]
        at1 = base + self.net.at[first] * part1
        at2 = self.net.at[second] * part2
        return base, first, second, part1, part2, at1, at2

    def each(self, act):
        for c in range(len(self.colors)):
            act(c)

    def step1(self):
        self.wait1 = {}

        def act(c):
            base, first, _, part1, *_ = self.parts(c)
            self.wait1[c] = self.scatter(first, self.mine, base, part1, self.buffers(c)[0])
            self.held.append(self.net.unsent.pop())

        self.each(act)

    def step2(self):
        self.wait2 = {}

        def act(c):
            base, first, second, part1, part2, at1, at2 = self.parts(c)
            land1, red, land2 = self.buffers(c)
            self.wait1[c]()
            self.add(self.mine, at1, land1, self.geo.sizes[first], red, 0, part1)
            self.wait2[c] = self.scatter(second, red, 0, part2, land2)

        self.each(act)

    def step3(self):
        self.wait3 = {}

        def act(c):
            base, first, second, part1, part2, at1, at2 = self.parts(c)
            land1, red, land2 = self.buffers(c)
            self.wait2[c]()
            self.add(red, at2, land2, self.geo.sizes[second], self.full, at1 + at2, part2)
            self.wait3[c] = self.spread(second, at1 + at2, part2)

        self.each(act)

    def step4(self):
        self.wait4 = {}

        def act(c):
            base, first, second, part1, part2, at1, at2 = self.parts(c)
            self.wait3[c]()
            self.wait4[c] = self.spread(first, at1, part1)

        self.each(act)

    def done(self):
        self.each(lambda c: self.wait4[c]())


def body(geo, names, *refs):
    T, H, W, J, S, N, Pn = geo.T, geo.H, geo.W, geo.J, geo.S, geo.N, geo.Pn
    (lengths, inputs, cotangent, gain, bias, in_proj, out_proj, rate, step, freq, feed, gluw, glub, rmean, rvar) = refs[:15]
    (o_act, o_ig, o_gx, o_gl, o_gi, o_small, o_lam) = refs[15:22]
    scr = refs[22:]
    m = dict(zip(names, scr))
    m["fX"], m["fI"], m["glf"] = o_gx, o_gi, o_gl
    m["xin"], m["cin"], m["pm"] = m["dgt"], m["dml"], m["r"].at[0, :, 0:T]
    send_sems, recv_sems, local_sems = scr[len(names) :]
    net = Net(geo, send_sems, recv_sems)
    me_d, me_s = net.at["dir"], net.at["seq"]
    local = [0]

    def fetch(src, dst):
        sem = local_sems.at[local[0]]
        local[0] += 1
        copy = pltpu.make_async_copy(src, dst, sem)
        copy.start()
        return copy.wait

    barrier = pltpu.get_barrier_semaphore()
    net.peers(AXES, lambda peer, lin, k: pl.semaphore_signal(barrier, 1, device_id=peer, device_id_type=MESH))
    w_x = fetch(inputs.at[me_d], m["xin"])
    w_c = fetch(cotangent.at[me_d], m["cin"])
    raw = (rate, step, freq)
    w_p = [fetch(raw[i], m["prm"].at[i, me_d]) for i in range(3)]
    w_in = [fetch(in_proj.at[l, 0], m["win"].at[l, me_d]) for l in range(LAYERS)]
    w_out = [fetch(out_proj.at[l, 0], m["wout"].at[l, me_d]) for l in range(LAYERS)]
    w_g = fetch(gluw, m["glw"])

    length = lengths[me_d]
    shape = (J, CHUNKS, LANES)
    position = (
        me_s * T
        + lax.broadcasted_iota(jnp.int32, shape, 1) * J
        + lax.broadcasted_iota(jnp.int32, shape, 0)
    )
    m["mask"][...] = jnp.where(position < length, 1.0, 0.0).astype(F32)

    def permutation(i, _):
        at = pl.ds(i * 64, 64)
        row = i * 64 + lax.broadcasted_iota(jnp.int32, (64, T), 0)
        col = lax.broadcasted_iota(jnp.int32, (64, T), 1)
        wanted = lax.rem(row, CHUNKS) * J + lax.div(row, CHUNKS)
        m["pm"][at] = jnp.where(col == wanted, 1.0, 0.0).astype(BF16)
        return 0

    lax.fori_loop(0, T // 64, permutation, 0)

    def product(a, b_at, ca, cb, n, out):
        def tile(i, _):
            at = pl.multiple_of(i * WIDE, WIDE)
            out(at, dot(a(), b_at(at), ca, cb))
            return 0

        lax.fori_loop(0, n // WIDE, tile, 0)

    def into(ref3):
        def store(at, value):
            ref3[:, :, pl.ds(at, WIDE)] = value.reshape(J, CHUNKS, WIDE)

        return store

    def reorder(src, dst):
        product(lambda: m["pm"][...], lambda at: src[:, pl.ds(at, WIDE)], 1, 0, H, into(dst))

    GROUP = 4
    ROWS = GROUP * CHUNKS

    def rows(ref, i):
        return ref[pl.ds(i * GROUP, GROUP)].astype(F32)

    def flat(ref, i):
        return ref[pl.ds(i * ROWS, ROWS)].astype(F32).reshape(GROUP, CHUNKS, -1)

    def put_flat(ref, i, value):
        ref[pl.ds(i * ROWS, ROWS)] = value.reshape(ROWS, -1).astype(BF16)

    def sweep(act, sums=0):
        zero = tuple(jnp.zeros((CHUNKS, H), F32) for _ in range(sums))

        def one(i, acc):
            more = act(i)
            if not sums:
                return acc
            return tuple(a + jnp.sum(v, axis=0) for a, v in zip(acc, more))

        acc = lax.fori_loop(0, T // ROWS, one, zero)
        return tuple(jnp.sum(a, axis=0, keepdims=True) for a in acc)

    def rep(row):
        return jnp.broadcast_to(row, (CHUNKS, row.shape[-1]))

    masked = lambda i: widen(rows(m["mask"], i))

    w_x()
    reorder(m["xin"], m["xs"].at[0])

    def first(i):
        x = rows(m["xs"].at[0], i)
        xm = x * masked(i)
        return xm, xm * x

    s1, s2 = sweep(first, 2)
    here = jnp.sum(jnp.sum(m["mask"][...], axis=0), axis=0, keepdims=True)
    m["msg0"][0:1, 0:H] = s1
    m["msg0"][1:2, 0:H] = s2
    m["msg0"][:, H:] = jnp.broadcast_to(here, (2, LANES))

    pl.semaphore_wait(barrier, N - 1)
    stats_wait = net.gather(m["msg0"], m["land0"], AXES)
    send_in, send_out = [None] * LAYERS, [None] * LAYERS
    prm_waits = net.swap([(raw[i], m["prm"].at[i, me_d], m["prm"].at[i, me_d]) for i in range(3)])
    for l in range(LAYERS):
        (send_in[l],) = net.swap([(in_proj.at[l, 0], m["win"].at[l, me_d], m["win"].at[l, me_d])])
        (send_out[l],) = net.swap([(out_proj.at[l, 0], m["wout"].at[l, me_d], m["wout"].at[l, me_d])])

    for w in w_p + prm_waits:
        w()
    for l in range(LAYERS):
        for dd in range(geo.D):
            lr, li, kr, ki = transition(*(m["prm"][i, dd, l] for i in range(3)))
            power = (lr, li)
            for _ in range((J).bit_length() - 1):
                power = cmul(power, power)
            ladder = [power]
            for _ in range(3):
                ladder.append(cmul(ladder[-1], ladder[-1]))
            wide = [tuple(rep(v) for v in p) for p in ladder]
            chunk = lax.broadcasted_iota(jnp.int32, (CHUNKS, Pn), 0)
            one = (jnp.ones((CHUNKS, Pn), F32), jnp.zeros((CHUNKS, Pn), F32))
            up, down = one, one
            for k in range(3):
                bit = lax.rem(lax.div(chunk, 1 << k), 2)
                grown = cmul(up, wide[k])
                up = tuple(jnp.where(bit == 1, a, b) for a, b in zip(grown, up))
                grown = cmul(down, wide[k])
                down = tuple(jnp.where(bit == 0, a, b) for a, b in zip(grown, down))
            table = [rep(lr), rep(li), *up, *down]
            for p in wide:
                table.extend(p)
            table.extend([rep(kr), rep(ki)])
            for k, v in enumerate(table):
                m["tab"][l, dd, k] = v

    def entry(l, dd, k, minus):
        re, im = m["tab"][l, dd, 2 * k], m["tab"][l, dd, 2 * k + 1]
        return (re, -im) if minus else (re, im)

    def fold(l):
        for dd in range(geo.D):
            kr, ki = m["tab"][l, dd, 14][0:1], m["tab"][l, dd, 15][0:1]

            def some(i, _):
                at = pl.ds(i * 16, 16)
                w = m["win"][l, dd, at].astype(F32)
                re, im = w[:, :Pn], w[:, Pn:]
                m["win"][l, dd, at] = jnp.concatenate([kr * re - ki * im, kr * im + ki * re], axis=1).astype(BF16)
                return 0

            lax.fori_loop(0, H // 16, some, 0)

    for l in range(LAYERS):
        w_in[l]()
        send_in[l]()
        fold(l)
        w_out[l]()
        send_out[l]()
    w_c()
    reorder(m["cin"], m["g"])
    w_g()

    def split(block):
        return block[:, :Pn], block[:, Pn:]

    def advance(lam, h, d):
        return (lam[0] * h[0] - lam[1] * h[1] + d[0], lam[0] * h[1] + lam[1] * h[0] + d[1])

    def scan(l, up_dd, src, minus, start, emit):
        dn_dd = 1 - up_dd
        lam_up, lam_dn = entry(l, up_dd, 0, minus), entry(l, dn_dd, 0, minus)
        n = T // 16

        def two(i, carry):
            hu, hd = carry[:2], carry[2:]
            at_u, at_d = i * 16, (n - 1 - i) * 16
            bu, bd = src[up_dd, pl.ds(at_u, 16)], src[dn_dd, pl.ds(at_d, 16)]
            keep_u, keep_d = [], []
            for k in range(2):
                hu = advance(lam_up, hu, split(bu[8 * k : 8 * k + 8]))
                hd = advance(lam_dn, hd, split(bd[8 - 8 * k : 16 - 8 * k]))
                keep_u.append(jnp.concatenate(hu, axis=1))
                keep_d.append(jnp.concatenate(hd, axis=1))
            if emit is not None:
                emit(up_dd, at_u, jnp.concatenate(keep_u, axis=0).astype(BF16))
                emit(dn_dd, at_d, jnp.concatenate(keep_d[::-1], axis=0).astype(BF16))
            return (*hu, *hd)

        out = lax.fori_loop(0, n, two, start, unroll=2)
        return out[:2], out[2:]

    chunk_at = lax.broadcasted_iota(jnp.int32, (CHUNKS, Pn), 0)

    def within(l, dd, ends, rising, minus):
        shift = (lambda v, k: pltpu.roll(v, k, 0)) if rising else (lambda v, k: pltpu.roll(v, CHUNKS - k, 0))
        inside = (lambda k: chunk_at >= k) if rising else (lambda k: chunk_at < CHUNKS - k)
        a = tuple(jnp.where(inside(1), shift(v, 1), 0.0) for v in ends)
        for k in range(3):
            far = tuple(jnp.where(inside(1 << k), shift(v, 1 << k), 0.0) for v in a)
            more = cmul(entry(l, dd, 3 + k, minus), far)
            a = (a[0] + more[0], a[1] + more[1])
        return a

    def carries(k, l, up_dd, ends_up, ends_dn, minus, meanwhile):
        dn_dd = 1 - up_dd
        pieces = [None] * geo.D
        for dd, ends, which in ((up_dd, ends_up, 2), (dn_dd, ends_dn, 1)):
            total = cmul(entry(l, dd, which, minus), ends)
            pieces[dd] = jnp.concatenate([jnp.sum(v, axis=0, keepdims=True) for v in total], axis=1)
        m["smsg"][k] = jnp.concatenate(pieces, axis=1)
        land = m["sland"].at[k]
        arrived = net.gather(m["smsg"].at[k], land, ("seq",))
        here_up = within(l, up_dd, ends_up, True, minus)
        here_dn = within(l, dn_dd, ends_dn, False, minus)
        meanwhile()
        arrived()

        def enter(dd, rising):
            whole = tuple(v[0:1] for v in entry(l, dd, 6, minus))
            zero = jnp.zeros((1, Pn), F32)

            def lap(i, state):
                at = i if rising else S - 1 - i
                piece = land[at][:, dd * W : (dd + 1) * W]
                new = advance(whole, state, split(piece))
                reached = (at < me_s) if rising else (at > me_s)
                return tuple(jnp.where(reached, a, b) for a, b in zip(new, state))

            state = (zero, zero)
            if S <= 8:
                for i in range(S):
                    state = lap(i, state)
                return state
            return lax.fori_loop(0, S, lap, state)

        outs = []
        for dd, rising, here_ends, which in ((up_dd, True, here_up, 1), (dn_dd, False, here_dn, 2)):
            far = cmul(entry(l, dd, which, minus), tuple(rep(v) for v in enter(dd, rising)))
            outs.append((here_ends[0] + far[0], here_ends[1] + far[1]))
        return outs

    zeros4 = tuple(jnp.zeros((CHUNKS, Pn), F32) for _ in range(4))
    nothing = lambda: None

    def stat(l, k):
        return m["stat"][4 * l + k : 4 * l + k + 1]

    def set_stat(l, k, value):
        m["stat"][4 * l + k : 4 * l + k + 1] = value

    c0 = 0.7978845608028654
    c1 = 0.044715
    for l in range(LAYERS):
        stats_wait()
        if l == 0:
            sums = jnp.sum(m["land0"][...], axis=0)
            m["stat"][15:16] = 1.0 / widen(sums[0:1, H:])
            sums = sums[:, :H]
        else:
            sums = jnp.sum(m["land"][0], axis=0)
        inv_count = m["stat"][15:16]
        mean = sums[0:1] * inv_count
        var = sums[1:2] * inv_count - mean * mean
        inv = lax.rsqrt(var + EPSILON)
        set_stat(l, 0, mean)
        set_stat(l, 1, inv)
        o_small[6 * l + 4 : 6 * l + 5] = MOMENTUM * rmean[l : l + 1] + (1.0 - MOMENTUM) * mean
        o_small[6 * l + 5 : 6 * l + 6] = MOMENTUM * rvar[l : l + 1] + (1.0 - MOMENTUM) * var
        v_mean, v_scale, v_bias = rep(mean), rep(inv * gain[l : l + 1]), rep(bias[l : l + 1])

        def normalise(i):
            x = rows(m["xs"].at[l], i)
            put_flat(m["nrm"].at[l], i, ((x - v_mean) * v_scale + v_bias) * masked(i))

        sweep(normalise)
        for dd in range(geo.D):

            def keep(at, value):
                m["u"][l, dd, :, pl.ds(at, WIDE)] = value

            product(lambda: m["nrm"][l], lambda at: m["win"][l, dd, :, pl.ds(at, WIDE)], 1, 0, W, keep)
        ends_up, ends_dn = scan(l, 0, m["u"].at[l], False, zeros4, None)
        in_up, in_dn = carries(l, l, 0, ends_up, ends_dn, False, nothing)
        both = lambda v: jnp.concatenate([jnp.concatenate(v, axis=1)] * 2, axis=0).astype(BF16)
        m["st"][l, 0, 0:16] = both(in_up)
        m["st"][l, 1, T + 16 : T + 32] = both(in_dn)

        def save(dd, at, value):
            m["st"][l, dd, pl.ds(16 + at, 16)] = value

        scan(l, 0, m["u"].at[l], False, (*in_up, *in_dn), save)

        def mix(i, _):
            at = pl.ds(pl.multiple_of(i * WIDE, WIDE), WIDE)
            total = dot(m["st"][l, 0, 16 : T + 16], m["wout"][l, 0, :, at], 1, 0)
            total = total + dot(m["st"][l, 1, 16 : T + 16], m["wout"][l, 1, :, at], 1, 0)
            m["tmp"][:, :, at] = total.reshape(J, CHUNKS, WIDE)
            return 0

        lax.fori_loop(0, H // WIDE, mix, 0)
        v_feed = rep(feed[l : l + 1])

        def activate(i):
            v = rows(m["tmp"], i) + v_feed * flat(m["nrm"].at[l], i)
            sq = v * v
            t = jnp.tanh(c0 * v * (1.0 + c1 * sq))
            half = 0.5 * (1.0 + t)
            put_flat(m["act"].at[l], i, v * half)
            slope = half + 0.5 * v * (1.0 - t * t) * (c0 * (1.0 + 3.0 * c1 * sq))
            m["dge"][l, pl.ds(i * GROUP, GROUP)] = slope.astype(BF16)

        sweep(activate)
        product(lambda: m["act"][l], lambda at: m["glw"][l, :, pl.ds(at, WIDE)], 1, 0, H, into(m["tmp"]))
        v_glub = rep(glub[l : l + 1])

        def gate(i):
            sig = 0.5 + 0.5 * jnp.tanh(0.5 * (rows(m["tmp"], i) + v_glub))
            m["sig"][l, pl.ds(i * GROUP, GROUP)] = sig.astype(BF16)
            mk = masked(i)
            x = rows(m["xs"].at[l], i) + mk * flat(m["act"].at[l], i) * sig
            m["xs"][l + 1, pl.ds(i * GROUP, GROUP)] = x
            if l + 1 < LAYERS:
                xm = x * mk
                return xm, xm * x

        sums = sweep(gate, 2 if l + 1 < LAYERS else 0)
        if l + 1 < LAYERS:
            m["msg"][0, 0:1] = sums[0]
            m["msg"][0, 1:2] = sums[1]
            stats_wait = net.gather(m["msg"].at[0], m["land"].at[0], AXES)

    out_waits = []

    def deliver(src, dst):
        send, recv = net.send_sem(), net.recv_sem()
        sem = local_sems.at[local[0]]
        local[0] += 1
        for c in range(CHUNKS):
            to = dst.at[me_d, pl.ds(c * J, J)]
            net.put(src.at[:, c], to, send, recv, {"dir": 1 - me_d})
            pltpu.make_async_copy(src.at[:, c], to, sem).start()
        net.unsent.append((dst.at[me_d], send))
        out_waits.append(functools.partial(net.wait, dst.at[1 - me_d], recv))
        out_waits.append(functools.partial(net.wait, dst.at[me_d], sem))

    deliver(m["xs"].at[LAYERS], o_act)

    reductions = {(k, l): Reduction(geo, net, k, l, m) for k in geo.rows for l in range(LAYERS)}

    def clear_rest(kind, l):
        used, rows_all = geo.used[kind], geo.rows[kind]
        if used < rows_all:
            for dd in range(geo.D):
                m["g" + kind][dd, used:rows_all] = jnp.zeros((rows_all - used, WIDE), BF16)

    def out_grads(l):
        if l + 1 < LAYERS:
            reductions["X", l + 1].settle()
        clear_rest("X", l)
        for dd in range(geo.D):

            def keep(i, _):
                at = pl.ds(pl.multiple_of(i * WIDE, WIDE), WIDE)
                value = dot(m["st"][l, dd, 16 : T + 16], m["dml"][:, at], 0, 0)
                m["gX"][dd, pl.ds(pl.multiple_of(i * W, 16), W)] = value.astype(BF16)
                return 0

            lax.fori_loop(0, H // WIDE, keep, 0)

        def keep_gate(i, _):
            at = pl.ds(pl.multiple_of(i * WIDE, WIDE), WIDE)
            value = dot(m["act"][l], m["dgt"][:, at], 0, 0).astype(BF16)
            half = H // 2
            for dd in range(2):
                m["gX"][dd, pl.ds(pl.multiple_of(geo.out_rows + i * half, 16), half)] = value[dd * half : (dd + 1) * half]
            return 0

        lax.fori_loop(0, H // WIDE, keep_gate, 0)

    def in_grads(l):
        if l + 1 < LAYERS:
            reductions["I", l + 1].settle()
        clear_rest("I", l)
        for dd in range(geo.D):

            def keep(i, _):
                at = pl.multiple_of(i * LANES, LANES)
                kr = m["tab"][l, dd, 14, 0:1, pl.ds(at, LANES)]
                ki = m["tab"][l, dd, 15, 0:1, pl.ds(at, LANES)]
                rhs = jnp.concatenate([m["r"][dd, :, pl.ds(at, LANES)], m["r"][dd, :, pl.ds(at + Pn, LANES)]], axis=1)
                value = dot(m["nrm"][l], rhs, 0, 0)
                re, im = value[:, :LANES], value[:, LANES:]
                value = jnp.concatenate([kr * re + ki * im, kr * im - ki * re], axis=1)
                m["gI"][dd, pl.ds(pl.multiple_of(i * H, 16), H)] = value.astype(BF16)
                return 0

            lax.fori_loop(0, Pn // LANES, keep, 0)

    def tiny_sums(l, d_glub, d_feed):
        m["tiny"][l, :, 0:H] = d_glub
        m["tiny"][l, :, H : 2 * H] = d_feed
        for dd in range(geo.D):

            def some(i, acc):
                at = i * 16
                rr, ri = split(m["r"][dd, pl.ds(at, 16)].astype(F32))
                ur, ui = split(m["u"][l, dd, pl.ds(at, 16)])
                cur = m["st"][l, dd, pl.ds(at + 16, 16)].astype(F32)
                if dd == 0:
                    near = m["st"][l, dd, pl.ds(at, 16)].astype(F32)
                    prev = jnp.concatenate([near[8:], cur[:8]], axis=0)
                else:
                    near = m["st"][l, dd, pl.ds(at + 32, 16)].astype(F32)
                    prev = jnp.concatenate([cur[8:], near[:8]], axis=0)
                hr, hi = split(prev)
                new = (rr * hr + ri * hi, ri * hr - rr * hi, rr * ur + ri * ui, ri * ur - rr * ui)
                return tuple(a + v[:8] + v[8:] for a, v in zip(acc, new))

            acc = lax.fori_loop(0, T // 16, some, zeros4)
            base = 2 * H + dd * 2 * W
            for k, v in enumerate(acc):
                m["tiny"][l, :, base + k * Pn : base + (k + 1) * Pn] = jnp.sum(v, axis=0, keepdims=True)
        return net.gather(m["tiny"].at[l], m["tland1"].at[l], ("dir", "batch"))

    def tiny_middle(l, wait):
        wait()
        m["tmid"][l] = jnp.sum(m["tland1"][l], axis=0)
        return net.gather(m["tmid"].at[l], m["tland2"].at[l], ("seq",))

    def tiny_end(l, wait):
        wait()
        m["tsum"][l] = jnp.sum(m["tland2"][l], axis=0)
        o_small[6 * l + 2 : 6 * l + 3] = m["tsum"][l, :, H : 2 * H]
        o_small[6 * l + 3 : 6 * l + 4] = m["tsum"][l, :, 0:H]
        base = pl.multiple_of(2 * H + me_d * 2 * W, LANES)
        dlr, dli, ar, ai = (m["tsum"][l, :, pl.ds(pl.multiple_of(base + k * Pn, LANES), Pn)] for k in range(4))
        kr, ki = m["tab"][l, me_d, 14][0:1], m["tab"][l, me_d, 15][0:1]
        size = kr * kr + ki * ki
        dkr, dki = (ar * kr - ai * ki) / size, (ar * ki + ai * kr) / size
        _, pull = jax.vjp(transition, *(m["prm"][i, me_d, l] for i in range(3)))
        for k, v in enumerate(pull((dlr, dli, dkr, dki))):
            o_lam[3 * l + k : 3 * l + k + 1] = v

    def gate_share(l):
        src = m["fX"].at[l, pl.ds(geo.out_rows, geo.half_rows)]
        dst = m["glf"].at[l, me_d]
        (wait,) = net.swap([(src, dst, dst)])
        m["glf"][l, me_d] = m["fX"][l, geo.out_rows : geo.out_rows + geo.half_rows]
        return wait

    tiny_wait = {}
    for l in reversed(range(LAYERS)):
        X, I = reductions["X", l], reductions["I", l]

        def open_gate(i):
            dout = rows(m["g"], i) * masked(i)
            sig = rows(m["sig"].at[l], i)
            v = (dout * flat(m["act"].at[l], i) * sig * (1.0 - sig)).astype(BF16)
            put_flat(m["dgt"], i, v)
            return (v.astype(F32),)

        (d_glub,) = sweep(open_gate, 1)
        product(lambda: m["dgt"][...], lambda at: m["glw"][l, pl.ds(at, WIDE)], 1, 1, H, into(m["tmp"]))

        def through(i):
            dout = rows(m["g"], i) * masked(i)
            d = (rows(m["tmp"], i) + dout * rows(m["sig"].at[l], i)) * rows(m["dge"].at[l], i)
            m["dmx"][pl.ds(i * GROUP, GROUP)] = d
            put_flat(m["dml"], i, d)
            return (d * flat(m["nrm"].at[l], i),)

        (d_feed,) = sweep(through, 1)
        for dd in range(geo.D):

            def keep(at, value):
                m["ds"][dd, :, pl.ds(at, WIDE)] = value

            product(lambda: m["dml"][...], lambda at: m["wout"][l, dd, pl.ds(at, WIDE)], 1, 1, W, keep)
        ends_up, ends_dn = scan(l, 1, m["ds"], True, zeros4, None)

        def window():
            out_grads(l)
            X.pair_send()
            if l == 0:
                reductions["I", 1].step2()
                reductions["X", 1].step3()
                tiny_wait[1] = tiny_middle(1, tiny_wait[1])

        in_up, in_dn = carries(LAYERS + l, l, 1, ends_up, ends_dn, True, window)

        def save(dd, at, value):
            m["r"][dd, pl.ds(at, 16)] = value

        scan(l, 1, m["ds"], True, (*in_up, *in_dn), save)

        def back(i, _):
            at = pl.ds(pl.multiple_of(i * WIDE, WIDE), WIDE)
            total = dot(m["r"][0], m["win"][l, 0, at], 1, 1)
            total = total + dot(m["r"][1], m["win"][l, 1, at], 1, 1)
            m["tmp"][:, :, at] = total.reshape(J, CHUNKS, WIDE)
            return 0

        lax.fori_loop(0, H // WIDE, back, 0)
        v_feed, v_mean, v_inv = rep(feed[l : l + 1]), rep(stat(l, 0)), rep(stat(l, 1))

        def normed_grad(i):
            d = (v_feed * rows(m["dmx"], i) + rows(m["tmp"], i)) * masked(i)
            m["tmp"][pl.ds(i * GROUP, GROUP)] = d
            return d, d * ((rows(m["xs"].at[l], i) - v_mean) * v_inv)

        plain, scaled = sweep(normed_grad, 2)
        slot = 1 + l
        m["msg"][slot, 0:1] = plain
        m["msg"][slot, 1:2] = scaled
        arrived = net.gather(m["msg"].at[slot], m["land"].at[slot], AXES)
        X.pair_done()
        X.step1()
        in_grads(l)
        I.pair_send()
        tiny_wait[l] = tiny_sums(l, d_glub, d_feed)
        if l == 0:
            reductions["X", 1].step4()
            reductions["I", 1].step3()
        I.pair_done()
        I.step1()
        if l > 0:
            X.step2()
        arrived()
        sums = jnp.sum(m["land"][slot], axis=0)
        plain, scaled = sums[0:1], sums[1:2]
        o_small[6 * l + 0 : 6 * l + 1] = scaled
        o_small[6 * l + 1 : 6 * l + 2] = plain
        inv = stat(l, 1)
        inv_count = m["stat"][15:16]
        v_scale = rep(inv * gain[l : l + 1])
        v_plain, v_scaled = rep(plain * inv_count), rep(scaled * inv_count * inv)

        def stream_grad(i):
            lead = rows(m["tmp"], i) - masked(i) * (v_plain + (rows(m["xs"].at[l], i) - v_mean) * v_scaled)
            at = pl.ds(i * GROUP, GROUP)
            m["g"][at] = m["g"][at] + v_scale * lead

        sweep(stream_grad)

    deliver(m["g"], o_ig)

    X1, I1, X0, I0 = (reductions[k, l] for l in (1, 0) for k in ("X", "I"))
    X1.done()
    g1 = gate_share(1)
    X0.step2()
    I1.step4()
    tiny_wait[0] = tiny_middle(0, tiny_wait[0])
    tiny_end(1, tiny_wait[1])
    I0.step2()
    X0.step3()
    I1.done()
    I0.step3()
    X0.step4()
    tiny_end(0, tiny_wait[0])
    g1()
    I0.step4()
    X0.done()
    g0 = gate_share(0)
    I0.done()
    g0()
    for k in geo.rows:
        reductions[k, 0].settle()
    for w in out_waits:
        w()
    net.finish()


def on_device(sizes, inputs, cotangent, lengths, gain, bias, in_proj, out_proj, rate, step, freq, feed, gluw, glub, rmean, rvar):
    geo = Geometry(sizes, inputs.shape, rate.shape[-1])
    T, H, W = geo.T, geo.H, geo.W
    v = scratch_shapes(geo)
    held = sum(math.prod(shape) * jnp.dtype(kind).itemsize for shape, kind in v.values())
    hbm = pl.BlockSpec(memory_space=pl.ANY)
    vmem = pl.BlockSpec(memory_space=pltpu.VMEM)
    smem = pl.BlockSpec(memory_space=pltpu.SMEM)
    outs = [
        pltpu.VMEM((geo.seqs, T, H), F32),
        pltpu.VMEM((geo.seqs, T, H), F32),
        pltpu.VMEM((LAYERS, geo.rows["X"], WIDE), BF16),
        pltpu.VMEM((LAYERS, geo.D, geo.half_rows, WIDE), BF16),
        pltpu.VMEM((LAYERS, geo.rows["I"], WIDE), BF16),
        pltpu.VMEM((6 * LAYERS, H), F32),
        pltpu.VMEM((3 * LAYERS, geo.Pn), F32),
    ]
    act, ig, gx, gl, gi, small, lam = pl.pallas_call(
        functools.partial(body, geo, tuple(v)),
        out_shape=outs,
        in_specs=[smem, hbm, hbm, vmem, vmem, hbm, hbm, hbm, hbm, hbm, vmem, hbm, vmem, vmem, vmem],
        out_specs=[vmem] * 7,
        scratch_shapes=[pltpu.VMEM(*s) for s in v.values()]
        + [pltpu.SemaphoreType.DMA((64,)), pltpu.SemaphoreType.DMA((64,)), pltpu.SemaphoreType.DMA((32,))],
        compiler_params=pltpu.CompilerParams(
            collective_id=0, has_side_effects=True, vmem_limit_bytes=held + SPARE_BYTES
        ),
    )(lengths, inputs, cotangent, gain, bias, in_proj, out_proj, rate, step, freq, feed, gluw, glub, rmean, rvar)
    return finish(geo, act, ig, gx, gl, gi, small, lam)


def results(geo, *refs):
    T, H, W, Pn, L = geo.T, geo.H, geo.W, geo.Pn, LAYERS
    act, ig, gx, gl, gi, small, lam = refs[:7]
    (o_act, o_ig, o_gain, o_bias, o_in, o_out, o_rate, o_step, o_freq, o_feed, o_glu, o_glub, o_mean, o_var) = refs[7:21]
    v_in, v_out, v_glu, sems = refs[21:]
    used = [0]

    def copy(src, dst):
        sem = sems.at[used[0]]
        used[0] += 1
        c = pltpu.make_async_copy(src, dst, sem)
        c.start()
        return c

    order = list(reversed(range(L)))
    waits = [copy(act, o_act), copy(ig, o_ig)]
    for l in range(L):
        for k, o in enumerate((o_gain, o_bias, o_feed, o_glub, o_mean, o_var)):
            o[l : l + 1] = small[6 * l + k : 6 * l + k + 1]
        for k, o in enumerate((o_rate, o_step, o_freq)):
            o[l] = lam[3 * l + k : 3 * l + k + 1]
    block = 64
    half = H // 2
    for l in order:
        for n in range(H // WIDE):

            def move(i, _):
                v_out[l, pl.ds(i * block, block), n * WIDE : (n + 1) * WIDE] = gx[
                    l, pl.ds(n * W + i * block, block)
                ].astype(F32)
                return 0

            lax.fori_loop(0, W // block, move, 0)
        waits.append(copy(v_out.at[l], o_out.at[l, 0]))
        for n in range(Pn // LANES):

            def move(i, _):
                value = gi[l, pl.ds(n * H + i * block, block)].astype(F32)
                at = pl.ds(i * block, block)
                v_in[l, at, n * LANES : (n + 1) * LANES] = value[:, :LANES]
                v_in[l, at, Pn + n * LANES : Pn + (n + 1) * LANES] = value[:, LANES:]
                return 0

            lax.fori_loop(0, H // block, move, 0)
        waits.append(copy(v_in.at[l], o_in.at[l, 0]))
        for d in range(geo.D):
            for n in range(H // WIDE):

                def move(i, _):
                    value = gl[l, d, pl.ds(n * half + i * block, block)].astype(F32)
                    v_glu[l, pl.ds(d * half + i * block, block), n * WIDE : (n + 1) * WIDE] = value
                    return 0

                lax.fori_loop(0, half // block, move, 0)
        waits.append(copy(v_glu.at[l], o_glu.at[l]))
    for c in waits:
        c.wait()


def finish(geo, act, ig, gx, gl, gi, small, lam):
    T, H, W, Pn, L = geo.T, geo.H, geo.W, geo.Pn, LAYERS
    hbm = pl.BlockSpec(memory_space=pl.ANY)
    vmem = pl.BlockSpec(memory_space=pltpu.VMEM)
    row = jax.ShapeDtypeStruct((L, H), F32)
    lam_row = jax.ShapeDtypeStruct((L, 1, Pn), F32)
    stream = jax.ShapeDtypeStruct((geo.seqs, T, H), F32)
    outs = [
        stream,
        stream,
        row,
        row,
        jax.ShapeDtypeStruct((L, 1, H, W), F32),
        jax.ShapeDtypeStruct((L, 1, W, H), F32),
        lam_row,
        lam_row,
        lam_row,
        row,
        jax.ShapeDtypeStruct((L, H, H), F32),
        row,
        row,
        row,
    ]
    where = [hbm, hbm, vmem, vmem, hbm, hbm, vmem, vmem, vmem, vmem, hbm, vmem, vmem, vmem]
    return pl.pallas_call(
        functools.partial(results, geo),
        out_shape=outs,
        in_specs=[vmem] * 7,
        out_specs=where,
        scratch_shapes=[
            pltpu.VMEM((L, H, W), F32),
            pltpu.VMEM((L, W, H), F32),
            pltpu.VMEM((L, H, H), F32),
            pltpu.SemaphoreType.DMA((16,)),
        ],
        compiler_params=pltpu.CompilerParams(vmem_limit_bytes=16 << 20),
    )(act, ig, gx, gl, gi, small, lam)


def solution(mesh):
    tokens = P("batch", "seq", None)
    per_dir = P(None, "dir", None)
    mats = P(None, "dir", None, None)
    in_specs = (tokens, tokens, P("batch"), P(), P(), mats, mats, per_dir, per_dir, per_dir) + (P(),) * 5
    out_specs = (tokens, tokens, P(), P(), mats, mats, per_dir, per_dir, per_dir) + (P(),) * 5
    return jax.shard_map(
        functools.partial(on_device, dict(mesh.shape)),
        mesh=mesh,
        in_specs=in_specs,
        out_specs=out_specs,
        check_vma=False,
    )
```

```python
import functools
import math

import jax
import jax.numpy as jnp
from jax import lax
from jax.experimental import pallas as pl
from jax.experimental.pallas import tpu as pltpu
from jax.sharding import PartitionSpec as P

LAYERS = 2
EPSILON = 1e-05
MOMENTUM = 0.9
F32 = jnp.float32
BF16 = jnp.bfloat16
AXES = ("dir", "seq", "batch")
MESH = pl.DeviceIdType.MESH
LANES = 128
CHUNKS = 8
WIDE = 256
SPARE_BYTES = 5 << 19
SEMAPHORES = 96


def transition(rate_vec, step_vec, freq_vec):
    half_a = 0.5 * step_vec * rate_vec
    half_c = 0.5 * step_vec * freq_vec
    denominator = (1.0 + half_a) * (1.0 + half_a) + half_c * half_c
    lam_re = (1.0 - half_a * half_a - half_c * half_c) / denominator
    lam_im = 2.0 * half_c / denominator
    kap_re = step_vec * (1.0 + half_a) / denominator
    kap_im = step_vec * half_c / denominator
    return (lam_re, lam_im, kap_re, kap_im)


def dot(a, b, ca, cb):
    return lax.dot_general(a, b, (((ca,), (cb,)), ((), ())), preferred_element_type=F32)


def cmul(a, b):
    return (a[0] * b[0] - a[1] * b[1], a[0] * b[1] + a[1] * b[0])


def conj(a):
    return (a[0], -a[1])


def widen(mask):
    return jnp.concatenate([mask] * 4, axis=-1)


class Geometry:
    def __init__(self, sizes, local_shape, states):
        self.D, self.S, self.B = (sizes[a] for a in AXES)
        self.sizes = dict(sizes)
        self.seqs, self.T, self.H = local_shape
        self.Pn = states
        self.W = 2 * states
        self.J = self.T // CHUNKS
        self.N = self.D * self.S * self.B
        self.unit = 16 * self.S * self.B
        up = lambda n: -(-n // self.unit) * self.unit
        self.out_rows = (self.H // WIDE) * self.W
        self.half_rows = (self.H // WIDE) * (self.H // 2)
        self.in_rows = (self.Pn // LANES) * self.H
        self.used = {"X": self.out_rows + self.half_rows, "I": self.in_rows}
        self.rows = {k: up(v) for k, v in self.used.items()}
        bits = tuple(("batch", k) for k in range((self.B - 1).bit_length()))
        seq = (("seq", None),)
        orders = (bits + seq, bits[::-1] + seq)
        self.colors = {}
        for k, n in self.rows.items():
            units = n // self.unit
            at, self.colors[k] = 0, []
            for count, order in zip((-(-units // 2), units // 2), orders):
                if count:
                    self.colors[k].append((at, count * self.unit, order))
                    at += count * self.unit
        self.direct = self.N <= 64

    def ways(self, dim):
        return self.S if dim[1] is None else 2


class Net:
    def __init__(self, geo, send_sems, recv_sems):
        self.geo, self.send_sems, self.recv_sems = geo, send_sems, recv_sems
        self.used_send = 0
        self.used_recv = 0
        self.at = {a: lax.axis_index(a) for a in AXES}
        self.unsent = []

    def send_sem(self):
        self.used_send += 1
        return self.send_sems.at[self.used_send - 1]

    def recv_sem(self):
        self.used_recv += 1
        return self.recv_sems.at[self.used_recv - 1]

    def index(self, axes):
        lin = 0
        for a in axes:
            lin = lin * self.geo.sizes[a] + self.at[a]
        return lin

    def count(self, axes):
        n = 1
        for a in axes:
            n *= self.geo.sizes[a]
        return n

    def peers(self, axes, act):
        n = self.count(axes)

        def at_offset(k):
            where, lin, rest, coords = {}, 0, k, []
            for a in reversed(axes):
                size = self.geo.sizes[a]
                off = rest % size
                rest = rest // size
                coords.append((a, lax.rem(self.at[a] + off, size)))
            for a, c in reversed(coords):
                where[a] = c
                lin = lin * self.geo.sizes[a] + c
            act(where, lin, k)

        if n <= 64:
            for k in range(n - 1, 0, -1):
                at_offset(k)
        else:

            def body(k, _):
                at_offset(k)
                return 0

            lax.fori_loop(1, n, body, 0)

    def place(self, dim):
        axis, bit = dim
        return self.at[axis] if bit is None else lax.rem(lax.div(self.at[axis], 1 << bit), 2)

    def others(self, dim, act):
        axis, bit = dim
        if bit is None:
            self.peers((axis,), act)
        else:
            mine = self.place(dim)
            act({axis: self.at[axis] + (1 - 2 * mine) * (1 << bit)}, 1 - mine, 1)

    def put(self, src, dst, send, recv, peer):
        pltpu.make_async_remote_copy(
            src_ref=src, dst_ref=dst, send_sem=send, recv_sem=recv, device_id=peer, device_id_type=MESH
        ).start()

    def wait(self, ref, sem):
        pltpu.make_async_copy(ref, ref, sem).wait()

    def gather(self, src, land, axes):
        n = self.count(axes)
        send, recv = self.send_sem(), self.recv_sem()
        slot = self.index(axes)
        self.peers(axes, lambda peer, lin, k: self.put(src, land.at[slot], send, recv, peer))
        land[slot] = src[...]
        size = land.at[pl.ds(0, n - 1)]
        self.unsent.append((size, send))
        return functools.partial(self.wait, size, recv)

    def swap(self, pieces):
        peer = {"dir": 1 - self.at["dir"]}
        waits = []
        for src, dst, size in pieces:
            send, recv = self.send_sem(), self.recv_sem()
            self.put(src, dst, send, recv, peer)
            self.unsent.append((size, send))
            waits.append(functools.partial(self.wait, size, recv))
        return waits

    def finish(self):
        for size, send in self.unsent:
            self.wait(size, send)


def scratch_shapes(geo):
    T, H, W, J, S, N, Pn = geo.T, geo.H, geo.W, geo.J, geo.S, geo.N, geo.Pn
    L, D = LAYERS, geo.D
    v = {
        "mask": ((J, CHUNKS, LANES), F32),
        "win": ((L, H, D * W), BF16),
        "wout": ((L, D * W, H), BF16),
        "glw": ((L, H, H), BF16),
        "prm": ((3, D, L, 1, Pn), F32),
        "tab": ((L, D, 16, CHUNKS, Pn), F32),
        "xs": ((L + 1, J, CHUNKS, H), F32),
        "stat": ((16, H), F32),
        "nrm": ((L, T, H), BF16),
        "u": ((L, T, D * W), F32),
        "st": ((L, T + 32, D * W), BF16),
        "act": ((L, T, H), BF16),
        "sig": ((L, J, CHUNKS, H), BF16),
        "dge": ((L, J, CHUNKS, H), BF16),
        "tmp": ((J, CHUNKS, H), F32),
        "g": ((J, CHUNKS, H), F32),
        "dmx": ((J, CHUNKS, H), F32),
        "dml": ((T, H), BF16),
        "dgt": ((T, H), BF16),
        "ds": ((T, D * W), F32),
        "r": ((T, D * W), BF16),
        "msg0": ((2, H + LANES), F32),
        "msg": ((3, 2, H), F32),
        "smsg": ((2 * L, 1, D * W), F32),
        "sland": ((2 * L, S, 1, D * W), F32),
        "tiny": ((L, 1, 2 * H + 4 * W), F32),
        "tland1": ((L, D * geo.B, 1, 2 * H + 4 * W), F32),
        "tmid": ((L, 1, 2 * H + 4 * W), F32),
        "tland2": ((L, S, 1, 2 * H + 4 * W), F32),
        "tsum": ((L, 1, 2 * H + 4 * W), F32),
    }
    for k, lead, wide in (("0", (), H + LANES), ("", (3,), H)):
        if geo.direct:
            v["land" + k] = ((*lead, N, 2, wide), F32)
        else:
            v["near" + k] = ((*lead, D * geo.B, 2, wide), F32)
            v["mid" + k] = ((*lead, 2, wide), F32)
            v["far" + k] = ((*lead, S, 2, wide), F32)
    for k, rows in geo.rows.items():
        v["g" + k] = ((D, rows, WIDE), BF16)
        v["p" + k] = ((L, rows, WIDE), BF16)
        for c, (_, n, order) in enumerate(geo.colors[k]):
            for i, dim in enumerate(order):
                ways = geo.ways(dim)
                n //= ways
                v[f"land{i}{k}{c}"] = ((L, ways - 1, n, WIDE), BF16)
                if i == 0:
                    v[f"red{k}{c}"] = ((L, n, WIDE), BF16)
    return v


class Reduction:
    def __init__(self, geo, net, kind, layer, m):
        self.geo, self.net, self.kind, self.layer, self.m = geo, net, kind, layer, m
        self.rows = geo.rows[kind]
        self.colors = geo.colors[kind]
        self.full = m["f" + kind].at[layer]
        self.mine = m["g" + kind].at[net.at["dir"]]
        self.flows = None

    def pair_send(self):
        landing = self.m["p" + self.kind].at[self.layer]
        other = self.m["g" + self.kind].at[1 - self.net.at["dir"]]
        (self.pair_wait,) = self.net.swap([(other, landing, landing)])
        self.held = [self.net.unsent.pop()]

    def settle(self):
        for size, send in self.held:
            self.net.wait(size, send)

    def pair_done(self):
        self.pair_wait()
        landing = self.m["p" + self.kind].at[self.layer]
        block = 64

        def body(i, _):
            at = pl.ds(i * block, block)
            self.mine[at] = (self.mine[at].astype(F32) + landing[at].astype(F32)).astype(BF16)
            return 0

        lax.fori_loop(0, self.rows // block, body, 0)

    def scatter(self, dim, src, base, part, land):
        net = self.net
        send, recv = net.send_sem(), net.recv_sem()
        net.others(
            dim,
            lambda peer, lin, k: net.put(
                src.at[pl.ds(base + lin * part, part)], land.at[k - 1], send, recv, peer
            ),
        )
        net.unsent.append((land, send))
        return functools.partial(net.wait, land, recv)

    def add(self, own, own_at, land, n, out, out_at, part):
        block = next(b for b in (64, 48, 32, 16) if part % b == 0)

        def body(i, _):
            total = own[pl.ds(own_at + i * block, block)].astype(F32)
            for k in range(min(n - 1, 7)):
                total = total + land[k, pl.ds(i * block, block)].astype(F32)
            if n - 1 > 7:
                total = lax.fori_loop(
                    7, n - 1, lambda k, t: t + land[k, pl.ds(i * block, block)].astype(F32), total
                )
            out[pl.ds(out_at + i * block, block)] = total.astype(BF16)
            return 0

        lax.fori_loop(0, part // block, body, 0)

    def spread(self, dim, base, part):
        net, n = self.net, self.geo.ways(dim)
        send, recv = net.send_sem(), net.recv_sem()
        mine = self.full.at[pl.ds(base, part)]
        net.others(dim, lambda peer, lin, k: net.put(mine, mine, send, recv, peer))
        size = self.full.at[pl.ds(0, (n - 1) * part)]
        net.unsent.append((size, send))
        return functools.partial(net.wait, size, recv)

    def flow(self, c):
        base, size, order = self.colors[c]
        red = self.m[f"red{self.kind}{c}"].at[self.layer]
        src, src_at, at = self.mine, base, base
        owned = []
        for i, dim in enumerate(order):
            n = self.geo.ways(dim)
            part = size // n
            land = self.m[f"land{i}{self.kind}{c}"].at[self.layer]
            wait = self.scatter(dim, src, src_at, part, land)
            if i == 0:
                self.held.append(self.net.unsent.pop())
            yield
            wait()
            mine = self.net.place(dim)
            own_at, at = src_at + mine * part, at + mine * part
            if i + 1 == len(order):
                out, out_at = self.full, at
            else:
                out, out_at = red, 0 if i == 0 else own_at
            self.add(src, own_at, land, n, out, out_at, part)
            src, src_at, size = red, out_at, part
            owned.append((dim, at, part))
        for dim, at, part in reversed(owned):
            wait = self.spread(dim, at, part)
            yield
            wait()

    def step(self):
        if self.flows is None:
            self.pair_done()
            self.flows = [self.flow(c) for c in range(len(self.colors))]
        for flow in self.flows:
            next(flow, None)

    def done(self):
        for flow in self.flows:
            for _ in flow:
                pass


def body(geo, names, *refs):
    T, H, W, J, S, N, Pn = geo.T, geo.H, geo.W, geo.J, geo.S, geo.N, geo.Pn
    (lengths, inputs, cotangent, gain, bias, in_proj, out_proj, rate, step, freq, feed, gluw, glub, rmean, rvar) = refs[:15]
    (o_act, o_ig, o_gx, o_gl, o_gi, o_small, o_lam) = refs[15:22]
    scr = refs[22:]
    m = dict(zip(names, scr))
    m["fX"], m["fI"], m["glf"] = o_gx, o_gi, o_gl
    m["xin"], m["cin"], m["pm"] = m["dgt"], m["dml"], m["r"].at[:, 0:T]
    send_sems, recv_sems, local_sems = scr[len(names) :]
    net = Net(geo, send_sems, recv_sems)
    me_d, me_s = net.at["dir"], net.at["seq"]
    local = [0]

    def fetch(src, dst):
        sem = local_sems.at[local[0]]
        local[0] += 1
        copy = pltpu.make_async_copy(src, dst, sem)
        copy.start()
        return copy.wait

    def sum_over_all(msg, which, slot=None):
        at = lambda name: m[name + which] if slot is None else m[name + which].at[slot]
        if geo.direct:
            arrived = net.gather(msg, at("land"), AXES)

            def total():
                arrived()
                return jnp.sum(at("land")[...], axis=0)

            return total
        arrived = net.gather(msg, at("near"), ("dir", "batch"))

        def total():
            arrived()
            at("mid")[...] = jnp.sum(at("near")[...], axis=0)
            net.gather(at("mid"), at("far"), ("seq",))()
            return jnp.sum(at("far")[...], axis=0)

        return total

    barrier = pltpu.get_barrier_semaphore()
    net.peers(AXES, lambda peer, lin, k: pl.semaphore_signal(barrier, 1, device_id=peer, device_id_type=MESH))
    w_x = fetch(inputs.at[me_d], m["xin"])
    w_c = fetch(cotangent.at[me_d], m["cin"])
    raw = (rate, step, freq)
    w_p = [fetch(raw[i], m["prm"].at[i, me_d]) for i in range(3)]
    cols = pl.ds(pl.multiple_of(me_d * W, LANES), W)
    rows_of = pl.ds(pl.multiple_of(me_d * W, 16), W)
    in_at = [m["win"].at[l, :, cols] for l in range(LAYERS)]
    out_at = [m["wout"].at[l, rows_of] for l in range(LAYERS)]
    w_in = [fetch(in_proj.at[l, 0], in_at[l]) for l in range(LAYERS)]
    w_out = [fetch(out_proj.at[l, 0], out_at[l]) for l in range(LAYERS)]
    w_g = fetch(gluw, m["glw"])

    length = lengths[me_d]
    shape = (J, CHUNKS, LANES)
    position = (
        me_s * T
        + lax.broadcasted_iota(jnp.int32, shape, 1) * J
        + lax.broadcasted_iota(jnp.int32, shape, 0)
    )
    m["mask"][...] = jnp.where(position < length, 1.0, 0.0).astype(F32)

    def permutation(i, _):
        at = pl.ds(i * 64, 64)
        row = i * 64 + lax.broadcasted_iota(jnp.int32, (64, T), 0)
        col = lax.broadcasted_iota(jnp.int32, (64, T), 1)
        wanted = lax.rem(row, CHUNKS) * J + lax.div(row, CHUNKS)
        m["pm"][at] = jnp.where(col == wanted, 1.0, 0.0).astype(BF16)
        return 0

    lax.fori_loop(0, T // 64, permutation, 0)

    def put3(ref3, value):
        ref3[...] = value.reshape(J, CHUNKS, H)

    def reorder(src, dst):
        put3(dst, dot(m["pm"][...], src[...], 1, 0))

    GROUP = 4
    ROWS = GROUP * CHUNKS

    def rows(ref, i):
        return ref[pl.ds(i * GROUP, GROUP)].astype(F32)

    def flat(ref, i):
        return ref[pl.ds(i * ROWS, ROWS)].astype(F32).reshape(GROUP, CHUNKS, -1)

    def put_flat(ref, i, value):
        ref[pl.ds(i * ROWS, ROWS)] = value.reshape(ROWS, -1).astype(BF16)

    def sweep(act, sums=0):
        zero = tuple(jnp.zeros((CHUNKS, H), F32) for _ in range(sums))

        def one(i, acc):
            more = act(i)
            if not sums:
                return acc
            return tuple(a + jnp.sum(v, axis=0) for a, v in zip(acc, more))

        acc = lax.fori_loop(0, T // ROWS, one, zero)
        return tuple(jnp.sum(a, axis=0, keepdims=True) for a in acc)

    def rep(row):
        return jnp.broadcast_to(row, (CHUNKS, row.shape[-1]))

    masked = lambda i: widen(rows(m["mask"], i))

    w_x()
    reorder(m["xin"], m["xs"].at[0])

    def first(i):
        x = rows(m["xs"].at[0], i)
        xm = x * masked(i)
        return xm, xm * x

    s1, s2 = sweep(first, 2)
    here = jnp.sum(jnp.sum(m["mask"][...], axis=0), axis=0, keepdims=True)
    m["msg0"][0:1, 0:H] = s1
    m["msg0"][1:2, 0:H] = s2
    m["msg0"][:, H:] = jnp.broadcast_to(here, (2, LANES))

    pl.semaphore_wait(barrier, N - 1)
    stats = sum_over_all(m["msg0"], "0")
    send_in, send_out = [None] * LAYERS, [None] * LAYERS
    prm_waits = net.swap([(raw[i], m["prm"].at[i, me_d], m["prm"].at[i, me_d]) for i in range(3)])
    for l in range(LAYERS):
        (send_in[l],) = net.swap([(in_proj.at[l, 0], in_at[l], in_at[l])])
        (send_out[l],) = net.swap([(out_proj.at[l, 0], out_at[l], out_at[l])])

    for w in w_p + prm_waits:
        w()
    for l in range(LAYERS):
        for dd in range(geo.D):
            lr, li, kr, ki = transition(*(m["prm"][i, dd, l] for i in range(3)))
            power = (lr, li)
            for _ in range((J).bit_length() - 1):
                power = cmul(power, power)
            ladder = [power]
            for _ in range(3):
                ladder.append(cmul(ladder[-1], ladder[-1]))
            wide = [tuple(rep(v) for v in p) for p in ladder]
            chunk = lax.broadcasted_iota(jnp.int32, (CHUNKS, Pn), 0)
            one = (jnp.ones((CHUNKS, Pn), F32), jnp.zeros((CHUNKS, Pn), F32))
            up, down = one, one
            for k in range(3):
                bit = lax.rem(lax.div(chunk, 1 << k), 2)
                grown = cmul(up, wide[k])
                up = tuple(jnp.where(bit == 1, a, b) for a, b in zip(grown, up))
                grown = cmul(down, wide[k])
                down = tuple(jnp.where(bit == 0, a, b) for a, b in zip(grown, down))
            table = [rep(lr), rep(li), *up, *down]
            for p in wide:
                table.extend(p)
            table.extend([rep(kr), rep(ki)])
            for k, v in enumerate(table):
                m["tab"][l, dd, k] = v

    def entry(l, dd, k, minus):
        re, im = m["tab"][l, dd, 2 * k], m["tab"][l, dd, 2 * k + 1]
        return (re, -im) if minus else (re, im)

    def fold(l):
        for dd in range(geo.D):
            kr, ki = m["tab"][l, dd, 14][0:1], m["tab"][l, dd, 15][0:1]

            def some(i, _):
                at = pl.ds(i * 32, 32)
                w = m["win"][l, at, dd * W : (dd + 1) * W].astype(F32)
                re, im = w[:, :Pn], w[:, Pn:]
                new = jnp.concatenate([kr * re - ki * im, kr * im + ki * re], axis=1)
                m["win"][l, at, dd * W : (dd + 1) * W] = new.astype(BF16)
                return 0

            lax.fori_loop(0, H // 32, some, 0)

    for l in range(LAYERS):
        w_in[l]()
        send_in[l]()
        fold(l)
        w_out[l]()
        send_out[l]()
    w_c()
    reorder(m["cin"], m["g"])
    w_g()

    def split(block):
        return block[:, :Pn], block[:, Pn:]

    def advance(lam, h, d):
        return (lam[0] * h[0] - lam[1] * h[1] + d[0], lam[0] * h[1] + lam[1] * h[0] + d[1])

    def scan(l, up_dd, src, minus, start, emit):
        dn_dd = 1 - up_dd
        lam_up, lam_dn = entry(l, up_dd, 0, minus), entry(l, dn_dd, 0, minus)
        n = T // 16

        def two(i, carry):
            hu, hd = carry[:2], carry[2:]
            at_u, at_d = i * 16, (n - 1 - i) * 16
            bu = src[pl.ds(at_u, 16), up_dd * W : (up_dd + 1) * W]
            bd = src[pl.ds(at_d, 16), dn_dd * W : (dn_dd + 1) * W]
            keep_u, keep_d = [], []
            for k in range(2):
                hu = advance(lam_up, hu, split(bu[8 * k : 8 * k + 8]))
                hd = advance(lam_dn, hd, split(bd[8 - 8 * k : 16 - 8 * k]))
                keep_u.append(jnp.concatenate(hu, axis=1))
                keep_d.append(jnp.concatenate(hd, axis=1))
            if emit is not None:
                emit(up_dd, at_u, jnp.concatenate(keep_u, axis=0).astype(BF16))
                emit(dn_dd, at_d, jnp.concatenate(keep_d[::-1], axis=0).astype(BF16))
            return (*hu, *hd)

        out = lax.fori_loop(0, n, two, start, unroll=2)
        return out[:2], out[2:]

    chunk_at = lax.broadcasted_iota(jnp.int32, (CHUNKS, Pn), 0)

    def within(l, dd, ends, rising, minus):
        shift = (lambda v, k: pltpu.roll(v, k, 0)) if rising else (lambda v, k: pltpu.roll(v, CHUNKS - k, 0))
        inside = (lambda k: chunk_at >= k) if rising else (lambda k: chunk_at < CHUNKS - k)
        a = tuple(jnp.where(inside(1), shift(v, 1), 0.0) for v in ends)
        for k in range(3):
            far = tuple(jnp.where(inside(1 << k), shift(v, 1 << k), 0.0) for v in a)
            more = cmul(entry(l, dd, 3 + k, minus), far)
            a = (a[0] + more[0], a[1] + more[1])
        return a

    def carries(k, l, up_dd, ends_up, ends_dn, minus, meanwhile):
        dn_dd = 1 - up_dd
        pieces = [None] * geo.D
        for dd, ends, which in ((up_dd, ends_up, 2), (dn_dd, ends_dn, 1)):
            total = cmul(entry(l, dd, which, minus), ends)
            pieces[dd] = jnp.concatenate([jnp.sum(v, axis=0, keepdims=True) for v in total], axis=1)
        m["smsg"][k] = jnp.concatenate(pieces, axis=1)
        land = m["sland"].at[k]
        arrived = net.gather(m["smsg"].at[k], land, ("seq",))
        here_up = within(l, up_dd, ends_up, True, minus)
        here_dn = within(l, dn_dd, ends_dn, False, minus)
        meanwhile()
        arrived()

        def enter(dd, rising):
            whole = tuple(v[0:1] for v in entry(l, dd, 6, minus))
            zero = jnp.zeros((1, Pn), F32)

            def lap(i, state):
                at = i if rising else S - 1 - i
                piece = land[at][:, dd * W : (dd + 1) * W]
                new = advance(whole, state, split(piece))
                reached = (at < me_s) if rising else (at > me_s)
                return tuple(jnp.where(reached, a, b) for a, b in zip(new, state))

            state = (zero, zero)
            if S <= 8:
                for i in range(S):
                    state = lap(i, state)
                return state
            return lax.fori_loop(0, S, lap, state)

        outs = []
        for dd, rising, here_ends, which in ((up_dd, True, here_up, 1), (dn_dd, False, here_dn, 2)):
            far = cmul(entry(l, dd, which, minus), tuple(rep(v) for v in enter(dd, rising)))
            outs.append((here_ends[0] + far[0], here_ends[1] + far[1]))
        return outs

    zeros4 = tuple(jnp.zeros((CHUNKS, Pn), F32) for _ in range(4))
    nothing = lambda: None

    def stat(l, k):
        return m["stat"][4 * l + k : 4 * l + k + 1]

    def set_stat(l, k, value):
        m["stat"][4 * l + k : 4 * l + k + 1] = value

    c0 = 0.7978845608028654
    c1 = 0.044715
    for l in range(LAYERS):
        sums = stats()
        if l == 0:
            m["stat"][15:16] = 1.0 / widen(sums[0:1, H:])
            sums = sums[:, :H]
        inv_count = m["stat"][15:16]
        mean = sums[0:1] * inv_count
        var = sums[1:2] * inv_count - mean * mean
        inv = lax.rsqrt(var + EPSILON)
        set_stat(l, 0, mean)
        set_stat(l, 1, inv)
        o_small[6 * l + 4 : 6 * l + 5] = MOMENTUM * rmean[l : l + 1] + (1.0 - MOMENTUM) * mean
        o_small[6 * l + 5 : 6 * l + 6] = MOMENTUM * rvar[l : l + 1] + (1.0 - MOMENTUM) * var
        v_mean, v_scale, v_bias = rep(mean), rep(inv * gain[l : l + 1]), rep(bias[l : l + 1])

        def normalise(i):
            x = rows(m["xs"].at[l], i)
            put_flat(m["nrm"].at[l], i, ((x - v_mean) * v_scale + v_bias) * masked(i))

        sweep(normalise)
        m["u"][l] = dot(m["nrm"][l], m["win"][l], 1, 0)
        ends_up, ends_dn = scan(l, 0, m["u"].at[l], False, zeros4, None)
        in_up, in_dn = carries(l, l, 0, ends_up, ends_dn, False, nothing)
        both = lambda v: jnp.concatenate([jnp.concatenate(v, axis=1)] * 2, axis=0).astype(BF16)
        m["st"][l, 0:16, 0:W] = both(in_up)
        m["st"][l, T + 16 : T + 32, W:] = both(in_dn)

        def save(dd, at, value):
            m["st"][l, pl.ds(16 + at, 16), dd * W : (dd + 1) * W] = value

        scan(l, 0, m["u"].at[l], False, (*in_up, *in_dn), save)

        put3(m["tmp"], dot(m["st"][l, 16 : T + 16], m["wout"][l], 1, 0))
        v_feed = rep(feed[l : l + 1])

        def activate(i):
            v = rows(m["tmp"], i) + v_feed * flat(m["nrm"].at[l], i)
            sq = v * v
            t = jnp.tanh(c0 * v * (1.0 + c1 * sq))
            half = 0.5 * (1.0 + t)
            put_flat(m["act"].at[l], i, v * half)
            slope = half + 0.5 * v * (1.0 - t * t) * (c0 * (1.0 + 3.0 * c1 * sq))
            m["dge"][l, pl.ds(i * GROUP, GROUP)] = slope.astype(BF16)

        sweep(activate)
        put3(m["tmp"], dot(m["act"][l], m["glw"][l], 1, 0))
        v_glub = rep(glub[l : l + 1])

        def gate(i):
            sig = 0.5 + 0.5 * jnp.tanh(0.5 * (rows(m["tmp"], i) + v_glub))
            m["sig"][l, pl.ds(i * GROUP, GROUP)] = sig.astype(BF16)
            mk = masked(i)
            x = rows(m["xs"].at[l], i) + mk * flat(m["act"].at[l], i) * sig
            m["xs"][l + 1, pl.ds(i * GROUP, GROUP)] = x
            if l + 1 < LAYERS:
                xm = x * mk
                return xm, xm * x

        sums = sweep(gate, 2 if l + 1 < LAYERS else 0)
        if l + 1 < LAYERS:
            m["msg"][0, 0:1] = sums[0]
            m["msg"][0, 1:2] = sums[1]
            stats = sum_over_all(m["msg"].at[0], "", 0)

    out_waits = []

    def deliver(src, dst):
        send, recv = net.send_sem(), net.recv_sem()
        sem = local_sems.at[local[0]]
        local[0] += 1
        for c in range(CHUNKS):
            to = dst.at[me_d, pl.ds(c * J, J)]
            net.put(src.at[:, c], to, send, recv, {"dir": 1 - me_d})
            pltpu.make_async_copy(src.at[:, c], to, sem).start()
        net.unsent.append((dst.at[me_d], send))
        out_waits.append(functools.partial(net.wait, dst.at[1 - me_d], recv))
        out_waits.append(functools.partial(net.wait, dst.at[me_d], sem))

    deliver(m["xs"].at[LAYERS], o_act)

    reductions = {(k, l): Reduction(geo, net, k, l, m) for k in geo.rows for l in range(LAYERS)}

    def clear_rest(kind, l):
        used, rows_all = geo.used[kind], geo.rows[kind]
        if used < rows_all:
            for dd in range(geo.D):
                m["g" + kind][dd, used:rows_all] = jnp.zeros((rows_all - used, WIDE), BF16)

    def out_grads(l):
        if l + 1 < LAYERS:
            reductions["X", l + 1].settle()
        clear_rest("X", l)
        value = dot(m["st"][l, 16 : T + 16], m["dml"][...], 0, 0).astype(BF16)
        gates = dot(m["act"][l], m["dgt"][...], 0, 0).astype(BF16)
        half = H // 2
        for dd in range(geo.D):
            for i in range(H // WIDE):
                across = slice(i * WIDE, (i + 1) * WIDE)
                m["gX"][dd, i * W : (i + 1) * W] = value[dd * W : (dd + 1) * W, across]
                at = geo.out_rows + i * half
                m["gX"][dd, at : at + half] = gates[dd * half : (dd + 1) * half, across]

    def in_grads(l):
        if l + 1 < LAYERS:
            reductions["I", l + 1].settle()
        clear_rest("I", l)
        value = dot(m["nrm"][l], m["r"][...], 0, 0)
        for dd in range(geo.D):
            for i in range(Pn // LANES):
                across = slice(i * LANES, (i + 1) * LANES)
                kr, ki = m["tab"][l, dd, 14, 0:1, across], m["tab"][l, dd, 15, 0:1, across]
                at = dd * W + i * LANES
                re, im = value[:, at : at + LANES], value[:, at + Pn : at + Pn + LANES]
                new = jnp.concatenate([kr * re + ki * im, kr * im - ki * re], axis=1)
                m["gI"][dd, i * H : (i + 1) * H] = new.astype(BF16)

    def tiny_sums(l, d_glub, d_feed):
        m["tiny"][l, :, 0:H] = d_glub
        m["tiny"][l, :, H : 2 * H] = d_feed
        for dd in range(geo.D):

            def some(i, acc):
                at = i * 16
                across = slice(dd * W, (dd + 1) * W)
                rr, ri = split(m["r"][pl.ds(at, 16), across].astype(F32))
                ur, ui = split(m["u"][l, pl.ds(at, 16), across])
                cur = m["st"][l, pl.ds(at + 16, 16), across].astype(F32)
                if dd == 0:
                    near = m["st"][l, pl.ds(at, 16), across].astype(F32)
                    prev = jnp.concatenate([near[8:], cur[:8]], axis=0)
                else:
                    near = m["st"][l, pl.ds(at + 32, 16), across].astype(F32)
                    prev = jnp.concatenate([cur[8:], near[:8]], axis=0)
                hr, hi = split(prev)
                new = (rr * hr + ri * hi, ri * hr - rr * hi, rr * ur + ri * ui, ri * ur - rr * ui)
                return tuple(a + v[:8] + v[8:] for a, v in zip(acc, new))

            acc = lax.fori_loop(0, T // 16, some, zeros4)
            base = 2 * H + dd * 2 * W
            for k, v in enumerate(acc):
                m["tiny"][l, :, base + k * Pn : base + (k + 1) * Pn] = jnp.sum(v, axis=0, keepdims=True)
        return net.gather(m["tiny"].at[l], m["tland1"].at[l], ("dir", "batch"))

    def tiny_middle(l, wait):
        wait()
        m["tmid"][l] = jnp.sum(m["tland1"][l], axis=0)
        return net.gather(m["tmid"].at[l], m["tland2"].at[l], ("seq",))

    def tiny_end(l, wait):
        wait()
        m["tsum"][l] = jnp.sum(m["tland2"][l], axis=0)
        o_small[6 * l + 2 : 6 * l + 3] = m["tsum"][l, :, H : 2 * H]
        o_small[6 * l + 3 : 6 * l + 4] = m["tsum"][l, :, 0:H]
        base = pl.multiple_of(2 * H + me_d * 2 * W, LANES)
        dlr, dli, ar, ai = (m["tsum"][l, :, pl.ds(pl.multiple_of(base + k * Pn, LANES), Pn)] for k in range(4))
        kr, ki = m["tab"][l, me_d, 14][0:1], m["tab"][l, me_d, 15][0:1]
        size = kr * kr + ki * ki
        dkr, dki = (ar * kr - ai * ki) / size, (ar * ki + ai * kr) / size
        _, pull = jax.vjp(transition, *(m["prm"][i, me_d, l] for i in range(3)))
        for k, v in enumerate(pull((dlr, dli, dkr, dki))):
            o_lam[3 * l + k : 3 * l + k + 1] = v

    def gate_share(l):
        src = m["fX"].at[l, pl.ds(geo.out_rows, geo.half_rows)]
        dst = m["glf"].at[l, me_d]
        (wait,) = net.swap([(src, dst, dst)])
        m["glf"][l, me_d] = m["fX"][l, geo.out_rows : geo.out_rows + geo.half_rows]
        return wait

    tiny_wait = {}
    for l in reversed(range(LAYERS)):
        X, I = reductions["X", l], reductions["I", l]

        def open_gate(i):
            dout = rows(m["g"], i) * masked(i)
            sig = rows(m["sig"].at[l], i)
            v = (dout * flat(m["act"].at[l], i) * sig * (1.0 - sig)).astype(BF16)
            put_flat(m["dgt"], i, v)
            return (v.astype(F32),)

        (d_glub,) = sweep(open_gate, 1)
        put3(m["tmp"], dot(m["dgt"][...], m["glw"][l], 1, 1))

        def through(i):
            dout = rows(m["g"], i) * masked(i)
            d = (rows(m["tmp"], i) + dout * rows(m["sig"].at[l], i)) * rows(m["dge"].at[l], i)
            m["dmx"][pl.ds(i * GROUP, GROUP)] = d
            put_flat(m["dml"], i, d)
            return (d * flat(m["nrm"].at[l], i),)

        (d_feed,) = sweep(through, 1)
        m["ds"][...] = dot(m["dml"][...], m["wout"][l], 1, 1)
        ends_up, ends_dn = scan(l, 1, m["ds"], True, zeros4, None)

        def window():
            out_grads(l)
            X.pair_send()
            if l == 0:
                reductions["X", 1].step()
                reductions["I", 1].step()
                tiny_wait[1] = tiny_middle(1, tiny_wait[1])
            X.step()

        in_up, in_dn = carries(LAYERS + l, l, 1, ends_up, ends_dn, True, window)

        def save(dd, at, value):
            m["r"][pl.ds(at, 16), dd * W : (dd + 1) * W] = value

        scan(l, 1, m["ds"], True, (*in_up, *in_dn), save)
        if l == 0:
            in_grads(l)
            I.pair_send()
        put3(m["tmp"], dot(m["r"][...], m["win"][l], 1, 1))
        if l == 0:
            reductions["I", 1].step()
            I.step()
        v_feed, v_mean, v_inv = rep(feed[l : l + 1]), rep(stat(l, 0)), rep(stat(l, 1))

        def normed_grad(i):
            d = (v_feed * rows(m["dmx"], i) + rows(m["tmp"], i)) * masked(i)
            m["tmp"][pl.ds(i * GROUP, GROUP)] = d
            return d, d * ((rows(m["xs"].at[l], i) - v_mean) * v_inv)

        plain, scaled = sweep(normed_grad, 2)
        slot = 1 + l
        m["msg"][slot, 0:1] = plain
        m["msg"][slot, 1:2] = scaled
        back_sums = sum_over_all(m["msg"].at[slot], "", slot)
        if l > 0:
            in_grads(l)
            I.pair_send()
        tiny_wait[l] = tiny_sums(l, d_glub, d_feed)
        if l > 0:
            I.step()
            X.step()
        else:
            reductions["X", 1].step()
            X.step()
        sums = back_sums()
        plain, scaled = sums[0:1], sums[1:2]
        o_small[6 * l + 0 : 6 * l + 1] = scaled
        o_small[6 * l + 1 : 6 * l + 2] = plain
        inv = stat(l, 1)
        inv_count = m["stat"][15:16]
        v_scale = rep(inv * gain[l : l + 1])
        v_plain, v_scaled = rep(plain * inv_count), rep(scaled * inv_count * inv)

        def stream_grad(i):
            lead = rows(m["tmp"], i) - masked(i) * (v_plain + (rows(m["xs"].at[l], i) - v_mean) * v_scaled)
            at = pl.ds(i * GROUP, GROUP)
            m["g"][at] = m["g"][at] + v_scale * lead

        sweep(stream_grad)

    deliver(m["g"], o_ig)

    X1, I1, X0, I0 = (reductions[k, l] for l in (1, 0) for k in ("X", "I"))
    tiny_wait[0] = tiny_middle(0, tiny_wait[0])
    tiny_end(1, tiny_wait[1])
    for red in (I1, I0, X0, I0, X1):
        red.step()
    tiny_end(0, tiny_wait[0])
    for red in (X1, I1, I0, X0, I1):
        red.step()
    X1.done()
    g1 = gate_share(1)
    I1.done()
    for red in (I0, X0, I0, X0):
        red.step()
    I0.done()
    X0.done()
    g0 = gate_share(0)
    g1()
    g0()
    for k in geo.rows:
        reductions[k, 0].settle()
    for w in out_waits:
        w()
    net.finish()


def on_device(sizes, inputs, cotangent, lengths, gain, bias, in_proj, out_proj, rate, step, freq, feed, gluw, glub, rmean, rvar):
    geo = Geometry(sizes, inputs.shape, rate.shape[-1])
    T, H, W = geo.T, geo.H, geo.W
    v = scratch_shapes(geo)
    held = sum(math.prod(shape) * jnp.dtype(kind).itemsize for shape, kind in v.values())
    hbm = pl.BlockSpec(memory_space=pl.ANY)
    vmem = pl.BlockSpec(memory_space=pltpu.VMEM)
    smem = pl.BlockSpec(memory_space=pltpu.SMEM)
    outs = [
        pltpu.VMEM((geo.seqs, T, H), F32),
        pltpu.VMEM((geo.seqs, T, H), F32),
        pltpu.VMEM((LAYERS, geo.rows["X"], WIDE), BF16),
        pltpu.VMEM((LAYERS, geo.D, geo.half_rows, WIDE), BF16),
        pltpu.VMEM((LAYERS, geo.rows["I"], WIDE), BF16),
        pltpu.VMEM((6 * LAYERS, H), F32),
        pltpu.VMEM((3 * LAYERS, geo.Pn), F32),
    ]
    act, ig, gx, gl, gi, small, lam = pl.pallas_call(
        functools.partial(body, geo, tuple(v)),
        out_shape=outs,
        in_specs=[smem, hbm, hbm, vmem, vmem, hbm, hbm, hbm, hbm, hbm, vmem, hbm, vmem, vmem, vmem],
        out_specs=[vmem] * 7,
        scratch_shapes=[pltpu.VMEM(*s) for s in v.values()]
        + [pltpu.SemaphoreType.DMA((SEMAPHORES,)), pltpu.SemaphoreType.DMA((SEMAPHORES,)), pltpu.SemaphoreType.DMA((32,))],
        compiler_params=pltpu.CompilerParams(
            collective_id=0, has_side_effects=True, vmem_limit_bytes=held + SPARE_BYTES
        ),
    )(lengths, inputs, cotangent, gain, bias, in_proj, out_proj, rate, step, freq, feed, gluw, glub, rmean, rvar)
    return finish(geo, act, ig, gx, gl, gi, small, lam)


def results(geo, *refs):
    T, H, W, Pn, L = geo.T, geo.H, geo.W, geo.Pn, LAYERS
    act, ig, gx, gl, gi, small, lam = refs[:7]
    (o_act, o_ig, o_gain, o_bias, o_in, o_out, o_rate, o_step, o_freq, o_feed, o_glu, o_glub, o_mean, o_var) = refs[7:21]
    v_in, v_out, v_glu, sems = refs[21:]
    used = [0]

    def copy(src, dst):
        sem = sems.at[used[0]]
        used[0] += 1
        c = pltpu.make_async_copy(src, dst, sem)
        c.start()
        return c

    order = list(reversed(range(L)))
    waits = [copy(act, o_act), copy(ig, o_ig)]
    for l in range(L):
        for k, o in enumerate((o_gain, o_bias, o_feed, o_glub, o_mean, o_var)):
            o[l : l + 1] = small[6 * l + k : 6 * l + k + 1]
        for k, o in enumerate((o_rate, o_step, o_freq)):
            o[l] = lam[3 * l + k : 3 * l + k + 1]
    block = 64
    half = H // 2
    for l in order:
        for n in range(H // WIDE):

            def move(i, _):
                v_out[l, pl.ds(i * block, block), n * WIDE : (n + 1) * WIDE] = gx[
                    l, pl.ds(n * W + i * block, block)
                ].astype(F32)
                return 0

            lax.fori_loop(0, W // block, move, 0)
        waits.append(copy(v_out.at[l], o_out.at[l, 0]))
        for n in range(Pn // LANES):

            def move(i, _):
                value = gi[l, pl.ds(n * H + i * block, block)].astype(F32)
                at = pl.ds(i * block, block)
                v_in[l, at, n * LANES : (n + 1) * LANES] = value[:, :LANES]
                v_in[l, at, Pn + n * LANES : Pn + (n + 1) * LANES] = value[:, LANES:]
                return 0

            lax.fori_loop(0, H // block, move, 0)
        waits.append(copy(v_in.at[l], o_in.at[l, 0]))
        for d in range(geo.D):
            for n in range(H // WIDE):

                def move(i, _):
                    value = gl[l, d, pl.ds(n * half + i * block, block)].astype(F32)
                    v_glu[l, pl.ds(d * half + i * block, block), n * WIDE : (n + 1) * WIDE] = value
                    return 0

                lax.fori_loop(0, half // block, move, 0)
        waits.append(copy(v_glu.at[l], o_glu.at[l]))
    for c in waits:
        c.wait()


def finish(geo, act, ig, gx, gl, gi, small, lam):
    T, H, W, Pn, L = geo.T, geo.H, geo.W, geo.Pn, LAYERS
    hbm = pl.BlockSpec(memory_space=pl.ANY)
    vmem = pl.BlockSpec(memory_space=pltpu.VMEM)
    row = jax.ShapeDtypeStruct((L, H), F32)
    lam_row = jax.ShapeDtypeStruct((L, 1, Pn), F32)
    stream = jax.ShapeDtypeStruct((geo.seqs, T, H), F32)
    outs = [
        stream,
        stream,
        row,
        row,
        jax.ShapeDtypeStruct((L, 1, H, W), F32),
        jax.ShapeDtypeStruct((L, 1, W, H), F32),
        lam_row,
        lam_row,
        lam_row,
        row,
        jax.ShapeDtypeStruct((L, H, H), F32),
        row,
        row,
        row,
    ]
    where = [hbm, hbm, vmem, vmem, hbm, hbm, vmem, vmem, vmem, vmem, hbm, vmem, vmem, vmem]
    return pl.pallas_call(
        functools.partial(results, geo),
        out_shape=outs,
        in_specs=[vmem] * 7,
        out_specs=where,
        scratch_shapes=[
            pltpu.VMEM((L, H, W), F32),
            pltpu.VMEM((L, W, H), F32),
            pltpu.VMEM((L, H, H), F32),
            pltpu.SemaphoreType.DMA((16,)),
        ],
        compiler_params=pltpu.CompilerParams(vmem_limit_bytes=16 << 20),
    )(act, ig, gx, gl, gi, small, lam)


def solution(mesh):
    tokens = P("batch", "seq", None)
    per_dir = P(None, "dir", None)
    mats = P(None, "dir", None, None)
    in_specs = (tokens, tokens, P("batch"), P(), P(), mats, mats, per_dir, per_dir, per_dir) + (P(),) * 5
    out_specs = (tokens, tokens, P(), P(), mats, mats, per_dir, per_dir, per_dir) + (P(),) * 5
    return jax.shard_map(
        functools.partial(on_device, dict(mesh.shape)),
        mesh=mesh,
        in_specs=in_specs,
        out_specs=out_specs,
        check_vma=False,
    )
```

```python
import functools
import math

import jax
import jax.numpy as jnp
from jax import lax
from jax.experimental import pallas as pl
from jax.experimental.pallas import tpu as pltpu
from jax.sharding import PartitionSpec as P

LAYERS = 2
EPSILON = 1e-05
MOMENTUM = 0.9
F32 = jnp.float32
BF16 = jnp.bfloat16
AXES = ("dir", "seq", "batch")
MESH = pl.DeviceIdType.MESH
LANES = 128
CHUNKS = 8
WIDE = 256
SPARE_BYTES = 5 << 19
SEMAPHORES = 144
SHARES = {"X": ((2, "xy"), (2, "yx"), (2, "xy"), (2, "yx")), "I": ((3, "xy"), (3, "yx"))}
SCHEDULE = (
    "B11- da1- B21- ds1-",
    "p11- og1- X1p X13",
    "X10 p21- dn1- B31-",
    "X11 X12 ig1- X13",
    "X10 ty1- I1p I11",
    "I10 X11 X12 X10",
    "B41- B10- da0- X13",
    "B20- og0- X10 ds0-",
    "I11 I10 X13 p10-",
    "X11 X0p X01 X02",
    "X00 X12 X03 I11",
    "p20- X11 X13 X01",
    "X02 X12 X10 I10",
    "ig0- tm1- X03 X00",
    "I0p I00 I01 X02",
    "X01 I11 X03 dn0-",
    "X00 X12 X10 ty0-",
    "X11 X02 X13 I01",
    "X01 I11 te1- I00",
    "I10 X11 X02 I01",
    "X01 X00 X03 I00",
    "X12 tm0- I10 X01",
    "X13 X02 B30- I01",
    "I10 X12 X03 X00",
    "I11 I00 I01 X01",
    "I00 X00 X03 I10",
    "I11 X10 X11 gs1-",
    "B40- I00 te0- I01",
    "X02 X00 X03 I00",
    "I01 gs0-",
)


def transition(rate_vec, step_vec, freq_vec):
    half_a = 0.5 * step_vec * rate_vec
    half_c = 0.5 * step_vec * freq_vec
    denominator = (1.0 + half_a) * (1.0 + half_a) + half_c * half_c
    lam_re = (1.0 - half_a * half_a - half_c * half_c) / denominator
    lam_im = 2.0 * half_c / denominator
    kap_re = step_vec * (1.0 + half_a) / denominator
    kap_im = step_vec * half_c / denominator
    return (lam_re, lam_im, kap_re, kap_im)


def dot(a, b, ca, cb):
    return lax.dot_general(a, b, (((ca,), (cb,)), ((), ())), preferred_element_type=F32)


def cmul(a, b):
    return (a[0] * b[0] - a[1] * b[1], a[0] * b[1] + a[1] * b[0])


def conj(a):
    return (a[0], -a[1])


def widen(mask):
    return jnp.concatenate([mask] * 4, axis=-1)


class Geometry:
    def __init__(self, sizes, local_shape, states):
        self.D, self.S, self.B = (sizes[a] for a in AXES)
        self.sizes = dict(sizes)
        self.seqs, self.T, self.H = local_shape
        self.Pn = states
        self.W = 2 * states
        self.J = self.T // CHUNKS
        self.N = self.D * self.S * self.B
        self.unit = 16 * self.S * self.B
        up = lambda n: -(-n // self.unit) * self.unit
        self.out_rows = (self.H // WIDE) * self.W
        self.half_rows = (self.H // WIDE) * (self.H // 2)
        self.in_rows = (self.Pn // LANES) * self.H
        self.used = {"X": self.out_rows + self.half_rows, "I": self.in_rows}
        self.rows = {k: up(v) for k, v in self.used.items()}
        bits = tuple(("batch", k) for k in range((self.B - 1).bit_length()))
        seq = (("seq", None),)
        ways = {"xy": bits + seq, "yx": bits[::-1] + seq, "zx": seq + bits, "zy": seq + bits[::-1]}
        self.colors = {}
        for k, n in self.rows.items():
            shares = SHARES[k]
            if n // self.unit != sum(count for count, _ in shares):
                shares = ((n // self.unit, "xy"),)
            at, self.colors[k] = 0, []
            for count, name in shares:
                self.colors[k].append((at, count * self.unit, ways[name]))
                at += count * self.unit
        self.direct = self.N <= 64

    def ways(self, dim):
        return self.S if dim[1] is None else 2


class Net:
    def __init__(self, geo, send_sems, recv_sems):
        self.geo, self.send_sems, self.recv_sems = geo, send_sems, recv_sems
        self.used_send = 0
        self.used_recv = 0
        self.at = {a: lax.axis_index(a) for a in AXES}
        self.unsent = []

    def send_sem(self):
        self.used_send += 1
        return self.send_sems.at[self.used_send - 1]

    def recv_sem(self):
        self.used_recv += 1
        return self.recv_sems.at[self.used_recv - 1]

    def index(self, axes):
        lin = 0
        for a in axes:
            lin = lin * self.geo.sizes[a] + self.at[a]
        return lin

    def count(self, axes):
        n = 1
        for a in axes:
            n *= self.geo.sizes[a]
        return n

    def peers(self, axes, act):
        n = self.count(axes)

        def at_offset(k):
            where, lin, rest, coords = {}, 0, k, []
            for a in reversed(axes):
                size = self.geo.sizes[a]
                off = rest % size
                rest = rest // size
                coords.append((a, lax.rem(self.at[a] + off, size)))
            for a, c in reversed(coords):
                where[a] = c
                lin = lin * self.geo.sizes[a] + c
            act(where, lin, k)

        if n <= 64:
            for k in range(n - 1, 0, -1):
                at_offset(k)
        else:

            def body(k, _):
                at_offset(k)
                return 0

            lax.fori_loop(1, n, body, 0)

    def place(self, dim):
        axis, bit = dim
        return self.at[axis] if bit is None else lax.rem(lax.div(self.at[axis], 1 << bit), 2)

    def others(self, dim, act):
        axis, bit = dim
        if bit is None:
            self.peers((axis,), act)
        else:
            mine = self.place(dim)
            act({axis: self.at[axis] + (1 - 2 * mine) * (1 << bit)}, 1 - mine, 1)

    def put(self, src, dst, send, recv, peer):
        pltpu.make_async_remote_copy(
            src_ref=src, dst_ref=dst, send_sem=send, recv_sem=recv, device_id=peer, device_id_type=MESH
        ).start()

    def wait(self, ref, sem):
        pltpu.make_async_copy(ref, ref, sem).wait()

    def gather(self, src, land, axes):
        n = self.count(axes)
        send, recv = self.send_sem(), self.recv_sem()
        slot = self.index(axes)
        self.peers(axes, lambda peer, lin, k: self.put(src, land.at[slot], send, recv, peer))
        land[slot] = src[...]
        size = land.at[pl.ds(0, n - 1)]
        self.unsent.append((size, send))
        return functools.partial(self.wait, size, recv)

    def swap(self, pieces):
        peer = {"dir": 1 - self.at["dir"]}
        waits = []
        for src, dst, size in pieces:
            send, recv = self.send_sem(), self.recv_sem()
            self.put(src, dst, send, recv, peer)
            self.unsent.append((size, send))
            waits.append(functools.partial(self.wait, size, recv))
        return waits

    def finish(self):
        for size, send in self.unsent:
            self.wait(size, send)


def scratch_shapes(geo):
    T, H, W, J, S, N, Pn = geo.T, geo.H, geo.W, geo.J, geo.S, geo.N, geo.Pn
    L, D = LAYERS, geo.D
    v = {
        "mask": ((J, CHUNKS, LANES), F32),
        "win": ((L, H, D * W), BF16),
        "wout": ((L, D * W, H), BF16),
        "glw": ((L, H, H), BF16),
        "prm": ((3, D, L, 1, Pn), F32),
        "tab": ((L, D, 16, CHUNKS, Pn), F32),
        "xs": ((L + 1, J, CHUNKS, H), F32),
        "stat": ((16, H), F32),
        "nrm": ((L, T, H), BF16),
        "u": ((L, T, D * W), F32),
        "st": ((L, T + 32, D * W), BF16),
        "act": ((L, T, H), BF16),
        "sig": ((L, J, CHUNKS, H), BF16),
        "dge": ((L, J, CHUNKS, H), BF16),
        "tmp": ((J, CHUNKS, H), F32),
        "g": ((J, CHUNKS, H), F32),
        "dmx": ((J, CHUNKS, H), F32),
        "dml": ((T, H), BF16),
        "dgt": ((T, H), BF16),
        "ds": ((T, D * W), F32),
        "r": ((T, D * W), BF16),
        "msg0": ((2, H + LANES), F32),
        "msg": ((3, 2, H), F32),
        "smsg": ((2 * L, 1, D * W), F32),
        "sland": ((2 * L, S, 1, D * W), F32),
        "tiny": ((L, 1, 2 * H + 4 * W), F32),
        "tland1": ((L, D * geo.B, 1, 2 * H + 4 * W), F32),
        "tmid": ((L, 1, 2 * H + 4 * W), F32),
        "tland2": ((L, S, 1, 2 * H + 4 * W), F32),
        "tsum": ((L, 1, 2 * H + 4 * W), F32),
    }
    for k, lead, wide in (("0", (), H + LANES), ("", (3,), H)):
        if geo.direct:
            v["land" + k] = ((*lead, N, 2, wide), F32)
        else:
            v["near" + k] = ((*lead, D * geo.B, 2, wide), F32)
            v["mid" + k] = ((*lead, 2, wide), F32)
            v["far" + k] = ((*lead, S, 2, wide), F32)
    for k, rows in geo.rows.items():
        v["g" + k] = ((D, rows, WIDE), BF16)
        v["p" + k] = ((L, rows, WIDE), BF16)
        for c, (_, n, order) in enumerate(geo.colors[k]):
            for i, dim in enumerate(order):
                ways = geo.ways(dim)
                n //= ways
                v[f"land{i}{k}{c}"] = ((L, ways - 1, n, WIDE), BF16)
                if i == 0:
                    v[f"red{k}{c}"] = ((L, n, WIDE), BF16)
    return v


class Reduction:
    def __init__(self, geo, net, kind, layer, m):
        self.geo, self.net, self.kind, self.layer, self.m = geo, net, kind, layer, m
        self.rows = geo.rows[kind]
        self.colors = geo.colors[kind]
        self.full = m["f" + kind].at[layer]
        self.mine = m["g" + kind].at[net.at["dir"]]
        self.flows = None

    def pair_send(self):
        landing = self.m["p" + self.kind].at[self.layer]
        other = self.m["g" + self.kind].at[1 - self.net.at["dir"]]
        (self.pair_wait,) = self.net.swap([(other, landing, landing)])
        self.held = [self.net.unsent.pop()]

    def settle(self):
        for size, send in self.held:
            self.net.wait(size, send)

    def pair_done(self):
        self.pair_wait()
        landing = self.m["p" + self.kind].at[self.layer]
        block = 64

        def body(i, _):
            at = pl.ds(i * block, block)
            self.mine[at] = self.mine[at] + landing[at]
            return 0

        lax.fori_loop(0, self.rows // block, body, 0)

    def scatter(self, dim, src, base, part, land):
        net = self.net
        send, recv = net.send_sem(), net.recv_sem()
        net.others(
            dim,
            lambda peer, lin, k: net.put(
                src.at[pl.ds(base + lin * part, part)], land.at[k - 1], send, recv, peer
            ),
        )
        net.unsent.append((land, send))
        return functools.partial(net.wait, land, recv)

    def add(self, own, own_at, land, n, out, out_at, part):
        block = next(b for b in (64, 48, 32, 16) if part % b == 0)

        def body(i, _):
            if n == 2:
                out[pl.ds(out_at + i * block, block)] = (
                    own[pl.ds(own_at + i * block, block)] + land[0, pl.ds(i * block, block)]
                )
                return 0
            total = own[pl.ds(own_at + i * block, block)].astype(F32)
            for k in range(min(n - 1, 7)):
                total = total + land[k, pl.ds(i * block, block)].astype(F32)
            if n - 1 > 7:
                total = lax.fori_loop(
                    7, n - 1, lambda k, t: t + land[k, pl.ds(i * block, block)].astype(F32), total
                )
            out[pl.ds(out_at + i * block, block)] = total.astype(BF16)
            return 0

        lax.fori_loop(0, part // block, body, 0)

    def spread(self, dim, base, part):
        net, n = self.net, self.geo.ways(dim)
        send, recv = net.send_sem(), net.recv_sem()
        mine = self.full.at[pl.ds(base, part)]
        net.others(dim, lambda peer, lin, k: net.put(mine, mine, send, recv, peer))
        size = self.full.at[pl.ds(0, (n - 1) * part)]
        net.unsent.append((size, send))
        return functools.partial(net.wait, size, recv)

    def flow(self, c):
        base, size, order = self.colors[c]
        red = self.m[f"red{self.kind}{c}"].at[self.layer]
        src, src_at, at = self.mine, base, base
        owned = []
        for i, dim in enumerate(order):
            n = self.geo.ways(dim)
            part = size // n
            land = self.m[f"land{i}{self.kind}{c}"].at[self.layer]
            wait = self.scatter(dim, src, src_at, part, land)
            if i == 0:
                self.held.append(self.net.unsent.pop())
            yield
            wait()
            mine = self.net.place(dim)
            own_at, at = src_at + mine * part, at + mine * part
            if i + 1 == len(order):
                out, out_at = self.full, at
            else:
                out, out_at = red, 0 if i == 0 else own_at
            self.add(src, own_at, land, n, out, out_at, part)
            src, src_at, size = red, out_at, part
            owned.append((dim, at, part))
        for dim, at, part in reversed(owned):
            wait = self.spread(dim, at, part)
            yield
            wait()

    def open(self):
        self.pair_done()
        self.flows = [self.flow(c) for c in range(len(self.colors))]

    def step(self, c):
        if c < len(self.flows):
            next(self.flows[c], None)

    def done(self):
        for flow in self.flows:
            for _ in flow:
                pass


def body(geo, names, *refs):
    T, H, W, J, S, N, Pn = geo.T, geo.H, geo.W, geo.J, geo.S, geo.N, geo.Pn
    (lengths, inputs, cotangent, gain, bias, in_proj, out_proj, rate, step, freq, feed, gluw, glub, rmean, rvar) = refs[:15]
    (o_act, o_ig, o_gx, o_gl, o_gi, o_small, o_lam) = refs[15:22]
    scr = refs[22:]
    m = dict(zip(names, scr))
    m["fX"], m["fI"], m["glf"] = o_gx, o_gi, o_gl
    m["xin"], m["cin"], m["pm"] = m["dgt"], m["dml"], m["r"].at[:, 0:T]
    send_sems, recv_sems, local_sems = scr[len(names) :]
    net = Net(geo, send_sems, recv_sems)
    me_d, me_s = net.at["dir"], net.at["seq"]
    local = [0]

    def fetch(src, dst):
        sem = local_sems.at[local[0]]
        local[0] += 1
        copy = pltpu.make_async_copy(src, dst, sem)
        copy.start()
        return copy.wait

    def sum_over_all(msg, which, slot=None):
        at = lambda name: m[name + which] if slot is None else m[name + which].at[slot]
        if geo.direct:
            arrived = net.gather(msg, at("land"), AXES)

            def total():
                arrived()
                return jnp.sum(at("land")[...], axis=0)

            return total
        arrived = net.gather(msg, at("near"), ("dir", "batch"))

        def total():
            arrived()
            at("mid")[...] = jnp.sum(at("near")[...], axis=0)
            net.gather(at("mid"), at("far"), ("seq",))()
            return jnp.sum(at("far")[...], axis=0)

        return total

    barrier = pltpu.get_barrier_semaphore()
    net.peers(AXES, lambda peer, lin, k: pl.semaphore_signal(barrier, 1, device_id=peer, device_id_type=MESH))
    w_x = fetch(inputs.at[me_d], m["xin"])
    w_c = fetch(cotangent.at[me_d], m["cin"])
    raw = (rate, step, freq)
    w_p = [fetch(raw[i], m["prm"].at[i, me_d]) for i in range(3)]
    cols = pl.ds(pl.multiple_of(me_d * W, LANES), W)
    rows_of = pl.ds(pl.multiple_of(me_d * W, 16), W)
    in_at = [m["win"].at[l, :, cols] for l in range(LAYERS)]
    out_at = [m["wout"].at[l, rows_of] for l in range(LAYERS)]
    w_in = [fetch(in_proj.at[l, 0], in_at[l]) for l in range(LAYERS)]
    w_out = [fetch(out_proj.at[l, 0], out_at[l]) for l in range(LAYERS)]
    w_g = fetch(gluw, m["glw"])

    length = lengths[me_d]
    shape = (J, CHUNKS, LANES)
    position = (
        me_s * T
        + lax.broadcasted_iota(jnp.int32, shape, 1) * J
        + lax.broadcasted_iota(jnp.int32, shape, 0)
    )
    m["mask"][...] = jnp.where(position < length, 1.0, 0.0).astype(F32)

    def permutation(i, _):
        at = pl.ds(i * 64, 64)
        row = i * 64 + lax.broadcasted_iota(jnp.int32, (64, T), 0)
        col = lax.broadcasted_iota(jnp.int32, (64, T), 1)
        wanted = lax.rem(row, CHUNKS) * J + lax.div(row, CHUNKS)
        m["pm"][at] = jnp.where(col == wanted, 1.0, 0.0).astype(BF16)
        return 0

    lax.fori_loop(0, T // 64, permutation, 0)

    def put3(ref3, value):
        ref3[...] = value.reshape(J, CHUNKS, H)

    def reorder(src, dst):
        put3(dst, dot(m["pm"][...], src[...], 1, 0))

    GROUP = 4
    ROWS = GROUP * CHUNKS

    def rows(ref, i):
        return ref[pl.ds(i * GROUP, GROUP)].astype(F32)

    def flat(ref, i):
        return ref[pl.ds(i * ROWS, ROWS)].astype(F32).reshape(GROUP, CHUNKS, -1)

    def put_flat(ref, i, value):
        ref[pl.ds(i * ROWS, ROWS)] = value.reshape(ROWS, -1).astype(BF16)

    def sweep(act, sums=0):
        zero = tuple(jnp.zeros((CHUNKS, H), F32) for _ in range(sums))

        def one(i, acc):
            more = act(i)
            if not sums:
                return acc
            return tuple(a + jnp.sum(v, axis=0) for a, v in zip(acc, more))

        acc = lax.fori_loop(0, T // ROWS, one, zero)
        return tuple(jnp.sum(a, axis=0, keepdims=True) for a in acc)

    def rep(row):
        return jnp.broadcast_to(row, (CHUNKS, row.shape[-1]))

    masked = lambda i: widen(rows(m["mask"], i))

    w_x()
    reorder(m["xin"], m["xs"].at[0])

    def first(i):
        x = rows(m["xs"].at[0], i)
        xm = x * masked(i)
        return xm, xm * x

    s1, s2 = sweep(first, 2)
    here = jnp.sum(jnp.sum(m["mask"][...], axis=0), axis=0, keepdims=True)
    m["msg0"][0:1, 0:H] = s1
    m["msg0"][1:2, 0:H] = s2
    m["msg0"][:, H:] = jnp.broadcast_to(here, (2, LANES))

    pl.semaphore_wait(barrier, N - 1)
    stats = sum_over_all(m["msg0"], "0")
    send_in, send_out = [None] * LAYERS, [None] * LAYERS
    prm_waits = net.swap([(raw[i], m["prm"].at[i, me_d], m["prm"].at[i, me_d]) for i in range(3)])
    for l in range(LAYERS):
        (send_in[l],) = net.swap([(in_proj.at[l, 0], in_at[l], in_at[l])])
        (send_out[l],) = net.swap([(out_proj.at[l, 0], out_at[l], out_at[l])])

    for w in w_p + prm_waits:
        w()
    for l in range(LAYERS):
        for dd in range(geo.D):
            lr, li, kr, ki = transition(*(m["prm"][i, dd, l] for i in range(3)))
            power = (lr, li)
            for _ in range((J).bit_length() - 1):
                power = cmul(power, power)
            ladder = [power]
            for _ in range(3):
                ladder.append(cmul(ladder[-1], ladder[-1]))
            wide = [tuple(rep(v) for v in p) for p in ladder]
            chunk = lax.broadcasted_iota(jnp.int32, (CHUNKS, Pn), 0)
            one = (jnp.ones((CHUNKS, Pn), F32), jnp.zeros((CHUNKS, Pn), F32))
            up, down = one, one
            for k in range(3):
                bit = lax.rem(lax.div(chunk, 1 << k), 2)
                grown = cmul(up, wide[k])
                up = tuple(jnp.where(bit == 1, a, b) for a, b in zip(grown, up))
                grown = cmul(down, wide[k])
                down = tuple(jnp.where(bit == 0, a, b) for a, b in zip(grown, down))
            table = [rep(lr), rep(li), *up, *down]
            for p in wide:
                table.extend(p)
            table.extend([rep(kr), rep(ki)])
            for k, v in enumerate(table):
                m["tab"][l, dd, k] = v

    def entry(l, dd, k, minus):
        re, im = m["tab"][l, dd, 2 * k], m["tab"][l, dd, 2 * k + 1]
        return (re, -im) if minus else (re, im)

    def fold(l):
        for dd in range(geo.D):
            kr, ki = m["tab"][l, dd, 14][0:1], m["tab"][l, dd, 15][0:1]

            def some(i, _):
                at = pl.ds(i * 32, 32)
                w = m["win"][l, at, dd * W : (dd + 1) * W].astype(F32)
                re, im = w[:, :Pn], w[:, Pn:]
                new = jnp.concatenate([kr * re - ki * im, kr * im + ki * re], axis=1)
                m["win"][l, at, dd * W : (dd + 1) * W] = new.astype(BF16)
                return 0

            lax.fori_loop(0, H // 32, some, 0)

    for l in range(LAYERS):
        w_in[l]()
        send_in[l]()
        fold(l)
        w_out[l]()
        send_out[l]()
    w_c()
    reorder(m["cin"], m["g"])
    w_g()

    def split(block):
        return block[:, :Pn], block[:, Pn:]

    def advance(lam, h, d):
        return (lam[0] * h[0] - lam[1] * h[1] + d[0], lam[0] * h[1] + lam[1] * h[0] + d[1])

    def scan(l, up_dd, src, minus, start, emit):
        dn_dd = 1 - up_dd
        lam_up, lam_dn = entry(l, up_dd, 0, minus), entry(l, dn_dd, 0, minus)
        n = T // 16

        def two(i, carry):
            hu, hd = carry[:2], carry[2:]
            at_u, at_d = i * 16, (n - 1 - i) * 16
            bu = src[pl.ds(at_u, 16), up_dd * W : (up_dd + 1) * W]
            bd = src[pl.ds(at_d, 16), dn_dd * W : (dn_dd + 1) * W]
            keep_u, keep_d = [], []
            for k in range(2):
                hu = advance(lam_up, hu, split(bu[8 * k : 8 * k + 8]))
                hd = advance(lam_dn, hd, split(bd[8 - 8 * k : 16 - 8 * k]))
                keep_u.append(jnp.concatenate(hu, axis=1))
                keep_d.append(jnp.concatenate(hd, axis=1))
            if emit is not None:
                emit(up_dd, at_u, jnp.concatenate(keep_u, axis=0).astype(BF16))
                emit(dn_dd, at_d, jnp.concatenate(keep_d[::-1], axis=0).astype(BF16))
            return (*hu, *hd)

        out = lax.fori_loop(0, n, two, start, unroll=2)
        return out[:2], out[2:]

    chunk_at = lax.broadcasted_iota(jnp.int32, (CHUNKS, Pn), 0)

    def within(l, dd, ends, rising, minus):
        shift = (lambda v, k: pltpu.roll(v, k, 0)) if rising else (lambda v, k: pltpu.roll(v, CHUNKS - k, 0))
        inside = (lambda k: chunk_at >= k) if rising else (lambda k: chunk_at < CHUNKS - k)
        a = tuple(jnp.where(inside(1), shift(v, 1), 0.0) for v in ends)
        for k in range(3):
            far = tuple(jnp.where(inside(1 << k), shift(v, 1 << k), 0.0) for v in a)
            more = cmul(entry(l, dd, 3 + k, minus), far)
            a = (a[0] + more[0], a[1] + more[1])
        return a

    def carries(k, l, up_dd, ends_up, ends_dn, minus):
        dn_dd = 1 - up_dd
        pieces = [None] * geo.D
        for dd, ends, which in ((up_dd, ends_up, 2), (dn_dd, ends_dn, 1)):
            total = cmul(entry(l, dd, which, minus), ends)
            pieces[dd] = jnp.concatenate([jnp.sum(v, axis=0, keepdims=True) for v in total], axis=1)
        m["smsg"][k] = jnp.concatenate(pieces, axis=1)
        land = m["sland"].at[k]
        arrived = net.gather(m["smsg"].at[k], land, ("seq",))
        here_up = within(l, up_dd, ends_up, True, minus)
        here_dn = within(l, dn_dd, ends_dn, False, minus)
        def finish_up():
            arrived()
            def enter(dd, rising):
                whole = tuple(v[0:1] for v in entry(l, dd, 6, minus))
                zero = jnp.zeros((1, Pn), F32)

                def lap(i, state):
                    at = i if rising else S - 1 - i
                    piece = land[at][:, dd * W : (dd + 1) * W]
                    new = advance(whole, state, split(piece))
                    reached = (at < me_s) if rising else (at > me_s)
                    return tuple(jnp.where(reached, a, b) for a, b in zip(new, state))

                state = (zero, zero)
                if S <= 8:
                    for i in range(S):
                        state = lap(i, state)
                    return state
                return lax.fori_loop(0, S, lap, state)

            outs = []
            for dd, rising, here_ends, which in ((up_dd, True, here_up, 1), (dn_dd, False, here_dn, 2)):
                far = cmul(entry(l, dd, which, minus), tuple(rep(v) for v in enter(dd, rising)))
                outs.append((here_ends[0] + far[0], here_ends[1] + far[1]))
            return outs

        return finish_up

    zeros4 = tuple(jnp.zeros((CHUNKS, Pn), F32) for _ in range(4))

    def stat(l, k):
        return m["stat"][4 * l + k : 4 * l + k + 1]

    def set_stat(l, k, value):
        m["stat"][4 * l + k : 4 * l + k + 1] = value

    c0 = 0.7978845608028654
    c1 = 0.044715
    for l in range(LAYERS):
        sums = stats()
        if l == 0:
            m["stat"][15:16] = 1.0 / widen(sums[0:1, H:])
            sums = sums[:, :H]
        inv_count = m["stat"][15:16]
        mean = sums[0:1] * inv_count
        var = sums[1:2] * inv_count - mean * mean
        inv = lax.rsqrt(var + EPSILON)
        set_stat(l, 0, mean)
        set_stat(l, 1, inv)
        o_small[6 * l + 4 : 6 * l + 5] = MOMENTUM * rmean[l : l + 1] + (1.0 - MOMENTUM) * mean
        o_small[6 * l + 5 : 6 * l + 6] = MOMENTUM * rvar[l : l + 1] + (1.0 - MOMENTUM) * var
        v_mean, v_scale, v_bias = rep(mean), rep(inv * gain[l : l + 1]), rep(bias[l : l + 1])

        def normalise(i):
            x = rows(m["xs"].at[l], i)
            put_flat(m["nrm"].at[l], i, ((x - v_mean) * v_scale + v_bias) * masked(i))

        sweep(normalise)
        m["u"][l] = dot(m["nrm"][l], m["win"][l], 1, 0)
        ends_up, ends_dn = scan(l, 0, m["u"].at[l], False, zeros4, None)
        in_up, in_dn = carries(l, l, 0, ends_up, ends_dn, False)()
        both = lambda v: jnp.concatenate([jnp.concatenate(v, axis=1)] * 2, axis=0).astype(BF16)
        m["st"][l, 0:16, 0:W] = both(in_up)
        m["st"][l, T + 16 : T + 32, W:] = both(in_dn)

        def save(dd, at, value):
            m["st"][l, pl.ds(16 + at, 16), dd * W : (dd + 1) * W] = value

        scan(l, 0, m["u"].at[l], False, (*in_up, *in_dn), save)

        put3(m["tmp"], dot(m["st"][l, 16 : T + 16], m["wout"][l], 1, 0))
        v_feed = rep(feed[l : l + 1])

        def activate(i):
            v = rows(m["tmp"], i) + v_feed * flat(m["nrm"].at[l], i)
            sq = v * v
            t = jnp.tanh(c0 * v * (1.0 + c1 * sq))
            half = 0.5 * (1.0 + t)
            put_flat(m["act"].at[l], i, v * half)
            slope = half + 0.5 * v * (1.0 - t * t) * (c0 * (1.0 + 3.0 * c1 * sq))
            m["dge"][l, pl.ds(i * GROUP, GROUP)] = slope.astype(BF16)

        sweep(activate)
        put3(m["tmp"], dot(m["act"][l], m["glw"][l], 1, 0))
        v_glub = rep(glub[l : l + 1])

        def gate(i):
            sig = 0.5 + 0.5 * jnp.tanh(0.5 * (rows(m["tmp"], i) + v_glub))
            m["sig"][l, pl.ds(i * GROUP, GROUP)] = sig.astype(BF16)
            mk = masked(i)
            x = rows(m["xs"].at[l], i) + mk * flat(m["act"].at[l], i) * sig
            m["xs"][l + 1, pl.ds(i * GROUP, GROUP)] = x
            if l + 1 < LAYERS:
                xm = x * mk
                return xm, xm * x

        sums = sweep(gate, 2 if l + 1 < LAYERS else 0)
        if l + 1 < LAYERS:
            m["msg"][0, 0:1] = sums[0]
            m["msg"][0, 1:2] = sums[1]
            stats = sum_over_all(m["msg"].at[0], "", 0)

    out_waits = []

    def deliver(src, dst):
        send, recv = net.send_sem(), net.recv_sem()
        sem = local_sems.at[local[0]]
        local[0] += 1
        for c in range(CHUNKS):
            to = dst.at[me_d, pl.ds(c * J, J)]
            net.put(src.at[:, c], to, send, recv, {"dir": 1 - me_d})
            pltpu.make_async_copy(src.at[:, c], to, sem).start()
        net.unsent.append((dst.at[me_d], send))
        out_waits.append(functools.partial(net.wait, dst.at[1 - me_d], recv))
        out_waits.append(functools.partial(net.wait, dst.at[me_d], sem))

    deliver(m["xs"].at[LAYERS], o_act)

    reductions = {(k, l): Reduction(geo, net, k, l, m) for k in geo.rows for l in range(LAYERS)}

    def clear_rest(kind, l):
        used, rows_all = geo.used[kind], geo.rows[kind]
        if used < rows_all:
            for dd in range(geo.D):
                m["g" + kind][dd, used:rows_all] = jnp.zeros((rows_all - used, WIDE), BF16)

    def out_grads(l):
        if l + 1 < LAYERS:
            reductions["X", l + 1].settle()
        clear_rest("X", l)
        value = dot(m["st"][l, 16 : T + 16], m["dml"][...], 0, 0).astype(BF16)
        gates = dot(m["act"][l], m["dgt"][...], 0, 0).astype(BF16)
        half = H // 2
        for dd in range(geo.D):
            for i in range(H // WIDE):
                across = slice(i * WIDE, (i + 1) * WIDE)
                m["gX"][dd, i * W : (i + 1) * W] = value[dd * W : (dd + 1) * W, across]
                at = geo.out_rows + i * half
                m["gX"][dd, at : at + half] = gates[dd * half : (dd + 1) * half, across]

    def in_grads(l):
        if l + 1 < LAYERS:
            reductions["I", l + 1].settle()
        clear_rest("I", l)
        value = dot(m["nrm"][l], m["r"][...], 0, 0)
        for dd in range(geo.D):
            for i in range(Pn // LANES):
                across = slice(i * LANES, (i + 1) * LANES)
                kr, ki = m["tab"][l, dd, 14, 0:1, across], m["tab"][l, dd, 15, 0:1, across]
                at = dd * W + i * LANES
                re, im = value[:, at : at + LANES], value[:, at + Pn : at + Pn + LANES]
                new = jnp.concatenate([kr * re + ki * im, kr * im - ki * re], axis=1)
                m["gI"][dd, i * H : (i + 1) * H] = new.astype(BF16)

    def tiny_sums(l, d_glub, d_feed):
        m["tiny"][l, :, 0:H] = d_glub
        m["tiny"][l, :, H : 2 * H] = d_feed
        for dd in range(geo.D):

            def some(i, acc):
                at = i * 16
                across = slice(dd * W, (dd + 1) * W)
                rr, ri = split(m["r"][pl.ds(at, 16), across].astype(F32))
                ur, ui = split(m["u"][l, pl.ds(at, 16), across])
                cur = m["st"][l, pl.ds(at + 16, 16), across].astype(F32)
                if dd == 0:
                    near = m["st"][l, pl.ds(at, 16), across].astype(F32)
                    prev = jnp.concatenate([near[8:], cur[:8]], axis=0)
                else:
                    near = m["st"][l, pl.ds(at + 32, 16), across].astype(F32)
                    prev = jnp.concatenate([cur[8:], near[:8]], axis=0)
                hr, hi = split(prev)
                new = (rr * hr + ri * hi, ri * hr - rr * hi, rr * ur + ri * ui, ri * ur - rr * ui)
                return tuple(a + v[:8] + v[8:] for a, v in zip(acc, new))

            acc = lax.fori_loop(0, T // 16, some, zeros4)
            base = 2 * H + dd * 2 * W
            for k, v in enumerate(acc):
                m["tiny"][l, :, base + k * Pn : base + (k + 1) * Pn] = jnp.sum(v, axis=0, keepdims=True)
        return net.gather(m["tiny"].at[l], m["tland1"].at[l], ("dir", "batch"))

    def tiny_middle(l, wait):
        wait()
        m["tmid"][l] = jnp.sum(m["tland1"][l], axis=0)
        return net.gather(m["tmid"].at[l], m["tland2"].at[l], ("seq",))

    def tiny_end(l, wait):
        wait()
        m["tsum"][l] = jnp.sum(m["tland2"][l], axis=0)
        o_small[6 * l + 2 : 6 * l + 3] = m["tsum"][l, :, H : 2 * H]
        o_small[6 * l + 3 : 6 * l + 4] = m["tsum"][l, :, 0:H]
        base = pl.multiple_of(2 * H + me_d * 2 * W, LANES)
        dlr, dli, ar, ai = (m["tsum"][l, :, pl.ds(pl.multiple_of(base + k * Pn, LANES), Pn)] for k in range(4))
        kr, ki = m["tab"][l, me_d, 14][0:1], m["tab"][l, me_d, 15][0:1]
        size = kr * kr + ki * ki
        dkr, dki = (ar * kr - ai * ki) / size, (ar * ki + ai * kr) / size
        _, pull = jax.vjp(transition, *(m["prm"][i, me_d, l] for i in range(3)))
        for k, v in enumerate(pull((dlr, dli, dkr, dki))):
            o_lam[3 * l + k : 3 * l + k + 1] = v

    def gate_share(l):
        src = m["fX"].at[l, pl.ds(geo.out_rows, geo.half_rows)]
        dst = m["glf"].at[l, me_d]
        (wait,) = net.swap([(src, dst, dst)])
        m["glf"][l, me_d] = m["fX"][l, geo.out_rows : geo.out_rows + geo.half_rows]
        return wait

    kept = {}

    def stage_b1(l):
        def open_gate(i):
            dout = rows(m["g"], i) * masked(i)
            sig = rows(m["sig"].at[l], i)
            v = (dout * flat(m["act"].at[l], i) * sig * (1.0 - sig)).astype(BF16)
            put_flat(m["dgt"], i, v)
            return (v.astype(F32),)

        (kept["glub", l],) = sweep(open_gate, 1)

    def stage_da(l):
        put3(m["tmp"], dot(m["dgt"][...], m["glw"][l], 1, 1))

    def stage_b2(l):
        def through(i):
            dout = rows(m["g"], i) * masked(i)
            d = (rows(m["tmp"], i) + dout * rows(m["sig"].at[l], i)) * rows(m["dge"].at[l], i)
            m["dmx"][pl.ds(i * GROUP, GROUP)] = d
            put_flat(m["dml"], i, d)
            return (d * flat(m["nrm"].at[l], i),)

        (kept["feed", l],) = sweep(through, 1)

    def stage_ds(l):
        m["ds"][...] = dot(m["dml"][...], m["wout"][l], 1, 1)

    def stage_p1(l):
        ends_up, ends_dn = scan(l, 1, m["ds"], True, zeros4, None)
        kept["enter", l] = carries(LAYERS + l, l, 1, ends_up, ends_dn, True)

    def stage_og(l):
        out_grads(l)
        reductions["X", l].pair_send()

    def stage_p2(l):
        in_up, in_dn = kept["enter", l]()

        def save(dd, at, value):
            m["r"][pl.ds(at, 16), dd * W : (dd + 1) * W] = value

        scan(l, 1, m["ds"], True, (*in_up, *in_dn), save)

    def stage_ig(l):
        in_grads(l)
        reductions["I", l].pair_send()

    def stage_dn(l):
        put3(m["tmp"], dot(m["r"][...], m["win"][l], 1, 1))

    def stage_b3(l):
        v_feed, v_mean, v_inv = rep(feed[l : l + 1]), rep(stat(l, 0)), rep(stat(l, 1))

        def normed_grad(i):
            d = (v_feed * rows(m["dmx"], i) + rows(m["tmp"], i)) * masked(i)
            m["tmp"][pl.ds(i * GROUP, GROUP)] = d
            return d, d * ((rows(m["xs"].at[l], i) - v_mean) * v_inv)

        plain, scaled = sweep(normed_grad, 2)
        slot = 1 + l
        m["msg"][slot, 0:1] = plain
        m["msg"][slot, 1:2] = scaled
        kept["sums", l] = sum_over_all(m["msg"].at[slot], "", slot)

    def stage_ty(l):
        kept["tiny", l] = tiny_sums(l, kept["glub", l], kept["feed", l])

    def stage_tm(l):
        kept["tiny", l] = tiny_middle(l, kept["tiny", l])

    def stage_te(l):
        tiny_end(l, kept["tiny", l])

    def stage_b4(l):
        sums = kept["sums", l]()
        plain, scaled = sums[0:1], sums[1:2]
        o_small[6 * l + 0 : 6 * l + 1] = scaled
        o_small[6 * l + 1 : 6 * l + 2] = plain
        inv = stat(l, 1)
        inv_count = m["stat"][15:16]
        v_scale, v_mean = rep(inv * gain[l : l + 1]), rep(stat(l, 0))
        v_plain, v_scaled = rep(plain * inv_count), rep(scaled * inv_count * inv)

        def stream_grad(i):
            lead = rows(m["tmp"], i) - masked(i) * (v_plain + (rows(m["xs"].at[l], i) - v_mean) * v_scaled)
            at = pl.ds(i * GROUP, GROUP)
            m["g"][at] = m["g"][at] + v_scale * lead

        sweep(stream_grad)
        if l == 0:
            deliver(m["g"], o_ig)

    def stage_gs(l):
        reductions["X", l].done()
        kept["share", l] = gate_share(l)

    stages = {
        "B1": stage_b1, "da": stage_da, "B2": stage_b2, "ds": stage_ds, "p1": stage_p1, "og": stage_og, "p2": stage_p2,
        "ig": stage_ig, "dn": stage_dn, "B3": stage_b3, "ty": stage_ty, "tm": stage_tm, "te": stage_te, "B4": stage_b4,
        "gs": stage_gs,
    }
    for token in " ".join(SCHEDULE).split():
        name, at = token[:-2], int(token[-2])
        if name in geo.rows:
            red = reductions[name, at]
            if token[-1] == "p":
                red.open()
            else:
                red.step(int(token[-1]))
        else:
            stages[name](at)
    for l in range(LAYERS):
        kept["share", l]()
    for red in reductions.values():
        red.done()
    for k in geo.rows:
        reductions[k, 0].settle()
    for w in out_waits:
        w()
    net.finish()


def on_device(sizes, inputs, cotangent, lengths, gain, bias, in_proj, out_proj, rate, step, freq, feed, gluw, glub, rmean, rvar):
    geo = Geometry(sizes, inputs.shape, rate.shape[-1])
    T, H, W = geo.T, geo.H, geo.W
    v = scratch_shapes(geo)
    held = sum(math.prod(shape) * jnp.dtype(kind).itemsize for shape, kind in v.values())
    hbm = pl.BlockSpec(memory_space=pl.ANY)
    vmem = pl.BlockSpec(memory_space=pltpu.VMEM)
    smem = pl.BlockSpec(memory_space=pltpu.SMEM)
    outs = [
        pltpu.VMEM((geo.seqs, T, H), F32),
        pltpu.VMEM((geo.seqs, T, H), F32),
        pltpu.VMEM((LAYERS, geo.rows["X"], WIDE), BF16),
        pltpu.VMEM((LAYERS, geo.D, geo.half_rows, WIDE), BF16),
        pltpu.VMEM((LAYERS, geo.rows["I"], WIDE), BF16),
        pltpu.VMEM((6 * LAYERS, H), F32),
        pltpu.VMEM((3 * LAYERS, geo.Pn), F32),
    ]
    act, ig, gx, gl, gi, small, lam = pl.pallas_call(
        functools.partial(body, geo, tuple(v)),
        out_shape=outs,
        in_specs=[smem, hbm, hbm, vmem, vmem, hbm, hbm, hbm, hbm, hbm, vmem, hbm, vmem, vmem, vmem],
        out_specs=[vmem] * 7,
        scratch_shapes=[pltpu.VMEM(*s) for s in v.values()]
        + [pltpu.SemaphoreType.DMA((SEMAPHORES,)), pltpu.SemaphoreType.DMA((SEMAPHORES,)), pltpu.SemaphoreType.DMA((32,))],
        compiler_params=pltpu.CompilerParams(
            collective_id=0, has_side_effects=True, vmem_limit_bytes=held + SPARE_BYTES
        ),
    )(lengths, inputs, cotangent, gain, bias, in_proj, out_proj, rate, step, freq, feed, gluw, glub, rmean, rvar)
    return finish(geo, act, ig, gx, gl, gi, small, lam)


def results(geo, *refs):
    T, H, W, Pn, L = geo.T, geo.H, geo.W, geo.Pn, LAYERS
    act, ig, gx, gl, gi, small, lam = refs[:7]
    (o_act, o_ig, o_gain, o_bias, o_in, o_out, o_rate, o_step, o_freq, o_feed, o_glu, o_glub, o_mean, o_var) = refs[7:21]
    v_in, v_out, v_glu, sems = refs[21:]
    used = [0]

    def copy(src, dst):
        sem = sems.at[used[0]]
        used[0] += 1
        c = pltpu.make_async_copy(src, dst, sem)
        c.start()
        return c

    order = list(reversed(range(L)))
    waits = [copy(act, o_act), copy(ig, o_ig)]
    for l in range(L):
        for k, o in enumerate((o_gain, o_bias, o_feed, o_glub, o_mean, o_var)):
            o[l : l + 1] = small[6 * l + k : 6 * l + k + 1]
        for k, o in enumerate((o_rate, o_step, o_freq)):
            o[l] = lam[3 * l + k : 3 * l + k + 1]
    block = 64
    half = H // 2
    for l in order:
        for n in range(H // WIDE):

            def move(i, _):
                v_out[l, pl.ds(i * block, block), n * WIDE : (n + 1) * WIDE] = gx[
                    l, pl.ds(n * W + i * block, block)
                ].astype(F32)
                return 0

            lax.fori_loop(0, W // block, move, 0)
        waits.append(copy(v_out.at[l], o_out.at[l, 0]))
        for n in range(Pn // LANES):

            def move(i, _):
                value = gi[l, pl.ds(n * H + i * block, block)].astype(F32)
                at = pl.ds(i * block, block)
                v_in[l, at, n * LANES : (n + 1) * LANES] = value[:, :LANES]
                v_in[l, at, Pn + n * LANES : Pn + (n + 1) * LANES] = value[:, LANES:]
                return 0

            lax.fori_loop(0, H // block, move, 0)
        waits.append(copy(v_in.at[l], o_in.at[l, 0]))
        for d in range(geo.D):
            for n in range(H // WIDE):

                def move(i, _):
                    value = gl[l, d, pl.ds(n * half + i * block, block)].astype(F32)
                    v_glu[l, pl.ds(d * half + i * block, block), n * WIDE : (n + 1) * WIDE] = value
                    return 0

                lax.fori_loop(0, half // block, move, 0)
        waits.append(copy(v_glu.at[l], o_glu.at[l]))
    for c in waits:
        c.wait()


def finish(geo, act, ig, gx, gl, gi, small, lam):
    T, H, W, Pn, L = geo.T, geo.H, geo.W, geo.Pn, LAYERS
    hbm = pl.BlockSpec(memory_space=pl.ANY)
    vmem = pl.BlockSpec(memory_space=pltpu.VMEM)
    row = jax.ShapeDtypeStruct((L, H), F32)
    lam_row = jax.ShapeDtypeStruct((L, 1, Pn), F32)
    stream = jax.ShapeDtypeStruct((geo.seqs, T, H), F32)
    outs = [
        stream,
        stream,
        row,
        row,
        jax.ShapeDtypeStruct((L, 1, H, W), F32),
        jax.ShapeDtypeStruct((L, 1, W, H), F32),
        lam_row,
        lam_row,
        lam_row,
        row,
        jax.ShapeDtypeStruct((L, H, H), F32),
        row,
        row,
        row,
    ]
    where = [hbm, hbm, vmem, vmem, hbm, hbm, vmem, vmem, vmem, vmem, hbm, vmem, vmem, vmem]
    return pl.pallas_call(
        functools.partial(results, geo),
        out_shape=outs,
        in_specs=[vmem] * 7,
        out_specs=where,
        scratch_shapes=[
            pltpu.VMEM((L, H, W), F32),
            pltpu.VMEM((L, W, H), F32),
            pltpu.VMEM((L, H, H), F32),
            pltpu.SemaphoreType.DMA((16,)),
        ],
        compiler_params=pltpu.CompilerParams(vmem_limit_bytes=16 << 20),
    )(act, ig, gx, gl, gi, small, lam)


def solution(mesh):
    tokens = P("batch", "seq", None)
    per_dir = P(None, "dir", None)
    mats = P(None, "dir", None, None)
    in_specs = (tokens, tokens, P("batch"), P(), P(), mats, mats, per_dir, per_dir, per_dir) + (P(),) * 5
    out_specs = (tokens, tokens, P(), P(), mats, mats, per_dir, per_dir, per_dir) + (P(),) * 5
    return jax.shard_map(
        functools.partial(on_device, dict(mesh.shape)),
        mesh=mesh,
        in_specs=in_specs,
        out_specs=out_specs,
        check_vma=False,
    )
```

```python
import functools
import math

import jax
import jax.numpy as jnp
from jax import lax
from jax.experimental import pallas as pl
from jax.experimental.pallas import tpu as pltpu
from jax.sharding import PartitionSpec as P

LAYERS = 2
EPSILON = 1e-05
MOMENTUM = 0.9
F32 = jnp.float32
BF16 = jnp.bfloat16
AXES = ("dir", "seq", "batch")
MESH = pl.DeviceIdType.MESH
LANES = 128
CHUNKS = 8
WIDE = 256
SPARE_BYTES = 5 << 19
SEMAPHORES = 144
SHARES = {"X": ((2, "xy"), (2, "yx"), (2, "xy"), (2, "yx")), "I": ((3, "xy"), (3, "yx"))}
STAGES = B1, DA, B2, DS, P1, OG, P2, IG, DN, B3, TY, TP, TM, TE, B4, GS = tuple(range(16))
SUMS = X0, X1, I0, I1 = tuple(range(16, 20))
OPEN = -1
SCHEDULE = (
    (B1, 1), (DA, 1), (B2, 1), (OG, 1), (DS, 1), (P1, 1), (X1, OPEN), (X1, 2),
    (X1, 1), (P2, 1), (DN, 1), (B3, 1), (X1, 2), (X1, 3), (X1, 0), (IG, 1),
    (TY, 1), (X1, 1), (I1, OPEN), (I1, 0), (I1, 1), (X1, 2), (X1, 0), (B4, 1),
    (B1, 0), (DA, 0), (X1, 1), (B2, 0), (X1, 3), (DS, 0), (X1, 2), (P1, 0),
    (OG, 0), (X1, 1), (I1, 1), (I1, 0), (X1, 2), (X1, 3), (X1, 0), (X0, OPEN),
    (X0, 2), (TP, 1), (P2, 0), (I1, 0), (X0, 1), (IG, 0), (X0, 0), (X1, 3),
    (X1, 0), (I1, 1), (X0, 3), (I0, OPEN), (I0, 0), (X0, 2), (X1, 1), (TY, 0),
    (X0, 0), (TM, 1), (X0, 1), (I0, 1), (I1, 0), (DN, 0), (X1, 2), (TP, 0),
    (X0, 2), (X0, 0), (X0, 3), (I1, 0), (I1, 1), (X0, 0), (I0, 0), (X1, 0),
    (X1, 3), (X0, 1), (I1, 1), (X0, 3), (B3, 0), (X0, 2), (X1, 3), (I0, 1),
    (TM, 0), (X1, 0), (I0, 0), (I1, 1), (I1, 0), (X0, 3), (X1, 2), (I0, 1),
    (X0, 2), (X0, 1), (X0, 0), (X0, 3), (TE, 1), (X1, 3), (X1, 1), (I0, 0),
    (X0, 1), (I0, 1), (X0, 2), (X0, 3), (I1, 0), (TE, 0), (I0, 0), (X0, 1),
    (I0, 1), (X1, 0), (X0, 0), (I0, 0), (X1, 1), (I0, 1), (I1, 1), (X0, 3),
    (B4, 0), (GS, 1), (X0, 0), (X0, 2), (X0, 1), (GS, 0), (I0, 0), (I0, 1),
)


def transition(rate_vec, step_vec, freq_vec):
    half_a = 0.5 * step_vec * rate_vec
    half_c = 0.5 * step_vec * freq_vec
    denominator = (1.0 + half_a) * (1.0 + half_a) + half_c * half_c
    lam_re = (1.0 - half_a * half_a - half_c * half_c) / denominator
    lam_im = 2.0 * half_c / denominator
    kap_re = step_vec * (1.0 + half_a) / denominator
    kap_im = step_vec * half_c / denominator
    return (lam_re, lam_im, kap_re, kap_im)


def dot(a, b, ca, cb):
    return lax.dot_general(a, b, (((ca,), (cb,)), ((), ())), preferred_element_type=F32)


def cmul(a, b):
    return (a[0] * b[0] - a[1] * b[1], a[0] * b[1] + a[1] * b[0])


def conj(a):
    return (a[0], -a[1])


def widen(mask):
    return jnp.concatenate([mask] * 4, axis=-1)


class Geometry:
    def __init__(self, sizes, local_shape, states):
        self.D, self.S, self.B = (sizes[a] for a in AXES)
        self.sizes = dict(sizes)
        self.seqs, self.T, self.H = local_shape
        self.Pn = states
        self.W = 2 * states
        self.J = self.T // CHUNKS
        self.N = self.D * self.S * self.B
        self.unit = 16 * self.S * self.B
        up = lambda n: -(-n // self.unit) * self.unit
        self.out_rows = (self.H // WIDE) * self.W
        self.half_rows = (self.H // WIDE) * (self.H // 2)
        self.in_rows = (self.Pn // LANES) * self.H
        self.used = {"X": self.out_rows + self.half_rows, "I": self.in_rows}
        self.rows = {k: up(v) for k, v in self.used.items()}
        bits = tuple(("batch", k) for k in range((self.B - 1).bit_length()))
        seq = (("seq", None),)
        ways = {"xy": bits + seq, "yx": bits[::-1] + seq, "zx": seq + bits, "zy": seq + bits[::-1]}
        self.colors = {}
        for k, n in self.rows.items():
            shares = SHARES[k]
            if n // self.unit != sum(count for count, _ in shares):
                shares = ((n // self.unit, "xy"),)
            at, self.colors[k] = 0, []
            for count, name in shares:
                self.colors[k].append((at, count * self.unit, ways[name]))
                at += count * self.unit
        self.direct = self.N <= 64

    def ways(self, dim):
        return self.S if dim[1] is None else 2


class Net:
    def __init__(self, geo, send_sems, recv_sems):
        self.geo, self.send_sems, self.recv_sems = geo, send_sems, recv_sems
        self.used_send = 0
        self.used_recv = 0
        self.at = {a: lax.axis_index(a) for a in AXES}
        self.unsent = []

    def send_sem(self):
        self.used_send += 1
        return self.send_sems.at[self.used_send - 1]

    def recv_sem(self):
        self.used_recv += 1
        return self.recv_sems.at[self.used_recv - 1]

    def index(self, axes):
        lin = 0
        for a in axes:
            lin = lin * self.geo.sizes[a] + self.at[a]
        return lin

    def count(self, axes):
        n = 1
        for a in axes:
            n *= self.geo.sizes[a]
        return n

    def peers(self, axes, act):
        n = self.count(axes)

        def at_offset(k):
            where, lin, rest, coords = {}, 0, k, []
            for a in reversed(axes):
                size = self.geo.sizes[a]
                off = rest % size
                rest = rest // size
                coords.append((a, lax.rem(self.at[a] + off, size)))
            for a, c in reversed(coords):
                where[a] = c
                lin = lin * self.geo.sizes[a] + c
            act(where, lin, k)

        if n <= 64:
            for k in range(n - 1, 0, -1):
                at_offset(k)
        else:

            def body(k, _):
                at_offset(k)
                return 0

            lax.fori_loop(1, n, body, 0)

    def place(self, dim):
        axis, bit = dim
        return self.at[axis] if bit is None else lax.rem(lax.div(self.at[axis], 1 << bit), 2)

    def others(self, dim, act):
        axis, bit = dim
        if bit is None:
            self.peers((axis,), act)
        else:
            mine = self.place(dim)
            act({axis: self.at[axis] + (1 - 2 * mine) * (1 << bit)}, 1 - mine, 1)

    def put(self, src, dst, send, recv, peer):
        pltpu.make_async_remote_copy(
            src_ref=src, dst_ref=dst, send_sem=send, recv_sem=recv, device_id=peer, device_id_type=MESH
        ).start()

    def wait(self, ref, sem):
        pltpu.make_async_copy(ref, ref, sem).wait()

    def gather(self, src, land, axes):
        n = self.count(axes)
        send, recv = self.send_sem(), self.recv_sem()
        slot = self.index(axes)
        self.peers(axes, lambda peer, lin, k: self.put(src, land.at[slot], send, recv, peer))
        land[slot] = src[...]
        size = land.at[pl.ds(0, n - 1)]
        self.unsent.append((size, send))
        return functools.partial(self.wait, size, recv)

    def swap(self, pieces):
        peer = {"dir": 1 - self.at["dir"]}
        waits = []
        for src, dst, size in pieces:
            send, recv = self.send_sem(), self.recv_sem()
            self.put(src, dst, send, recv, peer)
            self.unsent.append((size, send))
            waits.append(functools.partial(self.wait, size, recv))
        return waits

    def finish(self):
        for size, send in self.unsent:
            self.wait(size, send)


def scratch_shapes(geo):
    T, H, W, J, S, N, Pn = geo.T, geo.H, geo.W, geo.J, geo.S, geo.N, geo.Pn
    L, D = LAYERS, geo.D
    v = {
        "mask": ((J, CHUNKS, LANES), F32),
        "win": ((L, H, D * W), BF16),
        "wout": ((L, D * W, H), BF16),
        "glw": ((L, H, H), BF16),
        "prm": ((3, D, L, 1, Pn), F32),
        "tab": ((L, D, 16, CHUNKS, Pn), F32),
        "xs": ((L + 1, J, CHUNKS, H), F32),
        "stat": ((16, H), F32),
        "nrm": ((L, T, H), BF16),
        "u": ((L, T, D * W), F32),
        "st": ((L, T + 32, D * W), BF16),
        "act": ((L, T, H), BF16),
        "sig": ((L, J, CHUNKS, H), BF16),
        "dge": ((L, J, CHUNKS, H), BF16),
        "tmp": ((J, CHUNKS, H), F32),
        "g": ((J, CHUNKS, H), F32),
        "dmx": ((J, CHUNKS, H), F32),
        "dml": ((T, H), BF16),
        "dgt": ((T, H), BF16),
        "ds": ((T, D * W), F32),
        "r": ((T, D * W), BF16),
        "msg0": ((2, H + LANES), F32),
        "msg": ((3, 2, H), F32),
        "smsg": ((2 * L, 1, D * W), F32),
        "sland": ((2 * L, S, 1, D * W), F32),
        "tiny": ((L, D, 1, 2 * H + 2 * W), F32),
        "tpair": ((L, 1, 2 * H + 2 * W), F32),
        "tnear": ((L, 1, 2 * H + 2 * W), F32),
        "tland1": ((L, geo.B, 1, 2 * H + 2 * W), F32),
        "tmid": ((L, 1, 2 * H + 2 * W), F32),
        "tland2": ((L, S, 1, 2 * H + 2 * W), F32),
        "tsum": ((L, 1, 2 * H + 2 * W), F32),
    }
    for k, lead, wide in (("0", (), H + LANES), ("", (3,), H)):
        if geo.direct:
            v["land" + k] = ((*lead, N, 2, wide), F32)
        else:
            v["near" + k] = ((*lead, D * geo.B, 2, wide), F32)
            v["mid" + k] = ((*lead, 2, wide), F32)
            v["far" + k] = ((*lead, S, 2, wide), F32)
    for k, rows in geo.rows.items():
        v["g" + k] = ((D, rows, WIDE), BF16)
        v["p" + k] = ((L, rows, WIDE), BF16)
        for c, (_, n, order) in enumerate(geo.colors[k]):
            for i, dim in enumerate(order):
                ways = geo.ways(dim)
                n //= ways
                v[f"land{i}{k}{c}"] = ((L, ways - 1, n, WIDE), BF16)
                if i == 0:
                    v[f"red{k}{c}"] = ((L, n, WIDE), BF16)
    return v


class Reduction:
    def __init__(self, geo, net, kind, layer, m):
        self.geo, self.net, self.kind, self.layer, self.m = geo, net, kind, layer, m
        self.rows = geo.rows[kind]
        self.colors = geo.colors[kind]
        self.full = m["f" + kind].at[layer]
        self.mine = m["g" + kind].at[net.at["dir"]]
        self.flows = None

    def pair_send(self):
        landing = self.m["p" + self.kind].at[self.layer]
        other = self.m["g" + self.kind].at[1 - self.net.at["dir"]]
        (self.pair_wait,) = self.net.swap([(other, landing, landing)])
        self.held = [self.net.unsent.pop()]

    def settle(self):
        for size, send in self.held:
            self.net.wait(size, send)

    def pair_done(self):
        self.pair_wait()
        landing = self.m["p" + self.kind].at[self.layer]
        block = 64

        def body(i, _):
            at = pl.ds(i * block, block)
            self.mine[at] = self.mine[at] + landing[at]
            return 0

        lax.fori_loop(0, self.rows // block, body, 0)

    def scatter(self, dim, src, base, part, land):
        net = self.net
        send, recv = net.send_sem(), net.recv_sem()
        net.others(
            dim,
            lambda peer, lin, k: net.put(
                src.at[pl.ds(base + lin * part, part)], land.at[k - 1], send, recv, peer
            ),
        )
        net.unsent.append((land, send))
        return functools.partial(net.wait, land, recv)

    def add(self, own, own_at, land, n, out, out_at, part):
        block = next(b for b in (64, 48, 32, 16) if part % b == 0)

        def body(i, _):
            if n == 2:
                out[pl.ds(out_at + i * block, block)] = (
                    own[pl.ds(own_at + i * block, block)] + land[0, pl.ds(i * block, block)]
                )
                return 0
            total = own[pl.ds(own_at + i * block, block)].astype(F32)
            for k in range(min(n - 1, 7)):
                total = total + land[k, pl.ds(i * block, block)].astype(F32)
            if n - 1 > 7:
                total = lax.fori_loop(
                    7, n - 1, lambda k, t: t + land[k, pl.ds(i * block, block)].astype(F32), total
                )
            out[pl.ds(out_at + i * block, block)] = total.astype(BF16)
            return 0

        lax.fori_loop(0, part // block, body, 0)

    def spread(self, dim, base, part):
        net, n = self.net, self.geo.ways(dim)
        send, recv = net.send_sem(), net.recv_sem()
        mine = self.full.at[pl.ds(base, part)]
        net.others(dim, lambda peer, lin, k: net.put(mine, mine, send, recv, peer))
        size = self.full.at[pl.ds(0, (n - 1) * part)]
        net.unsent.append((size, send))
        return functools.partial(net.wait, size, recv)

    def flow(self, c):
        base, size, order = self.colors[c]
        red = self.m[f"red{self.kind}{c}"].at[self.layer]
        src, src_at, at = self.mine, base, base
        owned = []
        for i, dim in enumerate(order):
            n = self.geo.ways(dim)
            part = size // n
            land = self.m[f"land{i}{self.kind}{c}"].at[self.layer]
            wait = self.scatter(dim, src, src_at, part, land)
            if i == 0:
                self.held.append(self.net.unsent.pop())
            yield
            wait()
            mine = self.net.place(dim)
            own_at, at = src_at + mine * part, at + mine * part
            if i + 1 == len(order):
                out, out_at = self.full, at
            else:
                out, out_at = red, 0 if i == 0 else own_at
            self.add(src, own_at, land, n, out, out_at, part)
            src, src_at, size = red, out_at, part
            owned.append((dim, at, part))
        for dim, at, part in reversed(owned):
            wait = self.spread(dim, at, part)
            yield
            wait()

    def open(self):
        self.pair_done()
        self.flows = [self.flow(c) for c in range(len(self.colors))]

    def step(self, c):
        if c < len(self.flows):
            next(self.flows[c], None)

    def done(self):
        for flow in self.flows:
            for _ in flow:
                pass


def body(geo, names, *refs):
    T, H, W, J, S, N, Pn = geo.T, geo.H, geo.W, geo.J, geo.S, geo.N, geo.Pn
    (lengths, inputs, cotangent, gain, bias, in_proj, out_proj, rate, step, freq, feed, gluw, glub, rmean, rvar) = refs[:15]
    (o_act, o_ig, o_gx, o_gl, o_gi, o_small, o_lam) = refs[15:22]
    scr = refs[22:]
    m = dict(zip(names, scr))
    m["fX"], m["fI"], m["glf"] = o_gx, o_gi, o_gl
    m["xin"], m["cin"], m["pm"] = m["dgt"], m["dml"], m["r"].at[:, 0:T]
    send_sems, recv_sems, local_sems = scr[len(names) :]
    net = Net(geo, send_sems, recv_sems)
    me_d, me_s = net.at["dir"], net.at["seq"]
    local = [0]

    def fetch(src, dst):
        sem = local_sems.at[local[0]]
        local[0] += 1
        copy = pltpu.make_async_copy(src, dst, sem)
        copy.start()
        return copy.wait

    def sum_over_all(msg, which, slot=None):
        at = lambda name: m[name + which] if slot is None else m[name + which].at[slot]
        if geo.direct:
            arrived = net.gather(msg, at("land"), AXES)

            def total():
                arrived()
                return jnp.sum(at("land")[...], axis=0)

            return total
        arrived = net.gather(msg, at("near"), ("dir", "batch"))

        def total():
            arrived()
            at("mid")[...] = jnp.sum(at("near")[...], axis=0)
            net.gather(at("mid"), at("far"), ("seq",))()
            return jnp.sum(at("far")[...], axis=0)

        return total

    barrier = pltpu.get_barrier_semaphore()
    net.peers(AXES, lambda peer, lin, k: pl.semaphore_signal(barrier, 1, device_id=peer, device_id_type=MESH))
    w_x = fetch(inputs.at[me_d], m["xin"])
    w_c = fetch(cotangent.at[me_d], m["cin"])
    raw = (rate, step, freq)
    w_p = [fetch(raw[i], m["prm"].at[i, me_d]) for i in range(3)]
    cols = pl.ds(pl.multiple_of(me_d * W, LANES), W)
    rows_of = pl.ds(pl.multiple_of(me_d * W, 16), W)
    in_at = [m["win"].at[l, :, cols] for l in range(LAYERS)]
    out_at = [m["wout"].at[l, rows_of] for l in range(LAYERS)]
    w_in = [fetch(in_proj.at[l, 0], in_at[l]) for l in range(LAYERS)]
    w_out = [fetch(out_proj.at[l, 0], out_at[l]) for l in range(LAYERS)]
    w_g = fetch(gluw, m["glw"])

    length = lengths[me_d]
    shape = (J, CHUNKS, LANES)
    position = (
        me_s * T
        + lax.broadcasted_iota(jnp.int32, shape, 1) * J
        + lax.broadcasted_iota(jnp.int32, shape, 0)
    )
    m["mask"][...] = jnp.where(position < length, 1.0, 0.0).astype(F32)

    def permutation(i, _):
        at = pl.ds(i * 64, 64)
        row = i * 64 + lax.broadcasted_iota(jnp.int32, (64, T), 0)
        col = lax.broadcasted_iota(jnp.int32, (64, T), 1)
        wanted = lax.rem(row, CHUNKS) * J + lax.div(row, CHUNKS)
        m["pm"][at] = jnp.where(col == wanted, 1.0, 0.0).astype(BF16)
        return 0

    lax.fori_loop(0, T // 64, permutation, 0)

    def put3(ref3, value):
        ref3[...] = value.reshape(J, CHUNKS, H)

    def reorder(src, dst):
        put3(dst, dot(m["pm"][...], src[...], 1, 0))

    GROUP = 4
    ROWS = GROUP * CHUNKS

    def rows(ref, i):
        return ref[pl.ds(i * GROUP, GROUP)].astype(F32)

    def flat(ref, i):
        return ref[pl.ds(i * ROWS, ROWS)].astype(F32).reshape(GROUP, CHUNKS, -1)

    def put_flat(ref, i, value):
        ref[pl.ds(i * ROWS, ROWS)] = value.reshape(ROWS, -1).astype(BF16)

    def sweep(act, sums=0):
        zero = tuple(jnp.zeros((CHUNKS, H), F32) for _ in range(sums))

        def one(i, acc):
            more = act(i)
            if not sums:
                return acc
            return tuple(a + jnp.sum(v, axis=0) for a, v in zip(acc, more))

        acc = lax.fori_loop(0, T // ROWS, one, zero)
        return tuple(jnp.sum(a, axis=0, keepdims=True) for a in acc)

    def rep(row):
        return jnp.broadcast_to(row, (CHUNKS, row.shape[-1]))

    masked = lambda i: widen(rows(m["mask"], i))

    w_x()
    reorder(m["xin"], m["xs"].at[0])

    def first(i):
        x = rows(m["xs"].at[0], i)
        xm = x * masked(i)
        return xm, xm * x

    s1, s2 = sweep(first, 2)
    here = jnp.sum(jnp.sum(m["mask"][...], axis=0), axis=0, keepdims=True)
    m["msg0"][0:1, 0:H] = s1
    m["msg0"][1:2, 0:H] = s2
    m["msg0"][:, H:] = jnp.broadcast_to(here, (2, LANES))

    pl.semaphore_wait(barrier, N - 1)
    stats = sum_over_all(m["msg0"], "0")
    send_in, send_out = [None] * LAYERS, [None] * LAYERS
    prm_waits = net.swap([(raw[i], m["prm"].at[i, me_d], m["prm"].at[i, me_d]) for i in range(3)])
    for l in range(LAYERS):
        (send_in[l],) = net.swap([(in_proj.at[l, 0], in_at[l], in_at[l])])
        (send_out[l],) = net.swap([(out_proj.at[l, 0], out_at[l], out_at[l])])

    for w in w_p + prm_waits:
        w()
    for l in range(LAYERS):
        for dd in range(geo.D):
            lr, li, kr, ki = transition(*(m["prm"][i, dd, l] for i in range(3)))
            power = (lr, li)
            for _ in range((J).bit_length() - 1):
                power = cmul(power, power)
            ladder = [power]
            for _ in range(3):
                ladder.append(cmul(ladder[-1], ladder[-1]))
            wide = [tuple(rep(v) for v in p) for p in ladder]
            chunk = lax.broadcasted_iota(jnp.int32, (CHUNKS, Pn), 0)
            one = (jnp.ones((CHUNKS, Pn), F32), jnp.zeros((CHUNKS, Pn), F32))
            up, down = one, one
            for k in range(3):
                bit = lax.rem(lax.div(chunk, 1 << k), 2)
                grown = cmul(up, wide[k])
                up = tuple(jnp.where(bit == 1, a, b) for a, b in zip(grown, up))
                grown = cmul(down, wide[k])
                down = tuple(jnp.where(bit == 0, a, b) for a, b in zip(grown, down))
            table = [rep(lr), rep(li), *up, *down]
            for p in wide:
                table.extend(p)
            table.extend([rep(kr), rep(ki)])
            for k, v in enumerate(table):
                m["tab"][l, dd, k] = v

    def entry(l, dd, k, minus):
        re, im = m["tab"][l, dd, 2 * k], m["tab"][l, dd, 2 * k + 1]
        return (re, -im) if minus else (re, im)

    def fold(l):
        for dd in range(geo.D):
            kr, ki = m["tab"][l, dd, 14][0:1], m["tab"][l, dd, 15][0:1]

            def some(i, _):
                at = pl.ds(i * 32, 32)
                w = m["win"][l, at, dd * W : (dd + 1) * W].astype(F32)
                re, im = w[:, :Pn], w[:, Pn:]
                new = jnp.concatenate([kr * re - ki * im, kr * im + ki * re], axis=1)
                m["win"][l, at, dd * W : (dd + 1) * W] = new.astype(BF16)
                return 0

            lax.fori_loop(0, H // 32, some, 0)

    for l in range(LAYERS):
        w_in[l]()
        send_in[l]()
        fold(l)
        w_out[l]()
        send_out[l]()
    w_c()
    reorder(m["cin"], m["g"])
    w_g()

    def split(block):
        return block[:, :Pn], block[:, Pn:]

    def advance(lam, h, d):
        return (lam[0] * h[0] - lam[1] * h[1] + d[0], lam[0] * h[1] + lam[1] * h[0] + d[1])

    def scan(l, up_dd, src, minus, start, emit):
        dn_dd = 1 - up_dd
        lam_up, lam_dn = entry(l, up_dd, 0, minus), entry(l, dn_dd, 0, minus)
        n = T // 16

        def two(i, carry):
            hu, hd = carry[:2], carry[2:]
            at_u, at_d = i * 16, (n - 1 - i) * 16
            bu = src[pl.ds(at_u, 16), up_dd * W : (up_dd + 1) * W]
            bd = src[pl.ds(at_d, 16), dn_dd * W : (dn_dd + 1) * W]
            keep_u, keep_d = [], []
            for k in range(2):
                hu = advance(lam_up, hu, split(bu[8 * k : 8 * k + 8]))
                hd = advance(lam_dn, hd, split(bd[8 - 8 * k : 16 - 8 * k]))
                keep_u.append(jnp.concatenate(hu, axis=1))
                keep_d.append(jnp.concatenate(hd, axis=1))
            if emit is not None:
                emit(up_dd, at_u, jnp.concatenate(keep_u, axis=0).astype(BF16))
                emit(dn_dd, at_d, jnp.concatenate(keep_d[::-1], axis=0).astype(BF16))
            return (*hu, *hd)

        out = lax.fori_loop(0, n, two, start, unroll=2)
        return out[:2], out[2:]

    chunk_at = lax.broadcasted_iota(jnp.int32, (CHUNKS, Pn), 0)

    def within(l, dd, ends, rising, minus):
        shift = (lambda v, k: pltpu.roll(v, k, 0)) if rising else (lambda v, k: pltpu.roll(v, CHUNKS - k, 0))
        inside = (lambda k: chunk_at >= k) if rising else (lambda k: chunk_at < CHUNKS - k)
        a = tuple(jnp.where(inside(1), shift(v, 1), 0.0) for v in ends)
        for k in range(3):
            far = tuple(jnp.where(inside(1 << k), shift(v, 1 << k), 0.0) for v in a)
            more = cmul(entry(l, dd, 3 + k, minus), far)
            a = (a[0] + more[0], a[1] + more[1])
        return a

    def carries(k, l, up_dd, ends_up, ends_dn, minus):
        dn_dd = 1 - up_dd
        pieces = [None] * geo.D
        for dd, ends, which in ((up_dd, ends_up, 2), (dn_dd, ends_dn, 1)):
            total = cmul(entry(l, dd, which, minus), ends)
            pieces[dd] = jnp.concatenate([jnp.sum(v, axis=0, keepdims=True) for v in total], axis=1)
        m["smsg"][k] = jnp.concatenate(pieces, axis=1)
        land = m["sland"].at[k]
        arrived = net.gather(m["smsg"].at[k], land, ("seq",))
        here_up = within(l, up_dd, ends_up, True, minus)
        here_dn = within(l, dn_dd, ends_dn, False, minus)
        def finish_up():
            arrived()
            def enter(dd, rising):
                whole = tuple(v[0:1] for v in entry(l, dd, 6, minus))
                zero = jnp.zeros((1, Pn), F32)

                def lap(i, state):
                    at = i if rising else S - 1 - i
                    piece = land[at][:, dd * W : (dd + 1) * W]
                    new = advance(whole, state, split(piece))
                    reached = (at < me_s) if rising else (at > me_s)
                    return tuple(jnp.where(reached, a, b) for a, b in zip(new, state))

                state = (zero, zero)
                if S <= 8:
                    for i in range(S):
                        state = lap(i, state)
                    return state
                return lax.fori_loop(0, S, lap, state)

            outs = []
            for dd, rising, here_ends, which in ((up_dd, True, here_up, 1), (dn_dd, False, here_dn, 2)):
                far = cmul(entry(l, dd, which, minus), tuple(rep(v) for v in enter(dd, rising)))
                outs.append((here_ends[0] + far[0], here_ends[1] + far[1]))
            return outs

        return finish_up

    zeros4 = tuple(jnp.zeros((CHUNKS, Pn), F32) for _ in range(4))

    def stat(l, k):
        return m["stat"][4 * l + k : 4 * l + k + 1]

    def set_stat(l, k, value):
        m["stat"][4 * l + k : 4 * l + k + 1] = value

    c0 = 0.7978845608028654
    c1 = 0.044715
    for l in range(LAYERS):
        sums = stats()
        if l == 0:
            m["stat"][15:16] = 1.0 / widen(sums[0:1, H:])
            sums = sums[:, :H]
        inv_count = m["stat"][15:16]
        mean = sums[0:1] * inv_count
        var = sums[1:2] * inv_count - mean * mean
        inv = lax.rsqrt(var + EPSILON)
        set_stat(l, 0, mean)
        set_stat(l, 1, inv)
        o_small[6 * l + 4 : 6 * l + 5] = MOMENTUM * rmean[l : l + 1] + (1.0 - MOMENTUM) * mean
        o_small[6 * l + 5 : 6 * l + 6] = MOMENTUM * rvar[l : l + 1] + (1.0 - MOMENTUM) * var
        v_mean, v_scale, v_bias = rep(mean), rep(inv * gain[l : l + 1]), rep(bias[l : l + 1])

        def normalise(i):
            x = rows(m["xs"].at[l], i)
            put_flat(m["nrm"].at[l], i, ((x - v_mean) * v_scale + v_bias) * masked(i))

        sweep(normalise)
        m["u"][l] = dot(m["nrm"][l], m["win"][l], 1, 0)
        ends_up, ends_dn = scan(l, 0, m["u"].at[l], False, zeros4, None)
        in_up, in_dn = carries(l, l, 0, ends_up, ends_dn, False)()
        both = lambda v: jnp.concatenate([jnp.concatenate(v, axis=1)] * 2, axis=0).astype(BF16)
        m["st"][l, 0:16, 0:W] = both(in_up)
        m["st"][l, T + 16 : T + 32, W:] = both(in_dn)

        def save(dd, at, value):
            m["st"][l, pl.ds(16 + at, 16), dd * W : (dd + 1) * W] = value

        scan(l, 0, m["u"].at[l], False, (*in_up, *in_dn), save)

        put3(m["tmp"], dot(m["st"][l, 16 : T + 16], m["wout"][l], 1, 0))
        v_feed = rep(feed[l : l + 1])

        def activate(i):
            v = rows(m["tmp"], i) + v_feed * flat(m["nrm"].at[l], i)
            sq = v * v
            t = jnp.tanh(c0 * v * (1.0 + c1 * sq))
            half = 0.5 * (1.0 + t)
            put_flat(m["act"].at[l], i, v * half)
            slope = half + 0.5 * v * (1.0 - t * t) * (c0 * (1.0 + 3.0 * c1 * sq))
            m["dge"][l, pl.ds(i * GROUP, GROUP)] = slope.astype(BF16)

        sweep(activate)
        put3(m["tmp"], dot(m["act"][l], m["glw"][l], 1, 0))
        v_glub = rep(glub[l : l + 1])

        def gate(i):
            sig = 0.5 + 0.5 * jnp.tanh(0.5 * (rows(m["tmp"], i) + v_glub))
            m["sig"][l, pl.ds(i * GROUP, GROUP)] = sig.astype(BF16)
            mk = masked(i)
            x = rows(m["xs"].at[l], i) + mk * flat(m["act"].at[l], i) * sig
            m["xs"][l + 1, pl.ds(i * GROUP, GROUP)] = x
            if l + 1 < LAYERS:
                xm = x * mk
                return xm, xm * x

        sums = sweep(gate, 2 if l + 1 < LAYERS else 0)
        if l + 1 < LAYERS:
            m["msg"][0, 0:1] = sums[0]
            m["msg"][0, 1:2] = sums[1]
            stats = sum_over_all(m["msg"].at[0], "", 0)

    out_waits = []

    def deliver(src, dst):
        send, recv = net.send_sem(), net.recv_sem()
        sem = local_sems.at[local[0]]
        local[0] += 1
        for c in range(CHUNKS):
            to = dst.at[me_d, pl.ds(c * J, J)]
            net.put(src.at[:, c], to, send, recv, {"dir": 1 - me_d})
            pltpu.make_async_copy(src.at[:, c], to, sem).start()
        net.unsent.append((dst.at[me_d], send))
        out_waits.append(functools.partial(net.wait, dst.at[1 - me_d], recv))
        out_waits.append(functools.partial(net.wait, dst.at[me_d], sem))

    deliver(m["xs"].at[LAYERS], o_act)

    reductions = {(k, l): Reduction(geo, net, k, l, m) for k in geo.rows for l in range(LAYERS)}

    def clear_rest(kind, l):
        used, rows_all = geo.used[kind], geo.rows[kind]
        if used < rows_all:
            for dd in range(geo.D):
                m["g" + kind][dd, used:rows_all] = jnp.zeros((rows_all - used, WIDE), BF16)

    def out_grads(l):
        if l + 1 < LAYERS:
            reductions["X", l + 1].settle()
        clear_rest("X", l)
        value = dot(m["st"][l, 16 : T + 16], m["dml"][...], 0, 0).astype(BF16)
        gates = dot(m["act"][l], m["dgt"][...], 0, 0).astype(BF16)
        half = H // 2
        for dd in range(geo.D):
            for i in range(H // WIDE):
                across = slice(i * WIDE, (i + 1) * WIDE)
                m["gX"][dd, i * W : (i + 1) * W] = value[dd * W : (dd + 1) * W, across]
                at = geo.out_rows + i * half
                m["gX"][dd, at : at + half] = gates[dd * half : (dd + 1) * half, across]

    def in_grads(l):
        if l + 1 < LAYERS:
            reductions["I", l + 1].settle()
        clear_rest("I", l)
        value = dot(m["nrm"][l], m["r"][...], 0, 0)
        for dd in range(geo.D):
            for i in range(Pn // LANES):
                across = slice(i * LANES, (i + 1) * LANES)
                kr, ki = m["tab"][l, dd, 14, 0:1, across], m["tab"][l, dd, 15, 0:1, across]
                at = dd * W + i * LANES
                re, im = value[:, at : at + LANES], value[:, at + Pn : at + Pn + LANES]
                new = jnp.concatenate([kr * re + ki * im, kr * im - ki * re], axis=1)
                m["gI"][dd, i * H : (i + 1) * H] = new.astype(BF16)

    def tiny_sums(l, d_glub, d_feed):
        for dd in range(geo.D):
            m["tiny"][l, dd, :, 0:H] = d_glub
            m["tiny"][l, dd, :, H : 2 * H] = d_feed

            def some(i, acc):
                at = i * 16
                across = slice(dd * W, (dd + 1) * W)
                rr, ri = split(m["r"][pl.ds(at, 16), across].astype(F32))
                ur, ui = split(m["u"][l, pl.ds(at, 16), across])
                cur = m["st"][l, pl.ds(at + 16, 16), across].astype(F32)
                if dd == 0:
                    near = m["st"][l, pl.ds(at, 16), across].astype(F32)
                    prev = jnp.concatenate([near[8:], cur[:8]], axis=0)
                else:
                    near = m["st"][l, pl.ds(at + 32, 16), across].astype(F32)
                    prev = jnp.concatenate([cur[8:], near[:8]], axis=0)
                hr, hi = split(prev)
                new = (rr * hr + ri * hi, ri * hr - rr * hi, rr * ur + ri * ui, ri * ur - rr * ui)
                return tuple(a + v[:8] + v[8:] for a, v in zip(acc, new))

            acc = lax.fori_loop(0, T // 16, some, zeros4, unroll=2)
            for k, v in enumerate(acc):
                at = 2 * H + k * Pn
                m["tiny"][l, dd, :, at : at + Pn] = jnp.sum(v, axis=0, keepdims=True)
        landing = m["tpair"].at[l]
        (wait,) = net.swap([(m["tiny"].at[l, 1 - me_d], landing, landing)])
        return wait

    def tiny_near(l, wait):
        wait()
        m["tnear"][l] = m["tiny"][l, me_d] + m["tpair"][l]
        return net.gather(m["tnear"].at[l], m["tland1"].at[l], ("batch",))

    def tiny_middle(l, wait):
        wait()
        m["tmid"][l] = jnp.sum(m["tland1"][l], axis=0)
        return net.gather(m["tmid"].at[l], m["tland2"].at[l], ("seq",))

    def tiny_end(l, wait):
        wait()
        m["tsum"][l] = jnp.sum(m["tland2"][l], axis=0)
        o_small[6 * l + 2 : 6 * l + 3] = m["tsum"][l, :, H : 2 * H]
        o_small[6 * l + 3 : 6 * l + 4] = m["tsum"][l, :, 0:H]
        dlr, dli, ar, ai = (m["tsum"][l, :, 2 * H + k * Pn : 2 * H + (k + 1) * Pn] for k in range(4))
        kr, ki = m["tab"][l, me_d, 14][0:1], m["tab"][l, me_d, 15][0:1]
        size = kr * kr + ki * ki
        dkr, dki = (ar * kr - ai * ki) / size, (ar * ki + ai * kr) / size
        _, pull = jax.vjp(transition, *(m["prm"][i, me_d, l] for i in range(3)))
        for k, v in enumerate(pull((dlr, dli, dkr, dki))):
            o_lam[3 * l + k : 3 * l + k + 1] = v

    def gate_share(l):
        src = m["fX"].at[l, pl.ds(geo.out_rows, geo.half_rows)]
        dst = m["glf"].at[l, me_d]
        (wait,) = net.swap([(src, dst, dst)])
        m["glf"][l, me_d] = m["fX"][l, geo.out_rows : geo.out_rows + geo.half_rows]
        return wait

    kept = {}

    def stage_b1(l):
        def open_gate(i):
            dout = rows(m["g"], i) * masked(i)
            sig = rows(m["sig"].at[l], i)
            v = (dout * flat(m["act"].at[l], i) * sig * (1.0 - sig)).astype(BF16)
            put_flat(m["dgt"], i, v)
            return (v.astype(F32),)

        (kept["glub", l],) = sweep(open_gate, 1)

    def stage_da(l):
        put3(m["tmp"], dot(m["dgt"][...], m["glw"][l], 1, 1))

    def stage_b2(l):
        def through(i):
            dout = rows(m["g"], i) * masked(i)
            d = (rows(m["tmp"], i) + dout * rows(m["sig"].at[l], i)) * rows(m["dge"].at[l], i)
            m["dmx"][pl.ds(i * GROUP, GROUP)] = d
            put_flat(m["dml"], i, d)
            return (d * flat(m["nrm"].at[l], i),)

        (kept["feed", l],) = sweep(through, 1)

    def stage_ds(l):
        m["ds"][...] = dot(m["dml"][...], m["wout"][l], 1, 1)

    def stage_p1(l):
        ends_up, ends_dn = scan(l, 1, m["ds"], True, zeros4, None)
        kept["enter", l] = carries(LAYERS + l, l, 1, ends_up, ends_dn, True)

    def stage_og(l):
        out_grads(l)
        reductions["X", l].pair_send()

    def stage_p2(l):
        in_up, in_dn = kept["enter", l]()

        def save(dd, at, value):
            m["r"][pl.ds(at, 16), dd * W : (dd + 1) * W] = value

        scan(l, 1, m["ds"], True, (*in_up, *in_dn), save)

    def stage_ig(l):
        in_grads(l)
        reductions["I", l].pair_send()

    def stage_dn(l):
        put3(m["tmp"], dot(m["r"][...], m["win"][l], 1, 1))

    def stage_b3(l):
        v_feed, v_mean, v_inv = rep(feed[l : l + 1]), rep(stat(l, 0)), rep(stat(l, 1))

        def normed_grad(i):
            d = (v_feed * rows(m["dmx"], i) + rows(m["tmp"], i)) * masked(i)
            m["tmp"][pl.ds(i * GROUP, GROUP)] = d
            return d, d * ((rows(m["xs"].at[l], i) - v_mean) * v_inv)

        plain, scaled = sweep(normed_grad, 2)
        slot = 1 + l
        m["msg"][slot, 0:1] = plain
        m["msg"][slot, 1:2] = scaled
        kept["sums", l] = sum_over_all(m["msg"].at[slot], "", slot)

    def stage_ty(l):
        kept["tiny", l] = tiny_sums(l, kept["glub", l], kept["feed", l])

    def stage_tp(l):
        kept["tiny", l] = tiny_near(l, kept["tiny", l])

    def stage_tm(l):
        kept["tiny", l] = tiny_middle(l, kept["tiny", l])

    def stage_te(l):
        tiny_end(l, kept["tiny", l])

    def stage_b4(l):
        sums = kept["sums", l]()
        plain, scaled = sums[0:1], sums[1:2]
        o_small[6 * l + 0 : 6 * l + 1] = scaled
        o_small[6 * l + 1 : 6 * l + 2] = plain
        inv = stat(l, 1)
        inv_count = m["stat"][15:16]
        v_scale, v_mean = rep(inv * gain[l : l + 1]), rep(stat(l, 0))
        v_plain, v_scaled = rep(plain * inv_count), rep(scaled * inv_count * inv)

        def stream_grad(i):
            lead = rows(m["tmp"], i) - masked(i) * (v_plain + (rows(m["xs"].at[l], i) - v_mean) * v_scaled)
            at = pl.ds(i * GROUP, GROUP)
            m["g"][at] = m["g"][at] + v_scale * lead

        sweep(stream_grad)
        if l == 0:
            deliver(m["g"], o_ig)

    def stage_gs(l):
        reductions["X", l].done()
        kept["share", l] = gate_share(l)

    stages = dict(
        zip(
            STAGES,
            (
                stage_b1, stage_da, stage_b2, stage_ds, stage_p1, stage_og, stage_p2, stage_ig,
                stage_dn, stage_b3, stage_ty, stage_tp, stage_tm, stage_te, stage_b4, stage_gs,
            ),
        )
    )
    sums_of = dict(zip(SUMS, (reductions[k, l] for k in ("X", "I") for l in range(LAYERS))))
    for what, at in SCHEDULE:
        if what in stages:
            stages[what](at)
        elif at == OPEN:
            sums_of[what].open()
        else:
            sums_of[what].step(at)
    for l in range(LAYERS):
        kept["share", l]()
    for red in reductions.values():
        red.done()
    for k in geo.rows:
        reductions[k, 0].settle()
    for w in out_waits:
        w()
    net.finish()


def on_device(sizes, inputs, cotangent, lengths, gain, bias, in_proj, out_proj, rate, step, freq, feed, gluw, glub, rmean, rvar):
    geo = Geometry(sizes, inputs.shape, rate.shape[-1])
    T, H, W = geo.T, geo.H, geo.W
    v = scratch_shapes(geo)
    held = sum(math.prod(shape) * jnp.dtype(kind).itemsize for shape, kind in v.values())
    hbm = pl.BlockSpec(memory_space=pl.ANY)
    vmem = pl.BlockSpec(memory_space=pltpu.VMEM)
    smem = pl.BlockSpec(memory_space=pltpu.SMEM)
    outs = [
        pltpu.VMEM((geo.seqs, T, H), F32),
        pltpu.VMEM((geo.seqs, T, H), F32),
        pltpu.VMEM((LAYERS, geo.rows["X"], WIDE), BF16),
        pltpu.VMEM((LAYERS, geo.D, geo.half_rows, WIDE), BF16),
        pltpu.VMEM((LAYERS, geo.rows["I"], WIDE), BF16),
        pltpu.VMEM((6 * LAYERS, H), F32),
        pltpu.VMEM((3 * LAYERS, geo.Pn), F32),
    ]
    act, ig, gx, gl, gi, small, lam = pl.pallas_call(
        functools.partial(body, geo, tuple(v)),
        out_shape=outs,
        in_specs=[smem, hbm, hbm, vmem, vmem, hbm, hbm, hbm, hbm, hbm, vmem, hbm, vmem, vmem, vmem],
        out_specs=[vmem] * 7,
        scratch_shapes=[pltpu.VMEM(*s) for s in v.values()]
        + [pltpu.SemaphoreType.DMA((SEMAPHORES,)), pltpu.SemaphoreType.DMA((SEMAPHORES,)), pltpu.SemaphoreType.DMA((32,))],
        compiler_params=pltpu.CompilerParams(
            collective_id=0, has_side_effects=True, vmem_limit_bytes=held + SPARE_BYTES
        ),
    )(lengths, inputs, cotangent, gain, bias, in_proj, out_proj, rate, step, freq, feed, gluw, glub, rmean, rvar)
    return finish(geo, act, ig, gx, gl, gi, small, lam)


def results(geo, *refs):
    T, H, W, Pn, L = geo.T, geo.H, geo.W, geo.Pn, LAYERS
    act, ig, gx, gl, gi, small, lam = refs[:7]
    (o_act, o_ig, o_gain, o_bias, o_in, o_out, o_rate, o_step, o_freq, o_feed, o_glu, o_glub, o_mean, o_var) = refs[7:21]
    v_in, v_out, v_glu, sems = refs[21:]
    used = [0]

    def copy(src, dst):
        sem = sems.at[used[0]]
        used[0] += 1
        c = pltpu.make_async_copy(src, dst, sem)
        c.start()
        return c

    order = list(reversed(range(L)))
    waits = [copy(act, o_act), copy(ig, o_ig)]
    for l in range(L):
        for k, o in enumerate((o_gain, o_bias, o_feed, o_glub, o_mean, o_var)):
            o[l : l + 1] = small[6 * l + k : 6 * l + k + 1]
        for k, o in enumerate((o_rate, o_step, o_freq)):
            o[l] = lam[3 * l + k : 3 * l + k + 1]
    block = 64
    half = H // 2
    for l in order:
        for n in range(H // WIDE):

            def move(i, _):
                v_out[l, pl.ds(i * block, block), n * WIDE : (n + 1) * WIDE] = gx[
                    l, pl.ds(n * W + i * block, block)
                ].astype(F32)
                return 0

            lax.fori_loop(0, W // block, move, 0)
        waits.append(copy(v_out.at[l], o_out.at[l, 0]))
        for n in range(Pn // LANES):

            def move(i, _):
                value = gi[l, pl.ds(n * H + i * block, block)].astype(F32)
                at = pl.ds(i * block, block)
                v_in[l, at, n * LANES : (n + 1) * LANES] = value[:, :LANES]
                v_in[l, at, Pn + n * LANES : Pn + (n + 1) * LANES] = value[:, LANES:]
                return 0

            lax.fori_loop(0, H // block, move, 0)
        waits.append(copy(v_in.at[l], o_in.at[l, 0]))
        for d in range(geo.D):
            for n in range(H // WIDE):

                def move(i, _):
                    value = gl[l, d, pl.ds(n * half + i * block, block)].astype(F32)
                    v_glu[l, pl.ds(d * half + i * block, block), n * WIDE : (n + 1) * WIDE] = value
                    return 0

                lax.fori_loop(0, half // block, move, 0)
        waits.append(copy(v_glu.at[l], o_glu.at[l]))
    for c in waits:
        c.wait()


def finish(geo, act, ig, gx, gl, gi, small, lam):
    T, H, W, Pn, L = geo.T, geo.H, geo.W, geo.Pn, LAYERS
    hbm = pl.BlockSpec(memory_space=pl.ANY)
    vmem = pl.BlockSpec(memory_space=pltpu.VMEM)
    row = jax.ShapeDtypeStruct((L, H), F32)
    lam_row = jax.ShapeDtypeStruct((L, 1, Pn), F32)
    stream = jax.ShapeDtypeStruct((geo.seqs, T, H), F32)
    outs = [
        stream,
        stream,
        row,
        row,
        jax.ShapeDtypeStruct((L, 1, H, W), F32),
        jax.ShapeDtypeStruct((L, 1, W, H), F32),
        lam_row,
        lam_row,
        lam_row,
        row,
        jax.ShapeDtypeStruct((L, H, H), F32),
        row,
        row,
        row,
    ]
    where = [hbm, hbm, vmem, vmem, hbm, hbm, vmem, vmem, vmem, vmem, hbm, vmem, vmem, vmem]
    return pl.pallas_call(
        functools.partial(results, geo),
        out_shape=outs,
        in_specs=[vmem] * 7,
        out_specs=where,
        scratch_shapes=[
            pltpu.VMEM((L, H, W), F32),
            pltpu.VMEM((L, W, H), F32),
            pltpu.VMEM((L, H, H), F32),
            pltpu.SemaphoreType.DMA((16,)),
        ],
        compiler_params=pltpu.CompilerParams(vmem_limit_bytes=16 << 20),
    )(act, ig, gx, gl, gi, small, lam)


def solution(mesh):
    tokens = P("batch", "seq", None)
    per_dir = P(None, "dir", None)
    mats = P(None, "dir", None, None)
    in_specs = (tokens, tokens, P("batch"), P(), P(), mats, mats, per_dir, per_dir, per_dir) + (P(),) * 5
    out_specs = (tokens, tokens, P(), P(), mats, mats, per_dir, per_dir, per_dir) + (P(),) * 5
    return jax.shard_map(
        functools.partial(on_device, dict(mesh.shape)),
        mesh=mesh,
        in_specs=in_specs,
        out_specs=out_specs,
        check_vma=False,
    )
```

```python
import functools
import itertools
import math

import jax
import jax.numpy as jnp
from jax import lax
from jax.experimental import pallas as pl
from jax.experimental.pallas import tpu as pltpu
from jax.sharding import PartitionSpec as P

LAYERS = 2
EPSILON = 1e-05
MOMENTUM = 0.9
F32 = jnp.float32
BF16 = jnp.bfloat16
AXES = ("dir", "seq", "batch")
MESH = pl.DeviceIdType.MESH
LANES = 128
CHUNKS = 8
WIDE = 256
SPARE_BYTES = 5 << 19
SEMAPHORES = 144
SHARES = {"X": ((2, "xy"), (2, "yx"), (2, "xy"), (2, "yx")), "I": ((3, "xy"), (3, "yx"))}
STAGES = B1, DA, B2, DS, P1, OG, P2, IG, DN, B3, TY, TP, TM, TE, B4, GS = tuple(range(16))
SUMS = X0, X1, I0, I1 = tuple(range(16, 20))
OPEN = -1
SCHEDULE = (
    (B1, 1), (DA, 1), (B2, 1), (OG, 1), (DS, 1), (P1, 1), (X1, OPEN), (X1, 2),
    (X1, 1), (P2, 1), (DN, 1), (B3, 1), (X1, 2), (X1, 3), (X1, 0), (IG, 1),
    (TY, 1), (X1, 1), (I1, OPEN), (I1, 0), (I1, 1), (X1, 2), (X1, 0), (B4, 1),
    (B1, 0), (DA, 0), (X1, 1), (B2, 0), (X1, 3), (DS, 0), (X1, 2), (P1, 0),
    (OG, 0), (X1, 1), (I1, 1), (I1, 0), (X1, 2), (X1, 3), (X1, 0), (X0, OPEN),
    (X0, 2), (TP, 1), (P2, 0), (I1, 0), (X0, 1), (IG, 0), (X0, 0), (X1, 3),
    (X1, 0), (I1, 1), (X0, 3), (I0, OPEN), (I0, 0), (X0, 2), (X1, 1), (TY, 0),
    (X0, 0), (TM, 1), (X0, 1), (I0, 1), (I1, 0), (DN, 0), (X1, 2), (TP, 0),
    (X0, 2), (X0, 0), (X0, 3), (I1, 0), (I1, 1), (X0, 0), (I0, 0), (X1, 0),
    (X1, 3), (X0, 1), (I1, 1), (X0, 3), (B3, 0), (X0, 2), (X1, 3), (I0, 1),
    (TM, 0), (X1, 0), (I0, 0), (I1, 1), (I1, 0), (X0, 3), (X1, 2), (I0, 1),
    (X0, 2), (X0, 1), (X0, 0), (X0, 3), (TE, 1), (X1, 3), (X1, 1), (I0, 0),
    (X0, 1), (I0, 1), (X0, 2), (X0, 3), (I1, 0), (TE, 0), (I0, 0), (X0, 1),
    (I0, 1), (X1, 0), (X0, 0), (I0, 0), (X1, 1), (I0, 1), (I1, 1), (X0, 3),
    (B4, 0), (GS, 1), (X0, 0), (X0, 2), (X0, 1), (GS, 0), (I0, 0), (I0, 1),
)


def transition(rate_vec, step_vec, freq_vec):
    half_a = 0.5 * step_vec * rate_vec
    half_c = 0.5 * step_vec * freq_vec
    denominator = (1.0 + half_a) * (1.0 + half_a) + half_c * half_c
    lam_re = (1.0 - half_a * half_a - half_c * half_c) / denominator
    lam_im = 2.0 * half_c / denominator
    kap_re = step_vec * (1.0 + half_a) / denominator
    kap_im = step_vec * half_c / denominator
    return (lam_re, lam_im, kap_re, kap_im)


def dot(a, b, ca, cb):
    return lax.dot_general(a, b, (((ca,), (cb,)), ((), ())), preferred_element_type=F32)


def cmul(a, b):
    return (a[0] * b[0] - a[1] * b[1], a[0] * b[1] + a[1] * b[0])


def conj(a):
    return (a[0], -a[1])


def widen(mask):
    return jnp.concatenate([mask] * 4, axis=-1)


class Geometry:
    def __init__(self, sizes, local_shape, states):
        self.D, self.S, self.B = (sizes[a] for a in AXES)
        self.sizes = dict(sizes)
        self.seqs, self.T, self.H = local_shape
        self.Pn = states
        self.W = 2 * states
        self.J = self.T // CHUNKS
        self.N = self.D * self.S * self.B
        self.unit = 16 * self.S * self.B
        up = lambda n: -(-n // self.unit) * self.unit
        self.out_rows = (self.H // WIDE) * self.W
        self.half_rows = (self.H // WIDE) * (self.H // 2)
        self.in_rows = (self.Pn // LANES) * self.H
        self.used = {"X": self.out_rows + self.half_rows, "I": self.in_rows}
        self.rows = {k: up(v) for k, v in self.used.items()}
        bits = tuple(("batch", k) for k in range((self.B - 1).bit_length()))
        seq = (("seq", None),)
        ways = {"xy": bits + seq, "yx": bits[::-1] + seq, "zx": seq + bits, "zy": seq + bits[::-1]}
        self.colors = {}
        for k, n in self.rows.items():
            shares = SHARES[k]
            if n // self.unit != sum(count for count, _ in shares):
                shares = ((n // self.unit, "xy"),)
            at, self.colors[k] = 0, []
            for count, name in shares:
                self.colors[k].append((at, count * self.unit, ways[name]))
                at += count * self.unit
        self.direct = self.N <= 64

    def ways(self, dim):
        return self.S if dim[1] is None else 2


class Net:
    def __init__(self, geo, send_sems, recv_sems):
        self.geo, self.send_sems, self.recv_sems = geo, send_sems, recv_sems
        self.used_send = 0
        self.used_recv = 0
        self.at = {a: lax.axis_index(a) for a in AXES}
        self.unsent = []
        self.turned = {}

    def send_sem(self):
        self.used_send += 1
        return self.send_sems.at[self.used_send - 1]

    def recv_sem(self):
        self.used_recv += 1
        return self.recv_sems.at[self.used_recv - 1]

    def index(self, axes):
        lin = 0
        for a in axes:
            lin = lin * self.geo.sizes[a] + self.at[a]
        return lin

    def count(self, axes):
        n = 1
        for a in axes:
            n *= self.geo.sizes[a]
        return n

    def peers(self, axes, act):
        n = self.count(axes)
        sizes = [self.geo.sizes[a] for a in axes]
        if n <= 64 and all(size & (size - 1) == 0 for size in sizes):
            offsets = list(itertools.product(*(range(size) for size in sizes)))[1:]
            far = lambda off: sum(o if a == "seq" else 0.5 * (o > 0) if a == "dir" else bin(o).count("1") for a, o in zip(axes, off))
            for off in sorted(offsets, key=far, reverse=True):
                where, lin, k = {}, 0, 0
                for a, o, size in zip(axes, off, sizes):
                    where[a] = self.across(a, o)
                    lin = lin * size + where[a]
                    k = k * size + o
                act(where, lin, k)
            return

        def body(k, _):
            where, lin, rest, coords = {}, 0, k, []
            for a, size in zip(reversed(axes), reversed(sizes)):
                coords.append((a, lax.rem(self.at[a] + lax.rem(rest, size), size)))
                rest = lax.div(rest, size)
            for a, c in reversed(coords):
                where[a] = c
                lin = lin * self.geo.sizes[a] + c
            act(where, lin, k)
            return 0

        lax.fori_loop(1, n, body, 0)

    def across(self, axis, offset):
        if (axis, offset) not in self.turned:
            v = self.at[axis]
            for bit in range(offset.bit_length()):
                if offset >> bit & 1:
                    v = v + (1 - 2 * lax.rem(lax.div(v, 1 << bit), 2)) * (1 << bit)
            self.turned[axis, offset] = v
        return self.turned[axis, offset]

    def place(self, dim):
        axis, bit = dim
        return self.at[axis] if bit is None else lax.rem(lax.div(self.at[axis], 1 << bit), 2)

    def others(self, dim, act):
        axis, bit = dim
        if bit is None:
            self.peers((axis,), act)
        else:
            mine = self.place(dim)
            act({axis: self.at[axis] + (1 - 2 * mine) * (1 << bit)}, 1 - mine, 1)

    def put(self, src, dst, send, recv, peer):
        pltpu.make_async_remote_copy(
            src_ref=src, dst_ref=dst, send_sem=send, recv_sem=recv, device_id=peer, device_id_type=MESH
        ).start()

    def wait(self, ref, sem):
        pltpu.make_async_copy(ref, ref, sem).wait()

    def gather(self, src, land, axes):
        n = self.count(axes)
        send, recv = self.send_sem(), self.recv_sem()
        slot = self.index(axes)
        self.peers(axes, lambda peer, lin, k: self.put(src, land.at[slot], send, recv, peer))
        land[slot] = src[...]
        size = land.at[pl.ds(0, n - 1)]
        self.unsent.append((size, send))
        return functools.partial(self.wait, size, recv)

    def swap(self, pieces):
        peer = {"dir": 1 - self.at["dir"]}
        waits = []
        for src, dst, size in pieces:
            send, recv = self.send_sem(), self.recv_sem()
            self.put(src, dst, send, recv, peer)
            self.unsent.append((size, send))
            waits.append(functools.partial(self.wait, size, recv))
        return waits

    def finish(self):
        for size, send in self.unsent:
            self.wait(size, send)


def scratch_shapes(geo):
    T, H, W, J, S, N, Pn = geo.T, geo.H, geo.W, geo.J, geo.S, geo.N, geo.Pn
    L, D = LAYERS, geo.D
    v = {
        "mask": ((J, CHUNKS, LANES), F32),
        "win": ((L, H, D * W), BF16),
        "wout": ((L, D * W, H), BF16),
        "glw": ((L, H, H), BF16),
        "prm": ((3, D, L, 1, Pn), F32),
        "tab": ((L, D, 16, CHUNKS, Pn), F32),
        "xs": ((L + 1, J, CHUNKS, H), F32),
        "stat": ((16, H), F32),
        "nrm": ((L, T, H), BF16),
        "u": ((L, T, D * W), F32),
        "st": ((L, T + 32, D * W), BF16),
        "act": ((L, T, H), BF16),
        "sig": ((L, J, CHUNKS, H), BF16),
        "dge": ((L, J, CHUNKS, H), BF16),
        "tmp": ((J, CHUNKS, H), F32),
        "g": ((J, CHUNKS, H), F32),
        "dmx": ((J, CHUNKS, H), F32),
        "dml": ((T, H), BF16),
        "dgt": ((T, H), BF16),
        "ds": ((T, D * W), F32),
        "r": ((T, D * W), BF16),
        "msg0": ((2, H + LANES), F32),
        "msg": ((3, 2, H), F32),
        "smsg": ((2 * L, 1, D * W), F32),
        "sland": ((2 * L, S, 1, D * W), F32),
        "tiny": ((L, D, 1, 2 * H + 2 * W), F32),
        "tpair": ((L, 1, 2 * H + 2 * W), F32),
        "tnear": ((L, 1, 2 * H + 2 * W), F32),
        "tland1": ((L, geo.B, 1, 2 * H + 2 * W), F32),
        "tmid": ((L, 1, 2 * H + 2 * W), F32),
        "tland2": ((L, S, 1, 2 * H + 2 * W), F32),
        "tsum": ((L, 1, 2 * H + 2 * W), F32),
    }
    for k, lead, wide in (("0", (), H + LANES), ("", (3,), H)):
        if geo.direct:
            v["land" + k] = ((*lead, N, 2, wide), F32)
        else:
            v["near" + k] = ((*lead, D * geo.B, 2, wide), F32)
            v["mid" + k] = ((*lead, 2, wide), F32)
            v["far" + k] = ((*lead, S, 2, wide), F32)
    for k, rows in geo.rows.items():
        v["g" + k] = ((D, rows, WIDE), BF16)
        v["p" + k] = ((L, rows, WIDE), BF16)
        for c, (_, n, order) in enumerate(geo.colors[k]):
            for i, dim in enumerate(order):
                ways = geo.ways(dim)
                n //= ways
                v[f"land{i}{k}{c}"] = ((L, ways - 1, n, WIDE), BF16)
                if i == 0:
                    v[f"red{k}{c}"] = ((L, n, WIDE), BF16)
    return v


class Reduction:
    def __init__(self, geo, net, kind, layer, m):
        self.geo, self.net, self.kind, self.layer, self.m = geo, net, kind, layer, m
        self.rows = geo.rows[kind]
        self.colors = geo.colors[kind]
        self.full = m["f" + kind].at[layer]
        self.mine = m["g" + kind].at[net.at["dir"]]
        self.flows = None

    def pair_send(self):
        landing = self.m["p" + self.kind].at[self.layer]
        other = self.m["g" + self.kind].at[1 - self.net.at["dir"]]
        (self.pair_wait,) = self.net.swap([(other, landing, landing)])
        self.held = [self.net.unsent.pop()]

    def settle(self):
        for size, send in self.held:
            self.net.wait(size, send)

    def pair_done(self):
        self.pair_wait()
        landing = self.m["p" + self.kind].at[self.layer]
        block = 64

        def body(i, _):
            at = pl.ds(i * block, block)
            self.mine[at] = self.mine[at] + landing[at]
            return 0

        lax.fori_loop(0, self.rows // block, body, 0)

    def scatter(self, dim, src, base, part, land):
        net = self.net
        send, recv = net.send_sem(), net.recv_sem()
        net.others(
            dim,
            lambda peer, lin, k: net.put(
                src.at[pl.ds(base + lin * part, part)], land.at[k - 1], send, recv, peer
            ),
        )
        net.unsent.append((land, send))
        return functools.partial(net.wait, land, recv)

    def add(self, own, own_at, land, n, out, out_at, part):
        block = next(b for b in (64, 48, 32, 16) if part % b == 0)

        def body(i, _):
            if n == 2:
                out[pl.ds(out_at + i * block, block)] = (
                    own[pl.ds(own_at + i * block, block)] + land[0, pl.ds(i * block, block)]
                )
                return 0
            total = own[pl.ds(own_at + i * block, block)].astype(F32)
            for k in range(min(n - 1, 7)):
                total = total + land[k, pl.ds(i * block, block)].astype(F32)
            if n - 1 > 7:
                total = lax.fori_loop(
                    7, n - 1, lambda k, t: t + land[k, pl.ds(i * block, block)].astype(F32), total
                )
            out[pl.ds(out_at + i * block, block)] = total.astype(BF16)
            return 0

        lax.fori_loop(0, part // block, body, 0)

    def spread(self, dim, base, part):
        net, n = self.net, self.geo.ways(dim)
        send, recv = net.send_sem(), net.recv_sem()
        mine = self.full.at[pl.ds(base, part)]
        net.others(dim, lambda peer, lin, k: net.put(mine, mine, send, recv, peer))
        size = self.full.at[pl.ds(0, (n - 1) * part)]
        net.unsent.append((size, send))
        return functools.partial(net.wait, size, recv)

    def flow(self, c):
        base, size, order = self.colors[c]
        red = self.m[f"red{self.kind}{c}"].at[self.layer]
        src, src_at, at = self.mine, base, base
        owned = []
        for i, dim in enumerate(order):
            n = self.geo.ways(dim)
            part = size // n
            land = self.m[f"land{i}{self.kind}{c}"].at[self.layer]
            wait = self.scatter(dim, src, src_at, part, land)
            if i == 0:
                self.held.append(self.net.unsent.pop())
            yield
            wait()
            mine = self.net.place(dim)
            own_at, at = src_at + mine * part, at + mine * part
            if i + 1 == len(order):
                out, out_at = self.full, at
            else:
                out, out_at = red, 0 if i == 0 else own_at
            self.add(src, own_at, land, n, out, out_at, part)
            src, src_at, size = red, out_at, part
            owned.append((dim, at, part))
        for dim, at, part in reversed(owned):
            wait = self.spread(dim, at, part)
            yield
            wait()

    def open(self):
        self.pair_done()
        self.flows = [self.flow(c) for c in range(len(self.colors))]

    def step(self, c):
        if c < len(self.flows):
            next(self.flows[c], None)

    def done(self):
        for flow in self.flows:
            for _ in flow:
                pass


def body(geo, names, *refs):
    T, H, W, J, S, N, Pn = geo.T, geo.H, geo.W, geo.J, geo.S, geo.N, geo.Pn
    (lengths, inputs, cotangent, gain, bias, in_proj, out_proj, rate, step, freq, feed, gluw, glub, rmean, rvar) = refs[:15]
    (o_act, o_ig, o_gx, o_gl, o_gi, o_small, o_lam) = refs[15:22]
    scr = refs[22:]
    m = dict(zip(names, scr))
    m["fX"], m["fI"], m["glf"] = o_gx, o_gi, o_gl
    m["xin"], m["cin"], m["pm"] = m["dgt"], m["dml"], m["r"].at[:, 0:T]
    send_sems, recv_sems, local_sems = scr[len(names) :]
    net = Net(geo, send_sems, recv_sems)
    me_d, me_s = net.at["dir"], net.at["seq"]
    local = [0]

    def fetch(src, dst):
        sem = local_sems.at[local[0]]
        local[0] += 1
        copy = pltpu.make_async_copy(src, dst, sem)
        copy.start()
        return copy.wait

    def sum_over_all(msg, which, slot=None):
        at = lambda name: m[name + which] if slot is None else m[name + which].at[slot]
        if geo.direct:
            arrived = net.gather(msg, at("land"), AXES)

            def total():
                arrived()
                return jnp.sum(at("land")[...], axis=0)

            return total
        arrived = net.gather(msg, at("near"), ("dir", "batch"))

        def total():
            arrived()
            at("mid")[...] = jnp.sum(at("near")[...], axis=0)
            net.gather(at("mid"), at("far"), ("seq",))()
            return jnp.sum(at("far")[...], axis=0)

        return total

    barrier = pltpu.get_barrier_semaphore()
    net.peers(AXES, lambda peer, lin, k: pl.semaphore_signal(barrier, 1, device_id=peer, device_id_type=MESH))
    w_x = fetch(inputs.at[me_d], m["xin"])
    w_c = fetch(cotangent.at[me_d], m["cin"])
    raw = (rate, step, freq)
    w_p = [fetch(raw[i], m["prm"].at[i, me_d]) for i in range(3)]
    cols = pl.ds(pl.multiple_of(me_d * W, LANES), W)
    rows_of = pl.ds(pl.multiple_of(me_d * W, 16), W)
    in_at = [m["win"].at[l, :, cols] for l in range(LAYERS)]
    out_at = [m["wout"].at[l, rows_of] for l in range(LAYERS)]
    w_in = [fetch(in_proj.at[l, 0], in_at[l]) for l in range(LAYERS)]
    w_out = [fetch(out_proj.at[l, 0], out_at[l]) for l in range(LAYERS)]
    w_g = fetch(gluw, m["glw"])

    length = lengths[me_d]
    shape = (J, CHUNKS, LANES)
    position = (
        me_s * T
        + lax.broadcasted_iota(jnp.int32, shape, 1) * J
        + lax.broadcasted_iota(jnp.int32, shape, 0)
    )
    m["mask"][...] = jnp.where(position < length, 1.0, 0.0).astype(F32)

    def permutation(i, _):
        at = pl.ds(i * 64, 64)
        row = i * 64 + lax.broadcasted_iota(jnp.int32, (64, T), 0)
        col = lax.broadcasted_iota(jnp.int32, (64, T), 1)
        wanted = lax.rem(row, CHUNKS) * J + lax.div(row, CHUNKS)
        m["pm"][at] = jnp.where(col == wanted, 1.0, 0.0).astype(BF16)
        return 0

    lax.fori_loop(0, T // 64, permutation, 0)

    def put3(ref3, value):
        ref3[...] = value.reshape(J, CHUNKS, H)

    def reorder(src, dst):
        put3(dst, dot(m["pm"][...], src[...], 1, 0))

    GROUP = 4
    ROWS = GROUP * CHUNKS

    def rows(ref, i):
        return ref[pl.ds(i * GROUP, GROUP)].astype(F32)

    def flat(ref, i):
        return ref[pl.ds(i * ROWS, ROWS)].astype(F32).reshape(GROUP, CHUNKS, -1)

    def put_flat(ref, i, value):
        ref[pl.ds(i * ROWS, ROWS)] = value.reshape(ROWS, -1).astype(BF16)

    def sweep(act, sums=0):
        zero = tuple(jnp.zeros((CHUNKS, H), F32) for _ in range(sums))

        def one(i, acc):
            more = act(i)
            if not sums:
                return acc
            return tuple(a + jnp.sum(v, axis=0) for a, v in zip(acc, more))

        acc = lax.fori_loop(0, T // ROWS, one, zero)
        return tuple(jnp.sum(a, axis=0, keepdims=True) for a in acc)

    def rep(row):
        return jnp.broadcast_to(row, (CHUNKS, row.shape[-1]))

    masked = lambda i: widen(rows(m["mask"], i))

    w_x()
    reorder(m["xin"], m["xs"].at[0])

    def first(i):
        x = rows(m["xs"].at[0], i)
        xm = x * masked(i)
        return xm, xm * x

    s1, s2 = sweep(first, 2)
    here = jnp.sum(jnp.sum(m["mask"][...], axis=0), axis=0, keepdims=True)
    m["msg0"][0:1, 0:H] = s1
    m["msg0"][1:2, 0:H] = s2
    m["msg0"][:, H:] = jnp.broadcast_to(here, (2, LANES))

    pl.semaphore_wait(barrier, N - 1)
    stats = sum_over_all(m["msg0"], "0")
    send_in, send_out = [None] * LAYERS, [None] * LAYERS
    prm_waits = net.swap([(raw[i], m["prm"].at[i, me_d], m["prm"].at[i, me_d]) for i in range(3)])
    for l in range(LAYERS):
        (send_in[l],) = net.swap([(in_proj.at[l, 0], in_at[l], in_at[l])])
        (send_out[l],) = net.swap([(out_proj.at[l, 0], out_at[l], out_at[l])])

    for w in w_p + prm_waits:
        w()
    for l in range(LAYERS):
        for dd in range(geo.D):
            lr, li, kr, ki = transition(*(m["prm"][i, dd, l] for i in range(3)))
            power = (lr, li)
            for _ in range((J).bit_length() - 1):
                power = cmul(power, power)
            ladder = [power]
            for _ in range(3):
                ladder.append(cmul(ladder[-1], ladder[-1]))
            wide = [tuple(rep(v) for v in p) for p in ladder]
            chunk = lax.broadcasted_iota(jnp.int32, (CHUNKS, Pn), 0)
            one = (jnp.ones((CHUNKS, Pn), F32), jnp.zeros((CHUNKS, Pn), F32))
            up, down = one, one
            for k in range(3):
                bit = lax.rem(lax.div(chunk, 1 << k), 2)
                grown = cmul(up, wide[k])
                up = tuple(jnp.where(bit == 1, a, b) for a, b in zip(grown, up))
                grown = cmul(down, wide[k])
                down = tuple(jnp.where(bit == 0, a, b) for a, b in zip(grown, down))
            table = [rep(lr), rep(li), *up, *down]
            for p in wide:
                table.extend(p)
            table.extend([rep(kr), rep(ki)])
            for k, v in enumerate(table):
                m["tab"][l, dd, k] = v

    def entry(l, dd, k, minus):
        re, im = m["tab"][l, dd, 2 * k], m["tab"][l, dd, 2 * k + 1]
        return (re, -im) if minus else (re, im)

    def fold(l):
        for dd in range(geo.D):
            kr, ki = m["tab"][l, dd, 14][0:1], m["tab"][l, dd, 15][0:1]

            def some(i, _):
                at = pl.ds(i * 32, 32)
                w = m["win"][l, at, dd * W : (dd + 1) * W].astype(F32)
                re, im = w[:, :Pn], w[:, Pn:]
                new = jnp.concatenate([kr * re - ki * im, kr * im + ki * re], axis=1)
                m["win"][l, at, dd * W : (dd + 1) * W] = new.astype(BF16)
                return 0

            lax.fori_loop(0, H // 32, some, 0)

    for l in range(LAYERS):
        w_in[l]()
        send_in[l]()
        fold(l)
        w_out[l]()
        send_out[l]()
    w_c()
    reorder(m["cin"], m["g"])
    w_g()

    def split(block):
        return block[:, :Pn], block[:, Pn:]

    def advance(lam, h, d):
        return (lam[0] * h[0] - lam[1] * h[1] + d[0], lam[0] * h[1] + lam[1] * h[0] + d[1])

    def scan(l, up_dd, src, minus, start, emit):
        dn_dd = 1 - up_dd
        lam_up, lam_dn = entry(l, up_dd, 0, minus), entry(l, dn_dd, 0, minus)
        n = T // 16

        def two(i, carry):
            hu, hd = carry[:2], carry[2:]
            at_u, at_d = i * 16, (n - 1 - i) * 16
            bu = src[pl.ds(at_u, 16), up_dd * W : (up_dd + 1) * W]
            bd = src[pl.ds(at_d, 16), dn_dd * W : (dn_dd + 1) * W]
            keep_u, keep_d = [], []
            for k in range(2):
                hu = advance(lam_up, hu, split(bu[8 * k : 8 * k + 8]))
                hd = advance(lam_dn, hd, split(bd[8 - 8 * k : 16 - 8 * k]))
                keep_u.append(jnp.concatenate(hu, axis=1))
                keep_d.append(jnp.concatenate(hd, axis=1))
            if emit is not None:
                emit(up_dd, at_u, jnp.concatenate(keep_u, axis=0).astype(BF16))
                emit(dn_dd, at_d, jnp.concatenate(keep_d[::-1], axis=0).astype(BF16))
            return (*hu, *hd)

        out = lax.fori_loop(0, n, two, start, unroll=2)
        return out[:2], out[2:]

    chunk_at = lax.broadcasted_iota(jnp.int32, (CHUNKS, Pn), 0)

    def within(l, dd, ends, rising, minus):
        shift = (lambda v, k: pltpu.roll(v, k, 0)) if rising else (lambda v, k: pltpu.roll(v, CHUNKS - k, 0))
        inside = (lambda k: chunk_at >= k) if rising else (lambda k: chunk_at < CHUNKS - k)
        a = tuple(jnp.where(inside(1), shift(v, 1), 0.0) for v in ends)
        for k in range(3):
            far = tuple(jnp.where(inside(1 << k), shift(v, 1 << k), 0.0) for v in a)
            more = cmul(entry(l, dd, 3 + k, minus), far)
            a = (a[0] + more[0], a[1] + more[1])
        return a

    def carries(k, l, up_dd, ends_up, ends_dn, minus):
        dn_dd = 1 - up_dd
        pieces = [None] * geo.D
        for dd, ends, which in ((up_dd, ends_up, 2), (dn_dd, ends_dn, 1)):
            total = cmul(entry(l, dd, which, minus), ends)
            pieces[dd] = jnp.concatenate([jnp.sum(v, axis=0, keepdims=True) for v in total], axis=1)
        m["smsg"][k] = jnp.concatenate(pieces, axis=1)
        land = m["sland"].at[k]
        arrived = net.gather(m["smsg"].at[k], land, ("seq",))
        here_up = within(l, up_dd, ends_up, True, minus)
        here_dn = within(l, dn_dd, ends_dn, False, minus)
        def finish_up():
            arrived()
            def enter(dd, rising):
                whole = tuple(v[0:1] for v in entry(l, dd, 6, minus))
                zero = jnp.zeros((1, Pn), F32)

                def lap(i, state):
                    at = i if rising else S - 1 - i
                    piece = land[at][:, dd * W : (dd + 1) * W]
                    new = advance(whole, state, split(piece))
                    reached = (at < me_s) if rising else (at > me_s)
                    return tuple(jnp.where(reached, a, b) for a, b in zip(new, state))

                state = (zero, zero)
                if S <= 8:
                    for i in range(S):
                        state = lap(i, state)
                    return state
                return lax.fori_loop(0, S, lap, state)

            outs = []
            for dd, rising, here_ends, which in ((up_dd, True, here_up, 1), (dn_dd, False, here_dn, 2)):
                far = cmul(entry(l, dd, which, minus), tuple(rep(v) for v in enter(dd, rising)))
                outs.append((here_ends[0] + far[0], here_ends[1] + far[1]))
            return outs

        return finish_up

    zeros4 = tuple(jnp.zeros((CHUNKS, Pn), F32) for _ in range(4))

    def stat(l, k):
        return m["stat"][4 * l + k : 4 * l + k + 1]

    def set_stat(l, k, value):
        m["stat"][4 * l + k : 4 * l + k + 1] = value

    c0 = 0.7978845608028654
    c1 = 0.044715
    for l in range(LAYERS):
        sums = stats()
        if l == 0:
            m["stat"][15:16] = 1.0 / widen(sums[0:1, H:])
            sums = sums[:, :H]
        inv_count = m["stat"][15:16]
        mean = sums[0:1] * inv_count
        var = sums[1:2] * inv_count - mean * mean
        inv = lax.rsqrt(var + EPSILON)
        set_stat(l, 0, mean)
        set_stat(l, 1, inv)
        o_small[6 * l + 4 : 6 * l + 5] = MOMENTUM * rmean[l : l + 1] + (1.0 - MOMENTUM) * mean
        o_small[6 * l + 5 : 6 * l + 6] = MOMENTUM * rvar[l : l + 1] + (1.0 - MOMENTUM) * var
        v_mean, v_scale, v_bias = rep(mean), rep(inv * gain[l : l + 1]), rep(bias[l : l + 1])

        def normalise(i):
            x = rows(m["xs"].at[l], i)
            put_flat(m["nrm"].at[l], i, ((x - v_mean) * v_scale + v_bias) * masked(i))

        sweep(normalise)
        m["u"][l] = dot(m["nrm"][l], m["win"][l], 1, 0)
        ends_up, ends_dn = scan(l, 0, m["u"].at[l], False, zeros4, None)
        in_up, in_dn = carries(l, l, 0, ends_up, ends_dn, False)()
        both = lambda v: jnp.concatenate([jnp.concatenate(v, axis=1)] * 2, axis=0).astype(BF16)
        m["st"][l, 0:16, 0:W] = both(in_up)
        m["st"][l, T + 16 : T + 32, W:] = both(in_dn)

        def save(dd, at, value):
            m["st"][l, pl.ds(16 + at, 16), dd * W : (dd + 1) * W] = value

        scan(l, 0, m["u"].at[l], False, (*in_up, *in_dn), save)

        put3(m["tmp"], dot(m["st"][l, 16 : T + 16], m["wout"][l], 1, 0))
        v_feed = rep(feed[l : l + 1])

        def activate(i):
            v = rows(m["tmp"], i) + v_feed * flat(m["nrm"].at[l], i)
            sq = v * v
            t = jnp.tanh(c0 * v * (1.0 + c1 * sq))
            half = 0.5 * (1.0 + t)
            put_flat(m["act"].at[l], i, v * half)
            slope = half + 0.5 * v * (1.0 - t * t) * (c0 * (1.0 + 3.0 * c1 * sq))
            m["dge"][l, pl.ds(i * GROUP, GROUP)] = slope.astype(BF16)

        sweep(activate)
        put3(m["tmp"], dot(m["act"][l], m["glw"][l], 1, 0))
        v_glub = rep(glub[l : l + 1])

        def gate(i):
            sig = 0.5 + 0.5 * jnp.tanh(0.5 * (rows(m["tmp"], i) + v_glub))
            m["sig"][l, pl.ds(i * GROUP, GROUP)] = sig.astype(BF16)
            mk = masked(i)
            x = rows(m["xs"].at[l], i) + mk * flat(m["act"].at[l], i) * sig
            m["xs"][l + 1, pl.ds(i * GROUP, GROUP)] = x
            if l + 1 < LAYERS:
                xm = x * mk
                return xm, xm * x

        sums = sweep(gate, 2 if l + 1 < LAYERS else 0)
        if l + 1 < LAYERS:
            m["msg"][0, 0:1] = sums[0]
            m["msg"][0, 1:2] = sums[1]
            stats = sum_over_all(m["msg"].at[0], "", 0)

    out_waits = []

    def deliver(src, dst):
        send, recv = net.send_sem(), net.recv_sem()
        sem = local_sems.at[local[0]]
        local[0] += 1
        for c in range(CHUNKS):
            to = dst.at[me_d, pl.ds(c * J, J)]
            net.put(src.at[:, c], to, send, recv, {"dir": 1 - me_d})
            pltpu.make_async_copy(src.at[:, c], to, sem).start()
        net.unsent.append((dst.at[me_d], send))
        out_waits.append(functools.partial(net.wait, dst.at[1 - me_d], recv))
        out_waits.append(functools.partial(net.wait, dst.at[me_d], sem))

    deliver(m["xs"].at[LAYERS], o_act)

    reductions = {(k, l): Reduction(geo, net, k, l, m) for k in geo.rows for l in range(LAYERS)}

    def clear_rest(kind, l):
        used, rows_all = geo.used[kind], geo.rows[kind]
        if used < rows_all:
            for dd in range(geo.D):
                m["g" + kind][dd, used:rows_all] = jnp.zeros((rows_all - used, WIDE), BF16)

    def out_grads(l):
        if l + 1 < LAYERS:
            reductions["X", l + 1].settle()
        clear_rest("X", l)
        value = dot(m["st"][l, 16 : T + 16], m["dml"][...], 0, 0).astype(BF16)
        gates = dot(m["act"][l], m["dgt"][...], 0, 0).astype(BF16)
        half = H // 2
        for dd in range(geo.D):
            for i in range(H // WIDE):
                across = slice(i * WIDE, (i + 1) * WIDE)
                m["gX"][dd, i * W : (i + 1) * W] = value[dd * W : (dd + 1) * W, across]
                at = geo.out_rows + i * half
                m["gX"][dd, at : at + half] = gates[dd * half : (dd + 1) * half, across]

    def in_grads(l):
        if l + 1 < LAYERS:
            reductions["I", l + 1].settle()
        clear_rest("I", l)
        value = dot(m["nrm"][l], m["r"][...], 0, 0)
        for dd in range(geo.D):
            for i in range(Pn // LANES):
                across = slice(i * LANES, (i + 1) * LANES)
                kr, ki = m["tab"][l, dd, 14, 0:1, across], m["tab"][l, dd, 15, 0:1, across]
                at = dd * W + i * LANES
                re, im = value[:, at : at + LANES], value[:, at + Pn : at + Pn + LANES]
                new = jnp.concatenate([kr * re + ki * im, kr * im - ki * re], axis=1)
                m["gI"][dd, i * H : (i + 1) * H] = new.astype(BF16)

    def tiny_sums(l, d_glub, d_feed):
        for dd in range(geo.D):
            m["tiny"][l, dd, :, 0:H] = d_glub
            m["tiny"][l, dd, :, H : 2 * H] = d_feed

            def some(i, acc):
                at = i * 16
                across = slice(dd * W, (dd + 1) * W)
                rr, ri = split(m["r"][pl.ds(at, 16), across].astype(F32))
                ur, ui = split(m["u"][l, pl.ds(at, 16), across])
                cur = m["st"][l, pl.ds(at + 16, 16), across].astype(F32)
                if dd == 0:
                    near = m["st"][l, pl.ds(at, 16), across].astype(F32)
                    prev = jnp.concatenate([near[8:], cur[:8]], axis=0)
                else:
                    near = m["st"][l, pl.ds(at + 32, 16), across].astype(F32)
                    prev = jnp.concatenate([cur[8:], near[:8]], axis=0)
                hr, hi = split(prev)
                new = (rr * hr + ri * hi, ri * hr - rr * hi, rr * ur + ri * ui, ri * ur - rr * ui)
                return tuple(a + v[:8] + v[8:] for a, v in zip(acc, new))

            acc = lax.fori_loop(0, T // 16, some, zeros4, unroll=2)
            for k, v in enumerate(acc):
                at = 2 * H + k * Pn
                m["tiny"][l, dd, :, at : at + Pn] = jnp.sum(v, axis=0, keepdims=True)
        landing = m["tpair"].at[l]
        (wait,) = net.swap([(m["tiny"].at[l, 1 - me_d], landing, landing)])
        return wait

    def tiny_near(l, wait):
        wait()
        m["tnear"][l] = m["tiny"][l, me_d] + m["tpair"][l]
        return net.gather(m["tnear"].at[l], m["tland1"].at[l], ("batch",))

    def tiny_middle(l, wait):
        wait()
        m["tmid"][l] = jnp.sum(m["tland1"][l], axis=0)
        return net.gather(m["tmid"].at[l], m["tland2"].at[l], ("seq",))

    def tiny_end(l, wait):
        wait()
        m["tsum"][l] = jnp.sum(m["tland2"][l], axis=0)
        o_small[6 * l + 2 : 6 * l + 3] = m["tsum"][l, :, H : 2 * H]
        o_small[6 * l + 3 : 6 * l + 4] = m["tsum"][l, :, 0:H]
        dlr, dli, ar, ai = (m["tsum"][l, :, 2 * H + k * Pn : 2 * H + (k + 1) * Pn] for k in range(4))
        kr, ki = m["tab"][l, me_d, 14][0:1], m["tab"][l, me_d, 15][0:1]
        size = kr * kr + ki * ki
        dkr, dki = (ar * kr - ai * ki) / size, (ar * ki + ai * kr) / size
        _, pull = jax.vjp(transition, *(m["prm"][i, me_d, l] for i in range(3)))
        for k, v in enumerate(pull((dlr, dli, dkr, dki))):
            o_lam[3 * l + k : 3 * l + k + 1] = v

    def gate_share(l):
        src = m["fX"].at[l, pl.ds(geo.out_rows, geo.half_rows)]
        dst = m["glf"].at[l, me_d]
        (wait,) = net.swap([(src, dst, dst)])
        m["glf"][l, me_d] = m["fX"][l, geo.out_rows : geo.out_rows + geo.half_rows]
        return wait

    kept = {}

    def stage_b1(l):
        def open_gate(i):
            dout = rows(m["g"], i) * masked(i)
            sig = rows(m["sig"].at[l], i)
            v = (dout * flat(m["act"].at[l], i) * sig * (1.0 - sig)).astype(BF16)
            put_flat(m["dgt"], i, v)
            return (v.astype(F32),)

        (kept["glub", l],) = sweep(open_gate, 1)

    def stage_da(l):
        put3(m["tmp"], dot(m["dgt"][...], m["glw"][l], 1, 1))

    def stage_b2(l):
        def through(i):
            dout = rows(m["g"], i) * masked(i)
            d = (rows(m["tmp"], i) + dout * rows(m["sig"].at[l], i)) * rows(m["dge"].at[l], i)
            m["dmx"][pl.ds(i * GROUP, GROUP)] = d
            put_flat(m["dml"], i, d)
            return (d * flat(m["nrm"].at[l], i),)

        (kept["feed", l],) = sweep(through, 1)

    def stage_ds(l):
        m["ds"][...] = dot(m["dml"][...], m["wout"][l], 1, 1)

    def stage_p1(l):
        ends_up, ends_dn = scan(l, 1, m["ds"], True, zeros4, None)
        kept["enter", l] = carries(LAYERS + l, l, 1, ends_up, ends_dn, True)

    def stage_og(l):
        out_grads(l)
        reductions["X", l].pair_send()

    def stage_p2(l):
        in_up, in_dn = kept["enter", l]()

        def save(dd, at, value):
            m["r"][pl.ds(at, 16), dd * W : (dd + 1) * W] = value

        scan(l, 1, m["ds"], True, (*in_up, *in_dn), save)

    def stage_ig(l):
        in_grads(l)
        reductions["I", l].pair_send()

    def stage_dn(l):
        put3(m["tmp"], dot(m["r"][...], m["win"][l], 1, 1))

    def stage_b3(l):
        v_feed, v_mean, v_inv = rep(feed[l : l + 1]), rep(stat(l, 0)), rep(stat(l, 1))

        def normed_grad(i):
            d = (v_feed * rows(m["dmx"], i) + rows(m["tmp"], i)) * masked(i)
            m["tmp"][pl.ds(i * GROUP, GROUP)] = d
            return d, d * ((rows(m["xs"].at[l], i) - v_mean) * v_inv)

        plain, scaled = sweep(normed_grad, 2)
        slot = 1 + l
        m["msg"][slot, 0:1] = plain
        m["msg"][slot, 1:2] = scaled
        kept["sums", l] = sum_over_all(m["msg"].at[slot], "", slot)

    def stage_ty(l):
        kept["tiny", l] = tiny_sums(l, kept["glub", l], kept["feed", l])

    def stage_tp(l):
        kept["tiny", l] = tiny_near(l, kept["tiny", l])

    def stage_tm(l):
        kept["tiny", l] = tiny_middle(l, kept["tiny", l])

    def stage_te(l):
        tiny_end(l, kept["tiny", l])

    def stage_b4(l):
        sums = kept["sums", l]()
        plain, scaled = sums[0:1], sums[1:2]
        o_small[6 * l + 0 : 6 * l + 1] = scaled
        o_small[6 * l + 1 : 6 * l + 2] = plain
        inv = stat(l, 1)
        inv_count = m["stat"][15:16]
        v_scale, v_mean = rep(inv * gain[l : l + 1]), rep(stat(l, 0))
        v_plain, v_scaled = rep(plain * inv_count), rep(scaled * inv_count * inv)

        def stream_grad(i):
            lead = rows(m["tmp"], i) - masked(i) * (v_plain + (rows(m["xs"].at[l], i) - v_mean) * v_scaled)
            at = pl.ds(i * GROUP, GROUP)
            m["g"][at] = m["g"][at] + v_scale * lead

        sweep(stream_grad)
        if l == 0:
            deliver(m["g"], o_ig)

    def stage_gs(l):
        reductions["X", l].done()
        kept["share", l] = gate_share(l)

    stages = dict(
        zip(
            STAGES,
            (
                stage_b1, stage_da, stage_b2, stage_ds, stage_p1, stage_og, stage_p2, stage_ig,
                stage_dn, stage_b3, stage_ty, stage_tp, stage_tm, stage_te, stage_b4, stage_gs,
            ),
        )
    )
    sums_of = dict(zip(SUMS, (reductions[k, l] for k in ("X", "I") for l in range(LAYERS))))
    for what, at in SCHEDULE:
        if what in stages:
            stages[what](at)
        elif at == OPEN:
            sums_of[what].open()
        else:
            sums_of[what].step(at)
    for l in range(LAYERS):
        kept["share", l]()
    for red in reductions.values():
        red.done()
    for k in geo.rows:
        reductions[k, 0].settle()
    for w in out_waits:
        w()
    net.finish()


def on_device(sizes, inputs, cotangent, lengths, gain, bias, in_proj, out_proj, rate, step, freq, feed, gluw, glub, rmean, rvar):
    geo = Geometry(sizes, inputs.shape, rate.shape[-1])
    T, H, W = geo.T, geo.H, geo.W
    v = scratch_shapes(geo)
    held = sum(math.prod(shape) * jnp.dtype(kind).itemsize for shape, kind in v.values())
    hbm = pl.BlockSpec(memory_space=pl.ANY)
    vmem = pl.BlockSpec(memory_space=pltpu.VMEM)
    smem = pl.BlockSpec(memory_space=pltpu.SMEM)
    outs = [
        pltpu.VMEM((geo.seqs, T, H), F32),
        pltpu.VMEM((geo.seqs, T, H), F32),
        pltpu.VMEM((LAYERS, geo.rows["X"], WIDE), BF16),
        pltpu.VMEM((LAYERS, geo.D, geo.half_rows, WIDE), BF16),
        pltpu.VMEM((LAYERS, geo.rows["I"], WIDE), BF16),
        pltpu.VMEM((6 * LAYERS, H), F32),
        pltpu.VMEM((3 * LAYERS, geo.Pn), F32),
    ]
    act, ig, gx, gl, gi, small, lam = pl.pallas_call(
        functools.partial(body, geo, tuple(v)),
        out_shape=outs,
        in_specs=[smem, hbm, hbm, vmem, vmem, hbm, hbm, hbm, hbm, hbm, vmem, hbm, vmem, vmem, vmem],
        out_specs=[vmem] * 7,
        scratch_shapes=[pltpu.VMEM(*s) for s in v.values()]
        + [pltpu.SemaphoreType.DMA((SEMAPHORES,)), pltpu.SemaphoreType.DMA((SEMAPHORES,)), pltpu.SemaphoreType.DMA((32,))],
        compiler_params=pltpu.CompilerParams(
            collective_id=0, has_side_effects=True, vmem_limit_bytes=held + SPARE_BYTES
        ),
    )(lengths, inputs, cotangent, gain, bias, in_proj, out_proj, rate, step, freq, feed, gluw, glub, rmean, rvar)
    return finish(geo, act, ig, gx, gl, gi, small, lam)


def results(geo, *refs):
    T, H, W, Pn, L = geo.T, geo.H, geo.W, geo.Pn, LAYERS
    act, ig, gx, gl, gi, small, lam = refs[:7]
    (o_act, o_ig, o_gain, o_bias, o_in, o_out, o_rate, o_step, o_freq, o_feed, o_glu, o_glub, o_mean, o_var) = refs[7:21]
    v_in, v_out, v_glu, sems = refs[21:]
    used = [0]

    def copy(src, dst):
        sem = sems.at[used[0]]
        used[0] += 1
        c = pltpu.make_async_copy(src, dst, sem)
        c.start()
        return c

    order = list(reversed(range(L)))
    waits = [copy(act, o_act), copy(ig, o_ig)]
    for l in range(L):
        for k, o in enumerate((o_gain, o_bias, o_feed, o_glub, o_mean, o_var)):
            o[l : l + 1] = small[6 * l + k : 6 * l + k + 1]
        for k, o in enumerate((o_rate, o_step, o_freq)):
            o[l] = lam[3 * l + k : 3 * l + k + 1]
    block = 64
    half = H // 2
    for l in order:
        for n in range(H // WIDE):

            def move(i, _):
                v_out[l, pl.ds(i * block, block), n * WIDE : (n + 1) * WIDE] = gx[
                    l, pl.ds(n * W + i * block, block)
                ].astype(F32)
                return 0

            lax.fori_loop(0, W // block, move, 0)
        waits.append(copy(v_out.at[l], o_out.at[l, 0]))
        for n in range(Pn // LANES):

            def move(i, _):
                value = gi[l, pl.ds(n * H + i * block, block)].astype(F32)
                at = pl.ds(i * block, block)
                v_in[l, at, n * LANES : (n + 1) * LANES] = value[:, :LANES]
                v_in[l, at, Pn + n * LANES : Pn + (n + 1) * LANES] = value[:, LANES:]
                return 0

            lax.fori_loop(0, H // block, move, 0)
        waits.append(copy(v_in.at[l], o_in.at[l, 0]))
        for d in range(geo.D):
            for n in range(H // WIDE):

                def move(i, _):
                    value = gl[l, d, pl.ds(n * half + i * block, block)].astype(F32)
                    v_glu[l, pl.ds(d * half + i * block, block), n * WIDE : (n + 1) * WIDE] = value
                    return 0

                lax.fori_loop(0, half // block, move, 0)
        waits.append(copy(v_glu.at[l], o_glu.at[l]))
    for c in waits:
        c.wait()


def finish(geo, act, ig, gx, gl, gi, small, lam):
    T, H, W, Pn, L = geo.T, geo.H, geo.W, geo.Pn, LAYERS
    hbm = pl.BlockSpec(memory_space=pl.ANY)
    vmem = pl.BlockSpec(memory_space=pltpu.VMEM)
    row = jax.ShapeDtypeStruct((L, H), F32)
    lam_row = jax.ShapeDtypeStruct((L, 1, Pn), F32)
    stream = jax.ShapeDtypeStruct((geo.seqs, T, H), F32)
    outs = [
        stream,
        stream,
        row,
        row,
        jax.ShapeDtypeStruct((L, 1, H, W), F32),
        jax.ShapeDtypeStruct((L, 1, W, H), F32),
        lam_row,
        lam_row,
        lam_row,
        row,
        jax.ShapeDtypeStruct((L, H, H), F32),
        row,
        row,
        row,
    ]
    where = [hbm, hbm, vmem, vmem, hbm, hbm, vmem, vmem, vmem, vmem, hbm, vmem, vmem, vmem]
    return pl.pallas_call(
        functools.partial(results, geo),
        out_shape=outs,
        in_specs=[vmem] * 7,
        out_specs=where,
        scratch_shapes=[
            pltpu.VMEM((L, H, W), F32),
            pltpu.VMEM((L, W, H), F32),
            pltpu.VMEM((L, H, H), F32),
            pltpu.SemaphoreType.DMA((16,)),
        ],
        compiler_params=pltpu.CompilerParams(vmem_limit_bytes=16 << 20),
    )(act, ig, gx, gl, gi, small, lam)


def solution(mesh):
    tokens = P("batch", "seq", None)
    per_dir = P(None, "dir", None)
    mats = P(None, "dir", None, None)
    in_specs = (tokens, tokens, P("batch"), P(), P(), mats, mats, per_dir, per_dir, per_dir) + (P(),) * 5
    out_specs = (tokens, tokens, P(), P(), mats, mats, per_dir, per_dir, per_dir) + (P(),) * 5
    return jax.shard_map(
        functools.partial(on_device, dict(mesh.shape)),
        mesh=mesh,
        in_specs=in_specs,
        out_specs=out_specs,
        check_vma=False,
    )
```

```python
import functools
import itertools
import math

import jax
import jax.numpy as jnp
from jax import lax
from jax.experimental import pallas as pl
from jax.experimental.pallas import tpu as pltpu
from jax.sharding import PartitionSpec as P

LAYERS = 2
EPSILON = 1e-05
MOMENTUM = 0.9
F32 = jnp.float32
BF16 = jnp.bfloat16
AXES = ("dir", "seq", "batch")
MESH = pl.DeviceIdType.MESH
LANES = 128
CHUNKS = 8
WIDE = 256
SPARE_BYTES = 5 << 19
SEMAPHORES = 144
SHARES = {"X": ((2, "xy"), (2, "yx"), (2, "xy"), (2, "yx")), "I": ((3, "xy"), (3, "yx"))}
STAGES = B1, DA, B2, DS, P1, OG, P2, IG, DN, B3, TY, TP, TM, TE, B4, GS = tuple(range(16))
SUMS = X0, X1, I0, I1 = tuple(range(16, 20))
OPEN = -1
SCHEDULE = (
    (B1, 1), (DA, 1), (B2, 1), (OG, 1), (DS, 1), (P1, 1), (X1, OPEN), (X1, 2),
    (X1, 1), (P2, 1), (DN, 1), (B3, 1), (X1, 2), (X1, 3), (X1, 0), (IG, 1),
    (TY, 1), (X1, 1), (I1, OPEN), (I1, 0), (I1, 1), (X1, 2), (X1, 0), (B4, 1),
    (B1, 0), (DA, 0), (X1, 1), (B2, 0), (X1, 3), (DS, 0), (X1, 2), (P1, 0),
    (OG, 0), (X1, 1), (I1, 1), (I1, 0), (X1, 2), (X1, 3), (X1, 0), (X0, OPEN),
    (X0, 2), (TP, 1), (P2, 0), (I1, 0), (X0, 1), (IG, 0), (I1, 1), (X0, 0),
    (X1, 3), (X1, 0), (X0, 3), (I0, OPEN), (I0, 0), (X0, 2), (X1, 1), (TY, 0),
    (X0, 0), (TM, 1), (X0, 1), (I0, 1), (I1, 0), (DN, 0), (TP, 0), (X0, 2),
    (X0, 0), (X1, 2), (X0, 3), (I1, 0), (I1, 1), (X0, 0), (I0, 0), (X1, 0),
    (X1, 3), (X0, 1), (I1, 1), (X0, 3), (B3, 0), (X0, 2), (X1, 3), (I0, 1),
    (TM, 0), (X1, 0), (I0, 0), (I1, 1), (X0, 3), (I1, 0), (X1, 2), (I0, 1),
    (X0, 2), (X0, 1), (X0, 0), (X0, 3), (X1, 3), (TE, 1), (X1, 1), (I0, 0),
    (X0, 1), (I0, 1), (X0, 2), (X0, 3), (I1, 0), (TE, 0), (I0, 0), (X0, 1),
    (I0, 1), (X1, 0), (X0, 0), (I0, 0), (X1, 1), (I0, 1), (I1, 1), (X0, 3),
    (B4, 0), (GS, 1), (X0, 0), (X0, 2), (X0, 1), (GS, 0), (I0, 0), (I0, 1),
)


def transition(rate_vec, step_vec, freq_vec):
    half_a = 0.5 * step_vec * rate_vec
    half_c = 0.5 * step_vec * freq_vec
    denominator = (1.0 + half_a) * (1.0 + half_a) + half_c * half_c
    lam_re = (1.0 - half_a * half_a - half_c * half_c) / denominator
    lam_im = 2.0 * half_c / denominator
    kap_re = step_vec * (1.0 + half_a) / denominator
    kap_im = step_vec * half_c / denominator
    return (lam_re, lam_im, kap_re, kap_im)


def dot(a, b, ca, cb):
    return lax.dot_general(a, b, (((ca,), (cb,)), ((), ())), preferred_element_type=F32)


def cmul(a, b):
    return (a[0] * b[0] - a[1] * b[1], a[0] * b[1] + a[1] * b[0])


def conj(a):
    return (a[0], -a[1])


def widen(mask):
    return jnp.concatenate([mask] * 4, axis=-1)


class Geometry:
    def __init__(self, sizes, local_shape, states):
        self.D, self.S, self.B = (sizes[a] for a in AXES)
        self.sizes = dict(sizes)
        self.seqs, self.T, self.H = local_shape
        self.Pn = states
        self.W = 2 * states
        self.J = self.T // CHUNKS
        self.N = self.D * self.S * self.B
        self.unit = 16 * self.S * self.B
        up = lambda n: -(-n // self.unit) * self.unit
        self.out_rows = (self.H // WIDE) * self.W
        self.half_rows = (self.H // WIDE) * (self.H // 2)
        self.in_rows = (self.Pn // LANES) * self.H
        self.used = {"X": self.out_rows + self.half_rows, "I": self.in_rows}
        self.rows = {k: up(v) for k, v in self.used.items()}
        bits = tuple(("batch", k) for k in range((self.B - 1).bit_length()))
        seq = (("seq", None),)
        ways = {"xy": bits + seq, "yx": bits[::-1] + seq, "zx": seq + bits, "zy": seq + bits[::-1]}
        self.colors = {}
        for k, n in self.rows.items():
            shares = SHARES[k]
            if n // self.unit != sum(count for count, _ in shares):
                shares = ((n // self.unit, "xy"),)
            at, self.colors[k] = 0, []
            for count, name in shares:
                self.colors[k].append((at, count * self.unit, ways[name]))
                at += count * self.unit
        self.direct = self.N <= 64

    def ways(self, dim):
        return self.S if dim[1] is None else 2


class Net:
    def __init__(self, geo, send_sems, recv_sems):
        self.geo, self.send_sems, self.recv_sems = geo, send_sems, recv_sems
        self.used_send = 0
        self.used_recv = 0
        self.at = {a: lax.axis_index(a) for a in AXES}
        self.unsent = []
        self.turned = {}

    def send_sem(self):
        self.used_send += 1
        return self.send_sems.at[self.used_send - 1]

    def recv_sem(self):
        self.used_recv += 1
        return self.recv_sems.at[self.used_recv - 1]

    def index(self, axes):
        lin = 0
        for a in axes:
            lin = lin * self.geo.sizes[a] + self.at[a]
        return lin

    def count(self, axes):
        n = 1
        for a in axes:
            n *= self.geo.sizes[a]
        return n

    def peers(self, axes, act):
        n = self.count(axes)
        sizes = [self.geo.sizes[a] for a in axes]
        if n <= 64 and all(size & (size - 1) == 0 for size in sizes):
            offsets = list(itertools.product(*(range(size) for size in sizes)))[1:]
            far = lambda off: sum(o if a == "seq" else 0.5 * (o > 0) if a == "dir" else bin(o).count("1") for a, o in zip(axes, off))
            for off in sorted(offsets, key=far, reverse=True):
                where, lin, k = {}, 0, 0
                for a, o, size in zip(axes, off, sizes):
                    where[a] = self.across(a, o)
                    lin = lin * size + where[a]
                    k = k * size + o
                act(where, lin, k)
            return

        def body(k, _):
            where, lin, rest, coords = {}, 0, k, []
            for a, size in zip(reversed(axes), reversed(sizes)):
                coords.append((a, lax.rem(self.at[a] + lax.rem(rest, size), size)))
                rest = lax.div(rest, size)
            for a, c in reversed(coords):
                where[a] = c
                lin = lin * self.geo.sizes[a] + c
            act(where, lin, k)
            return 0

        lax.fori_loop(1, n, body, 0)

    def across(self, axis, offset):
        if (axis, offset) not in self.turned:
            v = self.at[axis]
            for bit in range(offset.bit_length()):
                if offset >> bit & 1:
                    v = v + (1 - 2 * lax.rem(lax.div(v, 1 << bit), 2)) * (1 << bit)
            self.turned[axis, offset] = v
        return self.turned[axis, offset]

    def place(self, dim):
        axis, bit = dim
        return self.at[axis] if bit is None else lax.rem(lax.div(self.at[axis], 1 << bit), 2)

    def others(self, dim, act):
        axis, bit = dim
        if bit is None:
            self.peers((axis,), act)
        else:
            mine = self.place(dim)
            act({axis: self.at[axis] + (1 - 2 * mine) * (1 << bit)}, 1 - mine, 1)

    def put(self, src, dst, send, recv, peer):
        pltpu.make_async_remote_copy(
            src_ref=src, dst_ref=dst, send_sem=send, recv_sem=recv, device_id=peer, device_id_type=MESH
        ).start()

    def wait(self, ref, sem):
        pltpu.make_async_copy(ref, ref, sem).wait()

    def gather(self, src, land, axes):
        n = self.count(axes)
        send, recv = self.send_sem(), self.recv_sem()
        slot = self.index(axes)
        self.peers(axes, lambda peer, lin, k: self.put(src, land.at[slot], send, recv, peer))
        land[slot] = src[...]
        size = land.at[pl.ds(0, n - 1)]
        self.unsent.append((size, send))
        return functools.partial(self.wait, size, recv)

    def swap(self, pieces):
        peer = {"dir": 1 - self.at["dir"]}
        waits = []
        for src, dst, size in pieces:
            send, recv = self.send_sem(), self.recv_sem()
            self.put(src, dst, send, recv, peer)
            self.unsent.append((size, send))
            waits.append(functools.partial(self.wait, size, recv))
        return waits

    def finish(self):
        for size, send in self.unsent:
            self.wait(size, send)


def scratch_shapes(geo):
    T, H, W, J, S, N, Pn = geo.T, geo.H, geo.W, geo.J, geo.S, geo.N, geo.Pn
    L, D = LAYERS, geo.D
    v = {
        "mask": ((J, CHUNKS, LANES), F32),
        "win": ((L, H, D * W), BF16),
        "wout": ((L, D * W, H), BF16),
        "glw": ((L, H, H), BF16),
        "prm": ((3, D, L, 1, Pn), F32),
        "tab": ((L, D, 16, CHUNKS, Pn), F32),
        "xs": ((L + 1, J, CHUNKS, H), F32),
        "stat": ((16, H), F32),
        "nrm": ((L, T, H), BF16),
        "u": ((L, T, D * W), F32),
        "st": ((L, T + 32, D * W), BF16),
        "act": ((L, T, H), BF16),
        "sig": ((L, J, CHUNKS, H), BF16),
        "dge": ((L, J, CHUNKS, H), BF16),
        "tmp": ((J, CHUNKS, H), F32),
        "g": ((J, CHUNKS, H), F32),
        "dmx": ((J, CHUNKS, H), F32),
        "dml": ((T, H), BF16),
        "dgt": ((T, H), BF16),
        "ds": ((T, D * W), F32),
        "r": ((T, D * W), BF16),
        "msg0": ((2, H + LANES), F32),
        "msg": ((3, 2, H), F32),
        "smsg": ((2 * L, 1, D * W), F32),
        "sland": ((2 * L, S, 1, D * W), F32),
        "tiny": ((L, D, 1, 2 * H + 2 * W), F32),
        "tpair": ((L, 1, 2 * H + 2 * W), F32),
        "tnear": ((L, 1, 2 * H + 2 * W), F32),
        "tland1": ((L, geo.B, 1, 2 * H + 2 * W), F32),
        "tmid": ((L, 1, 2 * H + 2 * W), F32),
        "tland2": ((L, S, 1, 2 * H + 2 * W), F32),
        "tsum": ((L, 1, 2 * H + 2 * W), F32),
    }
    for k, lead, wide in (("0", (), H + LANES), ("", (3,), H)):
        if geo.direct:
            v["land" + k] = ((*lead, N, 2, wide), F32)
        else:
            v["near" + k] = ((*lead, D * geo.B, 2, wide), F32)
            v["mid" + k] = ((*lead, 2, wide), F32)
            v["far" + k] = ((*lead, S, 2, wide), F32)
    for k, rows in geo.rows.items():
        v["g" + k] = ((D, rows, WIDE), BF16)
        v["p" + k] = ((L, rows, WIDE), BF16)
        for c, (_, n, order) in enumerate(geo.colors[k]):
            for i, dim in enumerate(order):
                ways = geo.ways(dim)
                n //= ways
                v[f"land{i}{k}{c}"] = ((L, ways - 1, n, WIDE), BF16)
                if i == 0:
                    v[f"red{k}{c}"] = ((L, n, WIDE), BF16)
    return v


class Reduction:
    def __init__(self, geo, net, kind, layer, m):
        self.geo, self.net, self.kind, self.layer, self.m = geo, net, kind, layer, m
        self.rows = geo.rows[kind]
        self.colors = geo.colors[kind]
        self.full = m["f" + kind].at[layer]
        self.mine = m["g" + kind].at[net.at["dir"]]
        self.flows = None

    def pair_send(self):
        landing = self.m["p" + self.kind].at[self.layer]
        other = self.m["g" + self.kind].at[1 - self.net.at["dir"]]
        (self.pair_wait,) = self.net.swap([(other, landing, landing)])
        self.held = [self.net.unsent.pop()]

    def settle(self):
        for size, send in self.held:
            self.net.wait(size, send)

    def pair_done(self):
        self.pair_wait()
        landing = self.m["p" + self.kind].at[self.layer]
        block = 64

        def body(i, _):
            at = pl.ds(i * block, block)
            self.mine[at] = self.mine[at] + landing[at]
            return 0

        lax.fori_loop(0, self.rows // block, body, 0)

    def scatter(self, dim, src, base, part, land):
        net = self.net
        send, recv = net.send_sem(), net.recv_sem()
        net.others(
            dim,
            lambda peer, lin, k: net.put(
                src.at[pl.ds(base + lin * part, part)], land.at[k - 1], send, recv, peer
            ),
        )
        net.unsent.append((land, send))
        return functools.partial(net.wait, land, recv)

    def add(self, own, own_at, land, n, out, out_at, part):
        block = next(b for b in (64, 48, 32, 16) if part % b == 0)

        def body(i, _):
            if n == 2:
                out[pl.ds(out_at + i * block, block)] = (
                    own[pl.ds(own_at + i * block, block)] + land[0, pl.ds(i * block, block)]
                )
                return 0
            total = own[pl.ds(own_at + i * block, block)].astype(F32)
            for k in range(min(n - 1, 7)):
                total = total + land[k, pl.ds(i * block, block)].astype(F32)
            if n - 1 > 7:
                total = lax.fori_loop(
                    7, n - 1, lambda k, t: t + land[k, pl.ds(i * block, block)].astype(F32), total
                )
            out[pl.ds(out_at + i * block, block)] = total.astype(BF16)
            return 0

        lax.fori_loop(0, part // block, body, 0)

    def spread(self, dim, base, part):
        net, n = self.net, self.geo.ways(dim)
        send, recv = net.send_sem(), net.recv_sem()
        mine = self.full.at[pl.ds(base, part)]
        net.others(dim, lambda peer, lin, k: net.put(mine, mine, send, recv, peer))
        size = self.full.at[pl.ds(0, (n - 1) * part)]
        net.unsent.append((size, send))
        return functools.partial(net.wait, size, recv)

    def flow(self, c):
        base, size, order = self.colors[c]
        red = self.m[f"red{self.kind}{c}"].at[self.layer]
        src, src_at, at = self.mine, base, base
        owned = []
        for i, dim in enumerate(order):
            n = self.geo.ways(dim)
            part = size // n
            land = self.m[f"land{i}{self.kind}{c}"].at[self.layer]
            wait = self.scatter(dim, src, src_at, part, land)
            if i == 0:
                self.held.append(self.net.unsent.pop())
            yield
            wait()
            mine = self.net.place(dim)
            own_at, at = src_at + mine * part, at + mine * part
            if i + 1 == len(order):
                out, out_at = self.full, at
            else:
                out, out_at = red, 0 if i == 0 else own_at
            self.add(src, own_at, land, n, out, out_at, part)
            src, src_at, size = red, out_at, part
            owned.append((dim, at, part))
        for dim, at, part in reversed(owned):
            wait = self.spread(dim, at, part)
            yield
            wait()

    def open(self):
        self.pair_done()
        self.flows = [self.flow(c) for c in range(len(self.colors))]

    def step(self, c):
        if c < len(self.flows):
            next(self.flows[c], None)

    def done(self):
        for flow in self.flows:
            for _ in flow:
                pass


def body(geo, names, *refs):
    T, H, W, J, S, N, Pn = geo.T, geo.H, geo.W, geo.J, geo.S, geo.N, geo.Pn
    (lengths, inputs, cotangent, gain, bias, in_proj, out_proj, rate, step, freq, feed, gluw, glub, rmean, rvar) = refs[:15]
    (o_act, o_ig, o_gx, o_gl, o_gi, o_small, o_lam) = refs[15:22]
    scr = refs[22:]
    m = dict(zip(names, scr))
    m["fX"], m["fI"], m["glf"] = o_gx, o_gi, o_gl
    m["xin"], m["cin"], m["pm"] = m["dgt"], m["dml"], m["r"].at[:, 0:T]
    send_sems, recv_sems, local_sems = scr[len(names) :]
    net = Net(geo, send_sems, recv_sems)
    me_d, me_s = net.at["dir"], net.at["seq"]
    local = [0]

    def fetch(src, dst):
        sem = local_sems.at[local[0]]
        local[0] += 1
        copy = pltpu.make_async_copy(src, dst, sem)
        copy.start()
        return copy.wait

    def sum_over_all(msg, which, slot=None):
        at = lambda name: m[name + which] if slot is None else m[name + which].at[slot]
        if geo.direct:
            arrived = net.gather(msg, at("land"), AXES)

            def total():
                arrived()
                return jnp.sum(at("land")[...], axis=0)

            return total
        arrived = net.gather(msg, at("near"), ("dir", "batch"))

        def total():
            arrived()
            at("mid")[...] = jnp.sum(at("near")[...], axis=0)
            net.gather(at("mid"), at("far"), ("seq",))()
            return jnp.sum(at("far")[...], axis=0)

        return total

    barrier = pltpu.get_barrier_semaphore()
    net.peers(AXES, lambda peer, lin, k: pl.semaphore_signal(barrier, 1, device_id=peer, device_id_type=MESH))
    w_x = fetch(inputs.at[me_d], m["xin"])
    w_c = fetch(cotangent.at[me_d], m["cin"])
    raw = (rate, step, freq)
    w_p = [fetch(raw[i], m["prm"].at[i, me_d]) for i in range(3)]
    cols = pl.ds(pl.multiple_of(me_d * W, LANES), W)
    rows_of = pl.ds(pl.multiple_of(me_d * W, 16), W)
    in_at = [m["win"].at[l, :, cols] for l in range(LAYERS)]
    out_at = [m["wout"].at[l, rows_of] for l in range(LAYERS)]
    w_in = [fetch(in_proj.at[l, 0], in_at[l]) for l in range(LAYERS)]
    w_out = [fetch(out_proj.at[l, 0], out_at[l]) for l in range(LAYERS)]
    w_g = fetch(gluw, m["glw"])

    length = lengths[me_d]
    shape = (J, CHUNKS, LANES)
    position = (
        me_s * T
        + lax.broadcasted_iota(jnp.int32, shape, 1) * J
        + lax.broadcasted_iota(jnp.int32, shape, 0)
    )
    m["mask"][...] = jnp.where(position < length, 1.0, 0.0).astype(F32)

    def permutation(i, _):
        at = pl.ds(i * 64, 64)
        row = i * 64 + lax.broadcasted_iota(jnp.int32, (64, T), 0)
        col = lax.broadcasted_iota(jnp.int32, (64, T), 1)
        wanted = lax.rem(row, CHUNKS) * J + lax.div(row, CHUNKS)
        m["pm"][at] = jnp.where(col == wanted, 1.0, 0.0).astype(BF16)
        return 0

    lax.fori_loop(0, T // 64, permutation, 0)

    def put3(ref3, value):
        ref3[...] = value.reshape(J, CHUNKS, H)

    def reorder(src, dst):
        put3(dst, dot(m["pm"][...], src[...], 1, 0))

    GROUP = 4
    ROWS = GROUP * CHUNKS

    def rows(ref, i):
        return ref[pl.ds(i * GROUP, GROUP)].astype(F32)

    def flat(ref, i):
        return ref[pl.ds(i * ROWS, ROWS)].astype(F32).reshape(GROUP, CHUNKS, -1)

    def put_flat(ref, i, value):
        ref[pl.ds(i * ROWS, ROWS)] = value.reshape(ROWS, -1).astype(BF16)

    def sweep(act, sums=0):
        zero = tuple(jnp.zeros((CHUNKS, H), F32) for _ in range(sums))

        def one(i, acc):
            more = act(i)
            if not sums:
                return acc
            return tuple(a + jnp.sum(v, axis=0) for a, v in zip(acc, more))

        acc = lax.fori_loop(0, T // ROWS, one, zero, unroll=2)
        return tuple(jnp.sum(a, axis=0, keepdims=True) for a in acc)

    def rep(row):
        return jnp.broadcast_to(row, (CHUNKS, row.shape[-1]))

    masked = lambda i: widen(rows(m["mask"], i))

    w_x()
    reorder(m["xin"], m["xs"].at[0])

    def first(i):
        x = rows(m["xs"].at[0], i)
        xm = x * masked(i)
        return xm, xm * x

    s1, s2 = sweep(first, 2)
    here = jnp.sum(jnp.sum(m["mask"][...], axis=0), axis=0, keepdims=True)
    m["msg0"][0:1, 0:H] = s1
    m["msg0"][1:2, 0:H] = s2
    m["msg0"][:, H:] = jnp.broadcast_to(here, (2, LANES))

    pl.semaphore_wait(barrier, N - 1)
    stats = sum_over_all(m["msg0"], "0")
    send_in, send_out = [None] * LAYERS, [None] * LAYERS
    prm_waits = net.swap([(raw[i], m["prm"].at[i, me_d], m["prm"].at[i, me_d]) for i in range(3)])
    for l in range(LAYERS):
        (send_in[l],) = net.swap([(in_proj.at[l, 0], in_at[l], in_at[l])])
        (send_out[l],) = net.swap([(out_proj.at[l, 0], out_at[l], out_at[l])])

    for w in w_p + prm_waits:
        w()
    for l in range(LAYERS):
        for dd in range(geo.D):
            lr, li, kr, ki = transition(*(m["prm"][i, dd, l] for i in range(3)))
            power = (lr, li)
            for _ in range((J).bit_length() - 1):
                power = cmul(power, power)
            ladder = [power]
            for _ in range(3):
                ladder.append(cmul(ladder[-1], ladder[-1]))
            wide = [tuple(rep(v) for v in p) for p in ladder]
            chunk = lax.broadcasted_iota(jnp.int32, (CHUNKS, Pn), 0)
            one = (jnp.ones((CHUNKS, Pn), F32), jnp.zeros((CHUNKS, Pn), F32))
            up, down = one, one
            for k in range(3):
                bit = lax.rem(lax.div(chunk, 1 << k), 2)
                grown = cmul(up, wide[k])
                up = tuple(jnp.where(bit == 1, a, b) for a, b in zip(grown, up))
                grown = cmul(down, wide[k])
                down = tuple(jnp.where(bit == 0, a, b) for a, b in zip(grown, down))
            table = [rep(lr), rep(li), *up, *down]
            for p in wide:
                table.extend(p)
            table.extend([rep(kr), rep(ki)])
            for k, v in enumerate(table):
                m["tab"][l, dd, k] = v

    def entry(l, dd, k, minus):
        re, im = m["tab"][l, dd, 2 * k], m["tab"][l, dd, 2 * k + 1]
        return (re, -im) if minus else (re, im)

    def fold(l):
        for dd in range(geo.D):
            kr, ki = m["tab"][l, dd, 14][0:1], m["tab"][l, dd, 15][0:1]

            def some(i, _):
                at = pl.ds(i * 32, 32)
                w = m["win"][l, at, dd * W : (dd + 1) * W].astype(F32)
                re, im = w[:, :Pn], w[:, Pn:]
                new = jnp.concatenate([kr * re - ki * im, kr * im + ki * re], axis=1)
                m["win"][l, at, dd * W : (dd + 1) * W] = new.astype(BF16)
                return 0

            lax.fori_loop(0, H // 32, some, 0)

    for l in range(LAYERS):
        w_in[l]()
        send_in[l]()
        fold(l)
        w_out[l]()
        send_out[l]()
    w_c()
    reorder(m["cin"], m["g"])
    w_g()

    def split(block):
        return block[:, :Pn], block[:, Pn:]

    def advance(lam, h, d):
        return (lam[0] * h[0] - lam[1] * h[1] + d[0], lam[0] * h[1] + lam[1] * h[0] + d[1])

    def scan(l, up_dd, src, minus, start, emit):
        dn_dd = 1 - up_dd
        lam_up, lam_dn = entry(l, up_dd, 0, minus), entry(l, dn_dd, 0, minus)
        n = T // 16

        def two(i, carry):
            hu, hd = carry[:2], carry[2:]
            at_u, at_d = i * 16, (n - 1 - i) * 16
            bu = src[pl.ds(at_u, 16), up_dd * W : (up_dd + 1) * W]
            bd = src[pl.ds(at_d, 16), dn_dd * W : (dn_dd + 1) * W]
            keep_u, keep_d = [], []
            for k in range(2):
                hu = advance(lam_up, hu, split(bu[8 * k : 8 * k + 8]))
                hd = advance(lam_dn, hd, split(bd[8 - 8 * k : 16 - 8 * k]))
                keep_u.append(jnp.concatenate(hu, axis=1))
                keep_d.append(jnp.concatenate(hd, axis=1))
            if emit is not None:
                emit(up_dd, at_u, jnp.concatenate(keep_u, axis=0).astype(BF16))
                emit(dn_dd, at_d, jnp.concatenate(keep_d[::-1], axis=0).astype(BF16))
            return (*hu, *hd)

        out = lax.fori_loop(0, n, two, start, unroll=4)
        return out[:2], out[2:]

    chunk_at = lax.broadcasted_iota(jnp.int32, (CHUNKS, Pn), 0)

    def within(l, dd, ends, rising, minus):
        shift = (lambda v, k: pltpu.roll(v, k, 0)) if rising else (lambda v, k: pltpu.roll(v, CHUNKS - k, 0))
        inside = (lambda k: chunk_at >= k) if rising else (lambda k: chunk_at < CHUNKS - k)
        a = tuple(jnp.where(inside(1), shift(v, 1), 0.0) for v in ends)
        for k in range(3):
            far = tuple(jnp.where(inside(1 << k), shift(v, 1 << k), 0.0) for v in a)
            more = cmul(entry(l, dd, 3 + k, minus), far)
            a = (a[0] + more[0], a[1] + more[1])
        return a

    def carries(k, l, up_dd, ends_up, ends_dn, minus):
        dn_dd = 1 - up_dd
        pieces = [None] * geo.D
        for dd, ends, which in ((up_dd, ends_up, 2), (dn_dd, ends_dn, 1)):
            total = cmul(entry(l, dd, which, minus), ends)
            pieces[dd] = jnp.concatenate([jnp.sum(v, axis=0, keepdims=True) for v in total], axis=1)
        m["smsg"][k] = jnp.concatenate(pieces, axis=1)
        land = m["sland"].at[k]
        arrived = net.gather(m["smsg"].at[k], land, ("seq",))
        here_up = within(l, up_dd, ends_up, True, minus)
        here_dn = within(l, dn_dd, ends_dn, False, minus)
        def finish_up():
            arrived()
            def enter(dd, rising):
                whole = tuple(v[0:1] for v in entry(l, dd, 6, minus))
                zero = jnp.zeros((1, Pn), F32)

                def lap(i, state):
                    at = i if rising else S - 1 - i
                    piece = land[at][:, dd * W : (dd + 1) * W]
                    new = advance(whole, state, split(piece))
                    reached = (at < me_s) if rising else (at > me_s)
                    return tuple(jnp.where(reached, a, b) for a, b in zip(new, state))

                state = (zero, zero)
                if S <= 8:
                    for i in range(S):
                        state = lap(i, state)
                    return state
                return lax.fori_loop(0, S, lap, state)

            outs = []
            for dd, rising, here_ends, which in ((up_dd, True, here_up, 1), (dn_dd, False, here_dn, 2)):
                far = cmul(entry(l, dd, which, minus), tuple(rep(v) for v in enter(dd, rising)))
                outs.append((here_ends[0] + far[0], here_ends[1] + far[1]))
            return outs

        return finish_up

    zeros4 = tuple(jnp.zeros((CHUNKS, Pn), F32) for _ in range(4))

    def stat(l, k):
        return m["stat"][4 * l + k : 4 * l + k + 1]

    def set_stat(l, k, value):
        m["stat"][4 * l + k : 4 * l + k + 1] = value

    c0 = 0.7978845608028654
    c1 = 0.044715
    for l in range(LAYERS):
        sums = stats()
        if l == 0:
            m["stat"][15:16] = 1.0 / widen(sums[0:1, H:])
            sums = sums[:, :H]
        inv_count = m["stat"][15:16]
        mean = sums[0:1] * inv_count
        var = sums[1:2] * inv_count - mean * mean
        inv = lax.rsqrt(var + EPSILON)
        set_stat(l, 0, mean)
        set_stat(l, 1, inv)
        o_small[6 * l + 4 : 6 * l + 5] = MOMENTUM * rmean[l : l + 1] + (1.0 - MOMENTUM) * mean
        o_small[6 * l + 5 : 6 * l + 6] = MOMENTUM * rvar[l : l + 1] + (1.0 - MOMENTUM) * var
        v_mean, v_scale, v_bias = rep(mean), rep(inv * gain[l : l + 1]), rep(bias[l : l + 1])

        def normalise(i):
            x = rows(m["xs"].at[l], i)
            put_flat(m["nrm"].at[l], i, ((x - v_mean) * v_scale + v_bias) * masked(i))

        sweep(normalise)
        m["u"][l] = dot(m["nrm"][l], m["win"][l], 1, 0)
        ends_up, ends_dn = scan(l, 0, m["u"].at[l], False, zeros4, None)
        in_up, in_dn = carries(l, l, 0, ends_up, ends_dn, False)()
        both = lambda v: jnp.concatenate([jnp.concatenate(v, axis=1)] * 2, axis=0).astype(BF16)
        m["st"][l, 0:16, 0:W] = both(in_up)
        m["st"][l, T + 16 : T + 32, W:] = both(in_dn)

        def save(dd, at, value):
            m["st"][l, pl.ds(16 + at, 16), dd * W : (dd + 1) * W] = value

        scan(l, 0, m["u"].at[l], False, (*in_up, *in_dn), save)

        put3(m["tmp"], dot(m["st"][l, 16 : T + 16], m["wout"][l], 1, 0))
        v_feed = rep(feed[l : l + 1])

        def activate(i):
            v = rows(m["tmp"], i) + v_feed * flat(m["nrm"].at[l], i)
            sq = v * v
            t = jnp.tanh(c0 * v * (1.0 + c1 * sq))
            half = 0.5 * (1.0 + t)
            put_flat(m["act"].at[l], i, v * half)
            slope = half + 0.5 * v * (1.0 - t * t) * (c0 * (1.0 + 3.0 * c1 * sq))
            m["dge"][l, pl.ds(i * GROUP, GROUP)] = slope.astype(BF16)

        sweep(activate)
        put3(m["tmp"], dot(m["act"][l], m["glw"][l], 1, 0))
        v_glub = rep(glub[l : l + 1])

        def gate(i):
            sig = 0.5 + 0.5 * jnp.tanh(0.5 * (rows(m["tmp"], i) + v_glub))
            m["sig"][l, pl.ds(i * GROUP, GROUP)] = sig.astype(BF16)
            mk = masked(i)
            x = rows(m["xs"].at[l], i) + mk * flat(m["act"].at[l], i) * sig
            m["xs"][l + 1, pl.ds(i * GROUP, GROUP)] = x
            if l + 1 < LAYERS:
                xm = x * mk
                return xm, xm * x

        sums = sweep(gate, 2 if l + 1 < LAYERS else 0)
        if l + 1 < LAYERS:
            m["msg"][0, 0:1] = sums[0]
            m["msg"][0, 1:2] = sums[1]
            stats = sum_over_all(m["msg"].at[0], "", 0)

    out_waits = []

    def deliver(src, dst):
        send, recv = net.send_sem(), net.recv_sem()
        sem = local_sems.at[local[0]]
        local[0] += 1
        for c in range(CHUNKS):
            to = dst.at[me_d, pl.ds(c * J, J)]
            net.put(src.at[:, c], to, send, recv, {"dir": 1 - me_d})
            pltpu.make_async_copy(src.at[:, c], to, sem).start()
        net.unsent.append((dst.at[me_d], send))
        out_waits.append(functools.partial(net.wait, dst.at[1 - me_d], recv))
        out_waits.append(functools.partial(net.wait, dst.at[me_d], sem))

    deliver(m["xs"].at[LAYERS], o_act)

    reductions = {(k, l): Reduction(geo, net, k, l, m) for k in geo.rows for l in range(LAYERS)}

    def clear_rest(kind, l):
        used, rows_all = geo.used[kind], geo.rows[kind]
        if used < rows_all:
            for dd in range(geo.D):
                m["g" + kind][dd, used:rows_all] = jnp.zeros((rows_all - used, WIDE), BF16)

    def out_grads(l):
        if l + 1 < LAYERS:
            reductions["X", l + 1].settle()
        clear_rest("X", l)
        value = dot(m["st"][l, 16 : T + 16], m["dml"][...], 0, 0).astype(BF16)
        gates = dot(m["act"][l], m["dgt"][...], 0, 0).astype(BF16)
        half = H // 2
        for dd in range(geo.D):
            for i in range(H // WIDE):
                across = slice(i * WIDE, (i + 1) * WIDE)
                m["gX"][dd, i * W : (i + 1) * W] = value[dd * W : (dd + 1) * W, across]
                at = geo.out_rows + i * half
                m["gX"][dd, at : at + half] = gates[dd * half : (dd + 1) * half, across]

    def in_grads(l):
        if l + 1 < LAYERS:
            reductions["I", l + 1].settle()
        clear_rest("I", l)
        value = dot(m["nrm"][l], m["r"][...], 0, 0)
        for dd in range(geo.D):
            for i in range(Pn // LANES):
                across = slice(i * LANES, (i + 1) * LANES)
                kr, ki = m["tab"][l, dd, 14, 0:1, across], m["tab"][l, dd, 15, 0:1, across]
                at = dd * W + i * LANES
                re, im = value[:, at : at + LANES], value[:, at + Pn : at + Pn + LANES]
                new = jnp.concatenate([kr * re + ki * im, kr * im - ki * re], axis=1)
                m["gI"][dd, i * H : (i + 1) * H] = new.astype(BF16)

    def tiny_sums(l, d_glub, d_feed):
        for dd in range(geo.D):
            m["tiny"][l, dd, :, 0:H] = d_glub
            m["tiny"][l, dd, :, H : 2 * H] = d_feed

            def some(i, acc):
                at = i * 16
                across = slice(dd * W, (dd + 1) * W)
                rr, ri = split(m["r"][pl.ds(at, 16), across].astype(F32))
                ur, ui = split(m["u"][l, pl.ds(at, 16), across])
                cur = m["st"][l, pl.ds(at + 16, 16), across].astype(F32)
                if dd == 0:
                    near = m["st"][l, pl.ds(at, 16), across].astype(F32)
                    prev = jnp.concatenate([near[8:], cur[:8]], axis=0)
                else:
                    near = m["st"][l, pl.ds(at + 32, 16), across].astype(F32)
                    prev = jnp.concatenate([cur[8:], near[:8]], axis=0)
                hr, hi = split(prev)
                new = (rr * hr + ri * hi, ri * hr - rr * hi, rr * ur + ri * ui, ri * ur - rr * ui)
                return tuple(a + v[:8] + v[8:] for a, v in zip(acc, new))

            acc = lax.fori_loop(0, T // 16, some, zeros4, unroll=2)
            for k, v in enumerate(acc):
                at = 2 * H + k * Pn
                m["tiny"][l, dd, :, at : at + Pn] = jnp.sum(v, axis=0, keepdims=True)
        landing = m["tpair"].at[l]
        (wait,) = net.swap([(m["tiny"].at[l, 1 - me_d], landing, landing)])
        return wait

    def tiny_near(l, wait):
        wait()
        m["tnear"][l] = m["tiny"][l, me_d] + m["tpair"][l]
        return net.gather(m["tnear"].at[l], m["tland1"].at[l], ("batch",))

    def tiny_middle(l, wait):
        wait()
        m["tmid"][l] = jnp.sum(m["tland1"][l], axis=0)
        return net.gather(m["tmid"].at[l], m["tland2"].at[l], ("seq",))

    def tiny_end(l, wait):
        wait()
        m["tsum"][l] = jnp.sum(m["tland2"][l], axis=0)
        o_small[6 * l + 2 : 6 * l + 3] = m["tsum"][l, :, H : 2 * H]
        o_small[6 * l + 3 : 6 * l + 4] = m["tsum"][l, :, 0:H]
        dlr, dli, ar, ai = (m["tsum"][l, :, 2 * H + k * Pn : 2 * H + (k + 1) * Pn] for k in range(4))
        kr, ki = m["tab"][l, me_d, 14][0:1], m["tab"][l, me_d, 15][0:1]
        size = kr * kr + ki * ki
        dkr, dki = (ar * kr - ai * ki) / size, (ar * ki + ai * kr) / size
        _, pull = jax.vjp(transition, *(m["prm"][i, me_d, l] for i in range(3)))
        for k, v in enumerate(pull((dlr, dli, dkr, dki))):
            o_lam[3 * l + k : 3 * l + k + 1] = v

    def gate_share(l):
        src = m["fX"].at[l, pl.ds(geo.out_rows, geo.half_rows)]
        dst = m["glf"].at[l, me_d]
        (wait,) = net.swap([(src, dst, dst)])
        m["glf"][l, me_d] = m["fX"][l, geo.out_rows : geo.out_rows + geo.half_rows]
        return wait

    kept = {}

    def stage_b1(l):
        def open_gate(i):
            dout = rows(m["g"], i) * masked(i)
            sig = rows(m["sig"].at[l], i)
            v = (dout * flat(m["act"].at[l], i) * sig * (1.0 - sig)).astype(BF16)
            put_flat(m["dgt"], i, v)
            return (v.astype(F32),)

        (kept["glub", l],) = sweep(open_gate, 1)

    def stage_da(l):
        put3(m["tmp"], dot(m["dgt"][...], m["glw"][l], 1, 1))

    def stage_b2(l):
        def through(i):
            dout = rows(m["g"], i) * masked(i)
            d = (rows(m["tmp"], i) + dout * rows(m["sig"].at[l], i)) * rows(m["dge"].at[l], i)
            m["dmx"][pl.ds(i * GROUP, GROUP)] = d
            put_flat(m["dml"], i, d)
            return (d * flat(m["nrm"].at[l], i),)

        (kept["feed", l],) = sweep(through, 1)

    def stage_ds(l):
        m["ds"][...] = dot(m["dml"][...], m["wout"][l], 1, 1)

    def stage_p1(l):
        ends_up, ends_dn = scan(l, 1, m["ds"], True, zeros4, None)
        kept["enter", l] = carries(LAYERS + l, l, 1, ends_up, ends_dn, True)

    def stage_og(l):
        out_grads(l)
        reductions["X", l].pair_send()

    def stage_p2(l):
        in_up, in_dn = kept["enter", l]()

        def save(dd, at, value):
            m["r"][pl.ds(at, 16), dd * W : (dd + 1) * W] = value

        scan(l, 1, m["ds"], True, (*in_up, *in_dn), save)

    def stage_ig(l):
        in_grads(l)
        reductions["I", l].pair_send()

    def stage_dn(l):
        put3(m["tmp"], dot(m["r"][...], m["win"][l], 1, 1))

    def stage_b3(l):
        v_feed, v_mean, v_inv = rep(feed[l : l + 1]), rep(stat(l, 0)), rep(stat(l, 1))

        def normed_grad(i):
            d = (v_feed * rows(m["dmx"], i) + rows(m["tmp"], i)) * masked(i)
            m["tmp"][pl.ds(i * GROUP, GROUP)] = d
            return d, d * ((rows(m["xs"].at[l], i) - v_mean) * v_inv)

        plain, scaled = sweep(normed_grad, 2)
        slot = 1 + l
        m["msg"][slot, 0:1] = plain
        m["msg"][slot, 1:2] = scaled
        kept["sums", l] = sum_over_all(m["msg"].at[slot], "", slot)

    def stage_ty(l):
        kept["tiny", l] = tiny_sums(l, kept["glub", l], kept["feed", l])

    def stage_tp(l):
        kept["tiny", l] = tiny_near(l, kept["tiny", l])

    def stage_tm(l):
        kept["tiny", l] = tiny_middle(l, kept["tiny", l])

    def stage_te(l):
        tiny_end(l, kept["tiny", l])

    def stage_b4(l):
        sums = kept["sums", l]()
        plain, scaled = sums[0:1], sums[1:2]
        o_small[6 * l + 0 : 6 * l + 1] = scaled
        o_small[6 * l + 1 : 6 * l + 2] = plain
        inv = stat(l, 1)
        inv_count = m["stat"][15:16]
        v_scale, v_mean = rep(inv * gain[l : l + 1]), rep(stat(l, 0))
        v_plain, v_scaled = rep(plain * inv_count), rep(scaled * inv_count * inv)

        def stream_grad(i):
            lead = rows(m["tmp"], i) - masked(i) * (v_plain + (rows(m["xs"].at[l], i) - v_mean) * v_scaled)
            at = pl.ds(i * GROUP, GROUP)
            m["g"][at] = m["g"][at] + v_scale * lead

        sweep(stream_grad)
        if l == 0:
            deliver(m["g"], o_ig)

    def stage_gs(l):
        reductions["X", l].done()
        kept["share", l] = gate_share(l)

    stages = dict(
        zip(
            STAGES,
            (
                stage_b1, stage_da, stage_b2, stage_ds, stage_p1, stage_og, stage_p2, stage_ig,
                stage_dn, stage_b3, stage_ty, stage_tp, stage_tm, stage_te, stage_b4, stage_gs,
            ),
        )
    )
    sums_of = dict(zip(SUMS, (reductions[k, l] for k in ("X", "I") for l in range(LAYERS))))
    for what, at in SCHEDULE:
        if what in stages:
            stages[what](at)
        elif at == OPEN:
            sums_of[what].open()
        else:
            sums_of[what].step(at)
    for l in range(LAYERS):
        kept["share", l]()
    for red in reductions.values():
        red.done()
    for k in geo.rows:
        reductions[k, 0].settle()
    for w in out_waits:
        w()
    net.finish()


def on_device(sizes, inputs, cotangent, lengths, gain, bias, in_proj, out_proj, rate, step, freq, feed, gluw, glub, rmean, rvar):
    geo = Geometry(sizes, inputs.shape, rate.shape[-1])
    T, H, W = geo.T, geo.H, geo.W
    v = scratch_shapes(geo)
    held = sum(math.prod(shape) * jnp.dtype(kind).itemsize for shape, kind in v.values())
    hbm = pl.BlockSpec(memory_space=pl.ANY)
    vmem = pl.BlockSpec(memory_space=pltpu.VMEM)
    smem = pl.BlockSpec(memory_space=pltpu.SMEM)
    outs = [
        pltpu.VMEM((geo.seqs, T, H), F32),
        pltpu.VMEM((geo.seqs, T, H), F32),
        pltpu.VMEM((LAYERS, geo.rows["X"], WIDE), BF16),
        pltpu.VMEM((LAYERS, geo.D, geo.half_rows, WIDE), BF16),
        pltpu.VMEM((LAYERS, geo.rows["I"], WIDE), BF16),
        pltpu.VMEM((6 * LAYERS, H), F32),
        pltpu.VMEM((3 * LAYERS, geo.Pn), F32),
    ]
    act, ig, gx, gl, gi, small, lam = pl.pallas_call(
        functools.partial(body, geo, tuple(v)),
        out_shape=outs,
        in_specs=[smem, hbm, hbm, vmem, vmem, hbm, hbm, hbm, hbm, hbm, vmem, hbm, vmem, vmem, vmem],
        out_specs=[vmem] * 7,
        scratch_shapes=[pltpu.VMEM(*s) for s in v.values()]
        + [pltpu.SemaphoreType.DMA((SEMAPHORES,)), pltpu.SemaphoreType.DMA((SEMAPHORES,)), pltpu.SemaphoreType.DMA((32,))],
        compiler_params=pltpu.CompilerParams(
            collective_id=0, has_side_effects=True, vmem_limit_bytes=held + SPARE_BYTES
        ),
    )(lengths, inputs, cotangent, gain, bias, in_proj, out_proj, rate, step, freq, feed, gluw, glub, rmean, rvar)
    return finish(geo, act, ig, gx, gl, gi, small, lam)


def results(geo, *refs):
    T, H, W, Pn, L = geo.T, geo.H, geo.W, geo.Pn, LAYERS
    act, ig, gx, gl, gi, small, lam = refs[:7]
    (o_act, o_ig, o_gain, o_bias, o_in, o_out, o_rate, o_step, o_freq, o_feed, o_glu, o_glub, o_mean, o_var) = refs[7:21]
    v_in, v_out, v_glu, sems = refs[21:]
    used = [0]

    def copy(src, dst):
        sem = sems.at[used[0]]
        used[0] += 1
        c = pltpu.make_async_copy(src, dst, sem)
        c.start()
        return c

    order = list(reversed(range(L)))
    waits = [copy(act, o_act), copy(ig, o_ig)]
    for l in range(L):
        for k, o in enumerate((o_gain, o_bias, o_feed, o_glub, o_mean, o_var)):
            o[l : l + 1] = small[6 * l + k : 6 * l + k + 1]
        for k, o in enumerate((o_rate, o_step, o_freq)):
            o[l] = lam[3 * l + k : 3 * l + k + 1]
    block = 64
    half = H // 2
    for l in order:
        for n in range(H // WIDE):

            def move(i, _):
                v_out[l, pl.ds(i * block, block), n * WIDE : (n + 1) * WIDE] = gx[
                    l, pl.ds(n * W + i * block, block)
                ].astype(F32)
                return 0

            lax.fori_loop(0, W // block, move, 0)
        waits.append(copy(v_out.at[l], o_out.at[l, 0]))
        for n in range(Pn // LANES):

            def move(i, _):
                value = gi[l, pl.ds(n * H + i * block, block)].astype(F32)
                at = pl.ds(i * block, block)
                v_in[l, at, n * LANES : (n + 1) * LANES] = value[:, :LANES]
                v_in[l, at, Pn + n * LANES : Pn + (n + 1) * LANES] = value[:, LANES:]
                return 0

            lax.fori_loop(0, H // block, move, 0)
        waits.append(copy(v_in.at[l], o_in.at[l, 0]))
        for d in range(geo.D):
            for n in range(H // WIDE):

                def move(i, _):
                    value = gl[l, d, pl.ds(n * half + i * block, block)].astype(F32)
                    v_glu[l, pl.ds(d * half + i * block, block), n * WIDE : (n + 1) * WIDE] = value
                    return 0

                lax.fori_loop(0, half // block, move, 0)
        waits.append(copy(v_glu.at[l], o_glu.at[l]))
    for c in waits:
        c.wait()


def finish(geo, act, ig, gx, gl, gi, small, lam):
    T, H, W, Pn, L = geo.T, geo.H, geo.W, geo.Pn, LAYERS
    hbm = pl.BlockSpec(memory_space=pl.ANY)
    vmem = pl.BlockSpec(memory_space=pltpu.VMEM)
    row = jax.ShapeDtypeStruct((L, H), F32)
    lam_row = jax.ShapeDtypeStruct((L, 1, Pn), F32)
    stream = jax.ShapeDtypeStruct((geo.seqs, T, H), F32)
    outs = [
        stream,
        stream,
        row,
        row,
        jax.ShapeDtypeStruct((L, 1, H, W), F32),
        jax.ShapeDtypeStruct((L, 1, W, H), F32),
        lam_row,
        lam_row,
        lam_row,
        row,
        jax.ShapeDtypeStruct((L, H, H), F32),
        row,
        row,
        row,
    ]
    where = [hbm, hbm, vmem, vmem, hbm, hbm, vmem, vmem, vmem, vmem, hbm, vmem, vmem, vmem]
    return pl.pallas_call(
        functools.partial(results, geo),
        out_shape=outs,
        in_specs=[vmem] * 7,
        out_specs=where,
        scratch_shapes=[
            pltpu.VMEM((L, H, W), F32),
            pltpu.VMEM((L, W, H), F32),
            pltpu.VMEM((L, H, H), F32),
            pltpu.SemaphoreType.DMA((16,)),
        ],
        compiler_params=pltpu.CompilerParams(vmem_limit_bytes=16 << 20),
    )(act, ig, gx, gl, gi, small, lam)


def solution(mesh):
    tokens = P("batch", "seq", None)
    per_dir = P(None, "dir", None)
    mats = P(None, "dir", None, None)
    in_specs = (tokens, tokens, P("batch"), P(), P(), mats, mats, per_dir, per_dir, per_dir) + (P(),) * 5
    out_specs = (tokens, tokens, P(), P(), mats, mats, per_dir, per_dir, per_dir) + (P(),) * 5
    return jax.shard_map(
        functools.partial(on_device, dict(mesh.shape)),
        mesh=mesh,
        in_specs=in_specs,
        out_specs=out_specs,
        check_vma=False,
    )
```
